32 devices in a mesh: replica: 2 (over y), group: 16 (over z, x, core).
Axes of the slice: x: 2, y: 2, z: 4, core: 2. Of those that a mesh axis runs over, the one named last changes fastest.
Arguments:
- tokens: bfloat16 [4, 4096, 640], P('replica', 'group'), may hold values from -6 to 6
- cotangent: bfloat16 [4, 4096, 640], P('replica', 'group'), may hold values from -6 to 6
- lengths: int32 [4, 2], P('replica'), may hold values from 1 to 3072, 4096 in all within a row
- w_qkv: float32 [640, 1536], P('group'), may hold values from -0.25 to 0.25
- w_out: float32 [1024, 640], P('group'), may hold values from -0.1875 to 0.1875
- w_gu: float32 [640, 4096], P('group'), may hold values from -0.25 to 0.25
- w_down: float32 [2048, 640], P('group'), may hold values from -0.125 to 0.125
- norm_gains: float32 [3072], P('group'), may hold values from 0.5 to 1.5
- first_qkv: float32 [640, 1536], P('group'), may hold values from -80 to 80
- first_out: float32 [1024, 640], P('group'), may hold values from -80 to 80
- first_gu: float32 [640, 4096], P('group'), may hold values from -56 to 56
- first_down: float32 [2048, 640], P('group'), may hold values from -80 to 80
- first_gains: float32 [3072], P('group'), may hold values from -128 to 128
- second_qkv: float32 [640, 1536], P('group'), may hold values from 19.6608 to 81.92
- second_out: float32 [1024, 640], P('group'), may hold values from 16.384 to 65.536
- second_gu: float32 [640, 4096], P('group'), may hold values from 6.5536 to 26.2144
- second_down: float32 [2048, 640], P('group'), may hold values from 16.384 to 65.536
- second_gains: float32 [3072], P('group'), may hold values from 36.0448 to 147.456
Outputs:
- layer_out: bfloat16 [4, 4096, 640], P('replica', 'group')
- token_grad: float32 [4, 4096, 640], P('replica', 'group')
- moment_qkv: float32 [640, 1536], P('group')
- square_qkv: float32 [640, 1536], P('group')
- master_qkv: float32 [640, 1536], P('group')
- moment_out: float32 [1024, 640], P('group')
- square_out: float32 [1024, 640], P('group')
- master_out: float32 [1024, 640], P('group')
- moment_gu: float32 [640, 4096], P('group')
- square_gu: float32 [640, 4096], P('group')
- master_gu: float32 [640, 4096], P('group')
- moment_down: float32 [2048, 640], P('group')
- square_down: float32 [2048, 640], P('group')
- master_down: float32 [2048, 640], P('group')
- moment_gains: float32 [3072], P('group')
- square_gains: float32 [3072], P('group')
- master_gains: float32 [3072], P('group')
The draws below stay inside these ranges and needn't reach their ends.
Inputs may be any that keep to these rules, and one draw needn't show every extreme that they name: Each row holds two sequences whose lengths sum to 4096.
All inputs are finite; a program needn't handle non-finite values.
Results may differ from the reference program's by a relative error of at most 0.035.
Values may be sent and summed in bfloat16 or wider, within the bound.
No kernel may reach another device: no remote copies, remote signals or barrier semaphores. Data moves between devices by JAX's collectives and lax.ppermute only.
A program may use at most 256 MiB of HBM per device.

```python
import math
import jax
import jax.numpy as jnp
import numpy as np
from jax import lax

D = 640
HQ = 4
HD = 256
FF = 2048
SEQS = 2
STEP = 10
STREAM = 4096
LONGEST = 3072
ROWS = 4
TOKENS_ALL = 16384
GAINS = 3072


def shard_levels(key, extent, pieces, low, top_value):
    loudness, own = 1.0, jax.random.fold_in(key, 6)
    for axis_at, shards_of in pieces:
        heights = jnp.exp(jax.random.uniform(jax.random.fold_in(own, axis_at), (shards_of,), jnp.float32, low / len(pieces), top_value / len(pieces)))
        loudness = loudness * jnp.repeat(heights, extent[axis_at] // shards_of).reshape([-1 if axis == axis_at else 1 for axis in range(len(extent))])
    return loudness


def profile(amount, total, limit, lean):
    portions = [(1 << 20) // math.isqrt(grade ** lean) + 1 for grade in range(2, amount + 1)]
    surplus, holding = total - limit - (amount - 1), [1] * (amount - 1)
    while surplus > 0:
        candidates = [i for i in range(amount - 1) if holding[i] < limit]
        mass, left = sum([portions[i] for i in candidates]), surplus
        for i in candidates:
            addition = min(limit - holding[i], max(1, left * portions[i] // mass), surplus)
            holding[i] = holding[i] + addition
            surplus = surplus - addition
    return np.array([limit] + holding)


def ragged(key, number_of, total, bound, slope):
    if number_of == 2:
        one = jax.random.randint(key, (), max(1, total - bound), min(bound, total - 1) + 1)
        return jnp.stack([one, total - one])
    sizes = jnp.asarray(profile(number_of, total, bound, slope), jnp.int32)
    couples = (number_of - 1) // 2
    donor, receiver = sizes[1:1 + 2 * couples:2], sizes[2:2 + 2 * couples:2]
    slack = jnp.minimum(donor - 1, bound - receiver)
    shifted = jax.random.randint(jax.random.fold_in(key, 1), (couples,), 0, 1 << 20) % (slack + 1)
    sizes = sizes.at[1:1 + 2 * couples:2].set(donor - shifted).at[2:2 + 2 * couples:2].set(receiver + shifted)
    return sizes[jax.random.permutation(jax.random.fold_in(key, 2), number_of)]


def noise(rng, extent, spread, most, pieces=(), kind=jnp.bfloat16):
    gain = shard_levels(rng, extent, pieces, -0.22, 0.18) if pieces else 1.0
    values = jax.random.normal(rng, extent, jnp.float32) * spread * gain
    return jnp.minimum(jnp.maximum(values, -most), most).astype(kind)


def setup_inputs(seed: int = 0) -> dict:
    seeds = jax.random.split(jax.random.key(seed), 19)
    tokens = noise(seeds[0], (ROWS, STREAM, D), 1.0, 6.0, ((0, 2), (1, 16)))
    cotangent = noise(seeds[1], (ROWS, STREAM, D), 1.0, 6.0, ((0, 2), (1, 16)))
    lengths = jax.vmap(lambda own: ragged(own, SEQS, STREAM, LONGEST, 2))(jax.random.split(seeds[2], ROWS)).reshape((ROWS, SEQS)).astype(jnp.int32)
    w_qkv = noise(seeds[3], (D, (HQ + 2) * HD), D ** -0.5, 0.25, ((0, 16),), jnp.float32)
    w_out = noise(seeds[4], (HQ * HD, D), (HQ * HD) ** -0.5, 0.1875, ((0, 16),), jnp.float32)
    w_gu = noise(seeds[5], (D, 2 * FF), D ** -0.5, 0.25, ((0, 16),), jnp.float32)
    w_down = noise(seeds[6], (FF, D), FF ** -0.5, 0.125, ((0, 16),), jnp.float32)
    norm_gains = jnp.clip(1.0 + 0.1 * jax.random.normal(seeds[7], (GAINS,), jnp.float32), 0.5, 1.5)
    first_qkv = noise(seeds[8], (D, (HQ + 2) * HD), (0.111 * TOKENS_ALL ** 0.5), 80.0, ((0, 16),), jnp.float32)
    first_out = noise(seeds[9], (HQ * HD, D), (0.111 * TOKENS_ALL ** 0.5), 80.0, ((0, 16),), jnp.float32)
    first_gu = noise(seeds[10], (D, 2 * FF), (0.07 * TOKENS_ALL ** 0.5), 56.0, ((0, 16),), jnp.float32)
    first_down = noise(seeds[11], (FF, D), (0.111 * TOKENS_ALL ** 0.5), 80.0, ((0, 16),), jnp.float32)
    first_gains = noise(seeds[12], (GAINS,), (0.167 * TOKENS_ALL ** 0.5), 128.0, ((0, 16),), jnp.float32)
    second_qkv = jnp.clip(jnp.exp(math.log(81.92) - 1.4271163 * jax.random.uniform(seeds[13], (D, (HQ + 2) * HD), jnp.float32) ** shard_levels(seeds[13], (D, (HQ + 2) * HD), ((0, 16),), -0.2, 0.2)), 19.6608, 81.92)
    second_out = jnp.clip(jnp.exp(math.log(65.536) - 1.3862944 * jax.random.uniform(seeds[14], (HQ * HD, D), jnp.float32) ** shard_levels(seeds[14], (HQ * HD, D), ((0, 16),), -0.2, 0.2)), 16.384, 65.536)
    second_gu = jnp.clip(jnp.exp(math.log(26.2144) - 1.3862944 * jax.random.uniform(seeds[15], (D, 2 * FF), jnp.float32) ** shard_levels(seeds[15], (D, 2 * FF), ((0, 16),), -0.2, 0.2)), 6.5536, 26.2144)
    second_down = jnp.clip(jnp.exp(math.log(65.536) - 1.3862944 * jax.random.uniform(seeds[16], (FF, D), jnp.float32) ** shard_levels(seeds[16], (FF, D), ((0, 16),), -0.2, 0.2)), 16.384, 65.536)
    second_gains = jnp.clip(jnp.exp(math.log(147.456) - 1.4087672 * jax.random.uniform(seeds[17], (GAINS,), jnp.float32) ** shard_levels(seeds[17], (GAINS,), ((0, 16),), -0.2, 0.2)), 36.0448, 147.456)
    return dict(tokens=tokens, cotangent=cotangent, lengths=lengths, w_qkv=w_qkv, w_out=w_out, w_gu=w_gu, w_down=w_down, norm_gains=norm_gains, first_qkv=first_qkv, first_out=first_out, first_gu=first_gu, first_down=first_down, first_gains=first_gains, second_qkv=second_qkv, second_out=second_out, second_gu=second_gu, second_down=second_down, second_gains=second_gains)


@jax.custom_vjp
def low(v):
    return lax.optimization_barrier(v.astype(jnp.bfloat16)).astype(jnp.float32)

@jax.custom_vjp
def low_back(v):
    return v

def low_keep(v):
    return (low(v), None)

def low_pass(kept, grad):
    return (grad,)

def back_keep(v):
    return (v, None)

def back_low(kept, grad):
    return (low(grad),)
low.defvjp(low_keep, low_pass)
low_back.defvjp(back_keep, back_low)
EPS_NORM = 1e-06
BETA_ONE = 0.9
BETA_TWO = 0.999
ADAM_EPS = 1e-08
RATE_MATRIX = 0.1
RATE_GAIN = 0.5
DECAY_RATE = 0.1
ROPE_BASE = 1000000.0
NEGATIVE = -1e+30
SCALE_SCORE = 0.0625
HIGHEST = lax.Precision.HIGHEST

def rms_norm(values, gain_row):
    factor = lax.rsqrt(lax.optimization_barrier(jnp.mean(values * values, axis=-1, keepdims=True)) + EPS_NORM)
    return values * factor * gain_row

def angles(position, width):
    half_width = width // 2
    frequency = jnp.exp(jnp.arange(half_width, dtype=jnp.float32) * (-2.0 * math.log(ROPE_BASE) / width))
    angle_table = position.astype(jnp.float32)[:, None] * frequency[None, :]
    return (jnp.cos(angle_table), jnp.sin(angle_table))

def rotate(values, cosine, sine):
    half_width = values.shape[-1] // 2
    leading = values[..., :half_width]
    trailing = values[..., half_width:]
    return jnp.concatenate([leading * cosine - trailing * sine, trailing * cosine + leading * sine], axis=-1)

def layout(lengths, total):
    seq_ends = jnp.cumsum(lengths).astype(jnp.int32)
    seq_starts = (seq_ends - lengths).astype(jnp.int32)
    stream_index = jnp.arange(total, dtype=jnp.int32)
    segment = lax.optimization_barrier(jnp.sum((stream_index[:, None] >= seq_ends[None, :]).astype(jnp.int32), axis=1)).astype(jnp.int32)
    seq_begin = lax.optimization_barrier(jnp.max(jnp.where(stream_index[:, None] >= seq_starts[None, :], seq_starts[None, :], 0), axis=1)).astype(jnp.int32)
    return (segment, (stream_index - seq_begin).astype(jnp.int32))

def heads_in(qkv_rows, gain_query, gain_key, cosine, sine):
    row_count = qkv_rows.shape[0]
    queries = qkv_rows[:, :HQ * HD].reshape(row_count, HQ, HD)
    keys_pre = qkv_rows[:, HQ * HD:(HQ + 1) * HD]
    values_pre = qkv_rows[:, (HQ + 1) * HD:]
    query_rot = rotate(rms_norm(queries, gain_query), cosine[:, None, :], sine[:, None, :])
    key_rot = rotate(rms_norm(keys_pre, gain_key), cosine, sine)
    return (query_rot, key_rot, values_pre)

def geglu(gate_up):
    return jax.nn.gelu(gate_up[:, :FF], approximate=True) * gate_up[:, FF:]

def split_gains(gain_all):
    return (gain_all[0:D], gain_all[D:2 * D], gain_all[2 * D:3 * D], gain_all[3 * D:4 * D], gain_all[4 * D:4 * D + HD], gain_all[4 * D + HD:4 * D + 2 * HD])

def stream_forward(stream_rows, stream_lengths, params):
    mat_qkv, mat_out, mat_gu, mat_down, gain_all = params
    gain_in, gain_pa, gain_pf, gain_po, gain_query, gain_key = split_gains(gain_all)
    segment, position = layout(stream_lengths, STREAM)
    stream_index = jnp.arange(STREAM, dtype=jnp.int32)
    cosine, sine = angles(position, HD)
    normed_in = low(rms_norm(stream_rows, gain_in))
    qkv_rows = low_back(jnp.dot(normed_in, mat_qkv, precision=HIGHEST))
    query_rot, key_rot, values_pre = heads_in(qkv_rows, gain_query, gain_key, cosine, sine)
    query_low = low(query_rot)
    key_low = low(key_rot)
    value_low = low(values_pre)
    block_rows = min(512, STREAM)
    block_count = STREAM // block_rows

    def attend(item):
        query_block, segment_block, index_block = item
        raw_scores = jnp.einsum('qhd,kd->hqk', query_block, key_low, precision=HIGHEST)
        scores = low_back(raw_scores * SCALE_SCORE)
        allowed = (segment_block[:, None] == segment[None, :]) & (index_block[:, None] >= stream_index[None, :])
        scores = jnp.where(allowed[None], scores, NEGATIVE)
        row_max = lax.optimization_barrier(jnp.max(scores, axis=-1, keepdims=True))
        exp_scores = jnp.exp(scores - row_max)
        weights = exp_scores / lax.optimization_barrier(jnp.sum(exp_scores, axis=-1, keepdims=True))
        return jnp.einsum('hqk,kd->qhd', low(weights), value_low, precision=HIGHEST)
    attended = lax.map(jax.checkpoint(attend), (query_low.reshape(block_count, block_rows, HQ, HD), segment.reshape(block_count, block_rows), stream_index.reshape(block_count, block_rows)))
    attn_low = low(low_back(attended.reshape(STREAM, HQ * HD)))
    attn_proj = low_back(jnp.dot(attn_low, mat_out, precision=HIGHEST))
    middle = stream_rows + rms_norm(attn_proj, gain_pa)
    ff_low = low(rms_norm(middle, gain_pf))
    gate_up = low_back(jnp.dot(ff_low, mat_gu, precision=HIGHEST))
    hidden_low = low(geglu(gate_up))
    down_proj = low_back(jnp.dot(hidden_low, mat_down, precision=HIGHEST))
    return middle + rms_norm(down_proj, gain_po)

def forward(token_rows, mat_qkv, mat_out, mat_gu, mat_down, gain_all, lengths):
    params = (low(mat_qkv), low(mat_out), low(mat_gu), low(mat_down), low(gain_all))

    def advance(carry, item):
        return (carry, stream_forward(item[0], item[1], params))
    _, result = lax.scan(jax.checkpoint(advance), jnp.zeros((), jnp.float32), (token_rows, lengths))
    return result

def adam_step(master, moment_one, moment_two, gradient, rate, decay):
    moment_new = BETA_ONE * moment_one + (1.0 - BETA_ONE) * gradient
    square_new = BETA_TWO * moment_two + (1.0 - BETA_TWO) * gradient * gradient
    moment_hat = moment_new / (1.0 - BETA_ONE ** STEP)
    square_hat = square_new / (1.0 - BETA_TWO ** STEP)
    master_new = master * (1.0 - rate * decay) - rate * moment_hat / (jnp.sqrt(square_hat) + ADAM_EPS)
    return (moment_new, square_new, master_new)

def reference(tokens, cotangent, lengths, w_qkv, w_out, w_gu, w_down, norm_gains, first_qkv, first_out, first_gu, first_down, first_gains, second_qkv, second_out, second_gu, second_down, second_gains):

    def run(token_rows, mat_qkv, mat_out, mat_gu, mat_down, gain_all):
        return forward(token_rows, mat_qkv, mat_out, mat_gu, mat_down, gain_all, lengths)
    result, pullback = jax.vjp(run, tokens.astype(jnp.float32), w_qkv, w_out, w_gu, w_down, norm_gains)
    grads = pullback(cotangent.astype(jnp.float32))
    upd_qkv = adam_step(w_qkv, first_qkv, second_qkv, grads[1], RATE_MATRIX, DECAY_RATE)
    upd_out = adam_step(w_out, first_out, second_out, grads[2], RATE_MATRIX, DECAY_RATE)
    upd_gu = adam_step(w_gu, first_gu, second_gu, grads[3], RATE_MATRIX, DECAY_RATE)
    upd_down = adam_step(w_down, first_down, second_down, grads[4], RATE_MATRIX, DECAY_RATE)
    upd_gains = adam_step(norm_gains, first_gains, second_gains, grads[5], RATE_GAIN, 0.0)
    return (result.astype(jnp.bfloat16), grads[0], upd_qkv[0], upd_qkv[1], upd_qkv[2], upd_out[0], upd_out[1], upd_out[2], upd_gu[0], upd_gu[1], upd_gu[2], upd_down[0], upd_down[1], upd_down[2], upd_gains[0], upd_gains[1], upd_gains[2])
```

```python
import math

import jax
import jax.numpy as jnp
from jax import lax
from jax.experimental import pallas as pl
from jax.experimental.pallas import tpu as pltpu
from jax.sharding import PartitionSpec as P

D = 640
HQ = 4
HD = 256
FF = 2048
SEG = 256
STEP = 10


EPS_NORM = 1e-06
BETA_ONE = 0.9
BETA_TWO = 0.999
ADAM_EPS = 1e-08
RATE_MATRIX = 0.1
RATE_GAIN = 0.5
DECAY_RATE = 0.1
ROPE_BASE = 1000000.0
NEGATIVE = -1e30
SCALE_SCORE = 0.0625


def rms_norm(values, gain_row):
    factor = lax.rsqrt(jnp.mean(values * values, axis=-1, keepdims=True) + EPS_NORM)
    return values * factor * gain_row


def angles(position, width):
    half_width = width // 2
    frequency = jnp.exp(
        jnp.arange(half_width, dtype=jnp.float32) * (-2.0 * math.log(ROPE_BASE) / width)
    )
    angle_table = position.astype(jnp.float32)[:, None] * frequency[None, :]
    return (jnp.cos(angle_table), jnp.sin(angle_table))


def rotate(values, cosine, sine):
    half_width = values.shape[-1] // 2
    leading = values[..., :half_width]
    trailing = values[..., half_width:]
    return jnp.concatenate(
        [leading * cosine - trailing * sine, trailing * cosine + leading * sine], axis=-1
    )


def layout(lengths, total):
    seq_ends = jnp.cumsum(lengths)
    seq_starts = seq_ends - lengths
    stream_index = jnp.arange(total, dtype=jnp.int32)
    segment = jnp.sum((stream_index[:, None] >= seq_ends[None, :]).astype(jnp.int32), axis=1)
    seq_begin = jnp.max(
        jnp.where(stream_index[:, None] >= seq_starts[None, :], seq_starts[None, :], 0), axis=1
    )
    return (segment, stream_index - seq_begin)


def heads_in(qkv_rows, gain_query, gain_key, cosine, sine):
    row_count = qkv_rows.shape[0]
    queries = qkv_rows[:, : HQ * HD].reshape(row_count, HQ, HD)
    keys_pre = qkv_rows[:, HQ * HD : (HQ + 1) * HD]
    values_pre = qkv_rows[:, (HQ + 1) * HD :]
    query_rot = rotate(rms_norm(queries, gain_query), cosine[:, None, :], sine[:, None, :])
    key_rot = rotate(rms_norm(keys_pre, gain_key), cosine, sine)
    return (query_rot, key_rot, values_pre)


def geglu(gate_up):
    return jax.nn.gelu(gate_up[:, :FF], approximate=True) * gate_up[:, FF:]


def split_gains(gain_all):
    return (
        gain_all[0:D],
        gain_all[D : 2 * D],
        gain_all[2 * D : 3 * D],
        gain_all[3 * D : 4 * D],
        gain_all[4 * D : 4 * D + HD],
        gain_all[4 * D + HD : 4 * D + 2 * HD],
    )


def adam_step(master, moment_one, moment_two, gradient, rate, decay):
    moment_new = BETA_ONE * moment_one + (1.0 - BETA_ONE) * gradient
    square_new = BETA_TWO * moment_two + (1.0 - BETA_TWO) * gradient * gradient
    moment_hat = moment_new / (1.0 - BETA_ONE**STEP)
    square_hat = square_new / (1.0 - BETA_TWO**STEP)
    master_new = master * (1.0 - rate * decay) - rate * moment_hat / (
        jnp.sqrt(square_hat) + ADAM_EPS
    )
    return (moment_new, square_new, master_new)


LOG2E = 1.4426950408889634
KEYS = 512
MEMBERS = 16
NT = (((1,), (1,)), ((), ()))
TN = (((0,), (0,)), ((), ()))
F32 = jnp.float32
BF16 = jnp.bfloat16


def step_z(values):
    return lax.ppermute(values, "group", [(i, (i + 4) % MEMBERS) for i in range(MEMBERS)])


def swap_x(values):
    return lax.ppermute(values, "group", [(i, i ^ 2) for i in range(MEMBERS)])


def swap_core(values):
    return lax.ppermute(values, "group", [(i, i ^ 1) for i in range(MEMBERS)])


def gather_blocks(own):
    lines = [own]
    for _ in range(3):
        lines.append(step_z(lines[-1]))
    near = []
    for line in lines:
        near += [line, swap_x(line)]
    return near + [swap_core(block) for block in near]


def scatter_blocks(far, near_far, near):
    running = None
    for k in (3, 2, 1, 0):
        came = swap_core(far[k]).astype(F32)
        over = swap_x((near_far[k].astype(F32) + came[1]).astype(BF16))
        total = near[k].astype(F32) + came[0] + over.astype(F32)
        if running is not None:
            total = total + running.astype(F32)
        if k:
            running = step_z(total.astype(BF16))
    return total


def key_range(info, stream):
    first = info[0]
    bound = info[4 + stream]
    last = first + SEG - 1
    low = jnp.where(first >= bound, bound, 0)
    high = jnp.where(last >= bound, bound, 0)
    begin = low // KEYS
    diagonal = first // KEYS
    clear = jnp.clip((high + KEYS - 1) // KEYS, begin, diagonal)
    return first, bound, begin, clear, diagonal


def load_blocks(info, blocks, kv, sem):
    z, x, c = info[1], info[2], info[3]
    copies = []
    for place in range(MEMBERS):
        cr, k, xr = place // 8, place // 2 % 4, place % 2
        owner = ((z - k) & 3) * 4 + (x ^ xr) * 2 + (c ^ cr)
        copies.append(pltpu.make_async_copy(blocks[place], kv.at[owner], sem.at[place]))
    for copy in copies:
        copy.start()
    return copies


def forward_kernel(info, q_ref, *refs):
    blocks = refs[:MEMBERS]
    o_ref, lse_ref, kv, acc, total, sem = refs[MEMBERS:]
    copies = load_blocks(info, blocks, kv, sem)
    for copy in copies:
        copy.wait()
    for stream in range(2):
        first, bound, begin, clear, diagonal = key_range(info, stream)
        acc[...] = jnp.zeros_like(acc)
        total[...] = jnp.zeros_like(total)

        def visit(j, masked):
            keys = kv[pl.ds(2 * j, 2), stream, :, 0:HD].reshape(KEYS, HD)
            values = kv[pl.ds(2 * j, 2), stream, :, HD : 2 * HD].reshape(KEYS, HD)
            if masked:
                row = first + lax.broadcasted_iota(jnp.int32, (SEG, KEYS), 0)
                col = j * KEYS + lax.broadcasted_iota(jnp.int32, (SEG, KEYS), 1)
                mask = (col <= row) & (col >= jnp.where(row >= bound, bound, 0))
            for head in range(HQ):
                rows = slice(head * SEG, (head + 1) * SEG)
                query = q_ref[stream * SEG : (stream + 1) * SEG, head * HD : (head + 1) * HD]
                score = lax.dot_general(query, keys, NT, preferred_element_type=F32)
                prob = jnp.exp2(score * (SCALE_SCORE * LOG2E))
                if masked:
                    prob = jnp.where(mask, prob, 0.0)
                total[rows] += (
                    prob[:, 0:128] + prob[:, 128:256] + prob[:, 256:384] + prob[:, 384:512]
                )
                acc[rows] += jnp.dot(prob.astype(BF16), values, preferred_element_type=F32)

        def masked_step(j, carry):
            visit(j, True)
            return carry

        def clear_step(j, carry):
            visit(j, False)
            return carry

        lax.fori_loop(begin, clear, masked_step, 0)
        lax.fori_loop(clear, diagonal, clear_step, 0)
        masked_step(diagonal, 0)
        for head in range(HQ):
            rows = slice(head * SEG, (head + 1) * SEG)
            part = total[rows]
            out = acc[rows] / jnp.sum(part, axis=1, keepdims=True)
            o_ref[stream * SEG : (stream + 1) * SEG, head * HD : (head + 1) * HD] = out.astype(BF16)
            lse_ref[stream, :, rows] = jnp.log2(jnp.sum(part.T, axis=0, keepdims=True))


def attention_forward(info, query, blocks):
    return pl.pallas_call(
        forward_kernel,
        out_shape=(
            jax.ShapeDtypeStruct((2 * SEG, HQ * HD), BF16),
            jax.ShapeDtypeStruct((2, 1, HQ * SEG), F32),
        ),
        in_specs=[
            pl.BlockSpec(memory_space=pltpu.SMEM),
            pl.BlockSpec(memory_space=pltpu.VMEM),
        ]
        + [pl.BlockSpec(memory_space=pl.ANY)] * MEMBERS,
        out_specs=(
            pl.BlockSpec(memory_space=pltpu.VMEM),
            pl.BlockSpec(memory_space=pltpu.VMEM),
        ),
        scratch_shapes=[
            pltpu.VMEM((MEMBERS, 2, SEG, 2 * HD), BF16),
            pltpu.VMEM((HQ * SEG, HD), F32),
            pltpu.VMEM((HQ * SEG, 128), F32),
            pltpu.SemaphoreType.DMA((MEMBERS,)),
        ],
        compiler_params=pltpu.CompilerParams(vmem_limit_bytes=40 * 1024 * 1024),
        cost_estimate=pl.CostEstimate(
            flops=7_000_000_000, bytes_accessed=11_000_000, transcendentals=7_000_000
        ),
        name="attention_forward",
    )(info, query, *blocks)


def backward_kernel(info, q_ref, o_ref, do_ref, lse_ref, *refs):
    blocks = refs[:MEMBERS]
    dq_ref = refs[MEMBERS]
    far = refs[MEMBERS + 1 : MEMBERS + 5]
    near_far = refs[MEMBERS + 5 : MEMBERS + 9]
    near = refs[MEMBERS + 9 : MEMBERS + 13]
    kv, dkv, qs, qt, dos, dot_, dqt, sem, out_sem = refs[MEMBERS + 13 :]
    copies = load_blocks(info, blocks, kv, sem)
    z, x, c = info[1], info[2], info[3]

    def clean(place, carry):
        dkv[place] = jnp.zeros((2, SEG, 2 * HD), BF16)
        return carry

    lax.fori_loop(0, MEMBERS, clean, 0)
    for copy in copies:
        copy.wait()
    for stream in range(2):
        first, bound, begin, clear, diagonal = key_range(info, stream)
        parts = []
        for head in range(HQ):
            rows = slice(head * SEG, (head + 1) * SEG)
            at = (slice(stream * SEG, (stream + 1) * SEG), slice(head * HD, (head + 1) * HD))
            query = q_ref[at]
            grad = do_ref[at]
            qs[rows] = query
            dos[rows] = grad
            qt[:, rows] = query.T
            dot_[:, rows] = grad.T
            both = grad.astype(F32) * o_ref[at].astype(F32)
            parts.append(
                jnp.sum((both[:, 0:128] + both[:, 128:256]).T, axis=0, keepdims=True)
            )
        delta = jnp.concatenate(parts, axis=1)
        lse = lse_ref[stream]
        dqt[...] = jnp.zeros_like(dqt)

        def visit(j, masked):
            keys = kv[pl.ds(2 * j, 2), stream, :, 0:HD].reshape(KEYS, HD)
            values = kv[pl.ds(2 * j, 2), stream, :, HD : 2 * HD].reshape(KEYS, HD)
            score = jnp.dot(keys, qt[...], preferred_element_type=F32)
            prob = jnp.exp2(score * (SCALE_SCORE * LOG2E) - lse)
            if masked:
                shape = (KEYS, HQ * SEG)
                row = first + (lax.broadcasted_iota(jnp.int32, shape, 1) & (SEG - 1))
                col = j * KEYS + lax.broadcasted_iota(jnp.int32, shape, 0)
                mask = (col <= row) & (col >= jnp.where(row >= bound, bound, 0))
                prob = jnp.where(mask, prob, 0.0)
            dprob = jnp.dot(values, dot_[...], preferred_element_type=F32)
            dscore = (prob * (dprob - delta)).astype(BF16)
            dv = jnp.dot(prob.astype(BF16), dos[...], preferred_element_type=F32).astype(BF16)
            dk = jnp.dot(dscore, qs[...], preferred_element_type=F32)
            dk = (dk * SCALE_SCORE).astype(BF16)
            dqt[...] += jnp.dot(keys.T, dscore, preferred_element_type=F32)
            for core in range(2):
                place = (core ^ c) * 8 + (((j >> 1) - z) & 3) * 2 + ((j & 1) ^ x)
                dkv[place, stream, :, 0:HD] = dk[core * SEG : (core + 1) * SEG]
                dkv[place, stream, :, HD : 2 * HD] = dv[core * SEG : (core + 1) * SEG]

        def masked_step(j, carry):
            visit(j, True)
            return carry

        def clear_step(j, carry):
            visit(j, False)
            return carry

        lax.fori_loop(begin, clear, masked_step, 0)
        lax.fori_loop(clear, diagonal, clear_step, 0)
        masked_step(diagonal, 0)
        for head in range(HQ):
            rows = slice(head * SEG, (head + 1) * SEG)
            at = (slice(stream * SEG, (stream + 1) * SEG), slice(head * HD, (head + 1) * HD))
            dq_ref[at] = dqt[:, rows].T * SCALE_SCORE
    outs = []
    for k in range(4):
        outs.append((dkv.at[pl.ds(8 + 2 * k, 2)], far[k]))
        outs.append((dkv.at[2 * k + 1], near_far[k]))
        outs.append((dkv.at[2 * k], near[k]))
    copies = [
        pltpu.make_async_copy(source, target, out_sem.at[n])
        for n, (source, target) in enumerate(outs)
    ]
    for copy in copies:
        copy.start()
    for copy in copies:
        copy.wait()


def attention_backward(info, query, out, grad_out, lse, blocks):
    one = jax.ShapeDtypeStruct((2, SEG, 2 * HD), BF16)
    two = jax.ShapeDtypeStruct((2, 2, SEG, 2 * HD), BF16)
    vmem = pl.BlockSpec(memory_space=pltpu.VMEM)
    anywhere = pl.BlockSpec(memory_space=pl.ANY)
    result = pl.pallas_call(
        backward_kernel,
        out_shape=[jax.ShapeDtypeStruct((2 * SEG, HQ * HD), F32)] + [two] * 4 + [one] * 8,
        in_specs=[pl.BlockSpec(memory_space=pltpu.SMEM)] + [vmem] * 4 + [anywhere] * MEMBERS,
        out_specs=[vmem] + [anywhere] * 12,
        scratch_shapes=[
            pltpu.VMEM((MEMBERS, 2, SEG, 2 * HD), BF16),
            pltpu.VMEM((MEMBERS, 2, SEG, 2 * HD), BF16),
            pltpu.VMEM((HQ * SEG, HD), BF16),
            pltpu.VMEM((HD, HQ * SEG), BF16),
            pltpu.VMEM((HQ * SEG, HD), BF16),
            pltpu.VMEM((HD, HQ * SEG), BF16),
            pltpu.VMEM((HD, HQ * SEG), F32),
            pltpu.SemaphoreType.DMA((MEMBERS,)),
            pltpu.SemaphoreType.DMA((12,)),
        ],
        compiler_params=pltpu.CompilerParams(vmem_limit_bytes=52 * 1024 * 1024),
        cost_estimate=pl.CostEstimate(
            flops=17_000_000_000, bytes_accessed=24_000_000, transcendentals=7_000_000
        ),
        name="attention_backward",
    )(info, query, out, grad_out, lse, *blocks)
    return result[0], result[1:5], result[5:9], result[9:13]


def per_device(
    tokens,
    cotangent,
    lengths,
    w_qkv,
    w_out,
    w_gu,
    w_down,
    norm_gains,
    first_qkv,
    first_out,
    first_gu,
    first_down,
    first_gains,
    second_qkv,
    second_out,
    second_gu,
    second_down,
    second_gains,
):
    streams = tokens.shape[0]
    row_count = streams * SEG
    member_index = lax.axis_index("group")
    tok_rows = tokens.reshape(row_count, D).astype(F32)
    grad_out = cotangent.reshape(row_count, D).astype(F32)
    qkv_rows_low = w_qkv.astype(BF16)
    gain_count = norm_gains.shape[0]
    gain_row = jnp.pad(norm_gains.astype(BF16), (0, qkv_rows_low.shape[1] - gain_count))
    first_rows = lax.all_gather(
        jnp.concatenate([qkv_rows_low, gain_row[None]], axis=0), "group", axis=0, tiled=False
    )
    full_qkv = first_rows[:, :-1].reshape(D, -1)
    full_gains = first_rows[:, -1, :gain_count].reshape(-1)
    out_rows = w_out.shape[0]
    mixed = lax.all_gather(
        jnp.concatenate([w_out.astype(BF16), w_down.astype(BF16)], axis=0),
        "group",
        axis=0,
        tiled=False,
    )
    full_out = mixed[:, :out_rows].reshape(HQ * HD, D)
    full_down = mixed[:, out_rows:].reshape(FF, D)
    full_gu = lax.all_gather(w_gu.astype(BF16), "group", axis=0, tiled=True)
    gain_in, gain_pa, gain_pf, gain_po, gain_query, gain_key = split_gains(full_gains.astype(F32))
    start_row = member_index * SEG
    index_mine = start_row + jnp.arange(SEG, dtype=jnp.int32)
    boundary = lengths[:, 0]
    position_mine = index_mine[None, :] - jnp.where(
        index_mine[None, :] >= boundary[:, None], boundary[:, None], 0
    )
    info = jnp.concatenate(
        [
            jnp.stack([start_row, member_index // 4, member_index // 2 % 2, member_index % 2]),
            boundary,
        ]
    ).astype(jnp.int32)
    cosine, sine = angles(position_mine.reshape(row_count), HD)
    normed_in, pull_in = jax.vjp(rms_norm, tok_rows, gain_in)
    input_low = normed_in.astype(BF16)
    qkv_rows = jnp.dot(input_low, full_qkv, preferred_element_type=F32)

    def project(rows_in, gain_q_in, gain_k_in):
        return heads_in(rows_in, gain_q_in, gain_k_in, cosine, sine)

    head_outs, pull_heads = jax.vjp(project, qkv_rows, gain_query, gain_key)
    query_low = head_outs[0].astype(BF16).reshape(row_count, HQ * HD)
    kv_low = jnp.concatenate([head_outs[1].astype(BF16), head_outs[2].astype(BF16)], axis=1)
    blocks = gather_blocks(kv_low.reshape(streams, SEG, 2 * HD))
    attn_low, lse = attention_forward(info, query_low, blocks)
    attn_proj = jnp.dot(attn_low, full_out, preferred_element_type=F32)
    post_attn, pull_attn = jax.vjp(rms_norm, attn_proj, gain_pa)
    middle = tok_rows + post_attn
    normed_ff, pull_ff = jax.vjp(rms_norm, middle, gain_pf)
    ff_low = normed_ff.astype(BF16)
    gate_up = jnp.dot(ff_low, full_gu, preferred_element_type=F32)
    hidden, pull_geglu = jax.vjp(geglu, gate_up)
    hidden_low = hidden.astype(BF16)
    down_proj = jnp.dot(hidden_low, full_down, preferred_element_type=F32)
    post_ff, pull_post = jax.vjp(rms_norm, down_proj, gain_po)
    layer_out = (middle + post_ff).astype(BF16).reshape(streams, SEG, D)
    grad_down, grad_gain_po = pull_post(grad_out)
    down_low = grad_down.astype(BF16)
    wgrad_down = jnp.dot(hidden_low.T, down_low, preferred_element_type=F32)
    grad_hidden = jnp.dot(down_low, full_down.T, preferred_element_type=F32)
    (grad_gate_up,) = pull_geglu(grad_hidden)
    gate_up_low = grad_gate_up.astype(BF16)
    wgrad_gu = jnp.dot(ff_low.T, gate_up_low, preferred_element_type=F32)
    grad_normed_ff = jnp.dot(gate_up_low, full_gu.T, preferred_element_type=F32)
    grad_middle_ff, grad_gain_pf = pull_ff(grad_normed_ff)
    grad_middle = grad_out + grad_middle_ff
    grad_attn_proj, grad_gain_pa = pull_attn(grad_middle)
    proj_low = grad_attn_proj.astype(BF16)
    wgrad_out = jnp.dot(attn_low.T, proj_low, preferred_element_type=F32)
    grad_attn_low = jnp.dot(proj_low, full_out.T, preferred_element_type=F32).astype(BF16)
    shard_gu = lax.psum_scatter(wgrad_gu.astype(BF16), "group", scatter_dimension=0, tiled=True)
    shard_mixed = lax.psum_scatter(
        jnp.concatenate(
            [
                wgrad_out.astype(BF16).reshape(MEMBERS, out_rows, D),
                wgrad_down.astype(BF16).reshape(MEMBERS, FF // MEMBERS, D),
            ],
            axis=1,
        ),
        "group",
        scatter_dimension=0,
        tiled=False,
    )
    grad_query, far, near_far, near = attention_backward(
        info, query_low, attn_low, grad_attn_low, lse, blocks
    )
    grad_kv = scatter_blocks(far, near_far, near).reshape(row_count, 2 * HD)
    grad_qkv, grad_gain_q, grad_gain_k = pull_heads(
        (grad_query.reshape(row_count, HQ, HD), grad_kv[:, :HD], grad_kv[:, HD:])
    )
    qkv_low = grad_qkv.astype(BF16)
    wgrad_qkv = jnp.dot(input_low.T, qkv_low, preferred_element_type=F32)
    grad_normed_in = jnp.dot(qkv_low, full_qkv.T, preferred_element_type=F32)
    grad_tokens_in, grad_gain_in = pull_in(grad_normed_in)
    token_grad = (grad_middle + grad_tokens_in).reshape(streams, SEG, D)
    wgrad_gains = jnp.concatenate(
        [grad_gain_in, grad_gain_pa, grad_gain_pf, grad_gain_po, grad_gain_q, grad_gain_k]
    )
    gains_out = jnp.pad(
        wgrad_gains.astype(BF16).reshape(MEMBERS, 1, gain_count),
        ((0, 0), (0, 0), (0, wgrad_qkv.shape[1] - gain_count)),
    )
    shard_first = lax.psum_scatter(
        jnp.concatenate(
            [wgrad_qkv.astype(BF16).reshape(MEMBERS, D // MEMBERS, -1), gains_out], axis=1
        ),
        "group",
        scatter_dimension=0,
        tiled=False,
    )

    def over_replicas(shard):
        if lax.axis_size("replica") == 2:
            other = lax.ppermute(shard, "replica", [(0, 1), (1, 0)])
            return shard.astype(F32) + other.astype(F32)
        return lax.psum(shard, "replica").astype(F32)

    sum_gu, sum_mixed, sum_first = (
        over_replicas(shard_gu),
        over_replicas(shard_mixed),
        over_replicas(shard_first),
    )
    shard_qkv, shard_gains = sum_first[:-1], sum_first[-1, :gain_count]
    shard_out, shard_down = sum_mixed[:out_rows], sum_mixed[out_rows:]
    upd_qkv = adam_step(w_qkv, first_qkv, second_qkv, shard_qkv, RATE_MATRIX, DECAY_RATE)
    upd_out = adam_step(w_out, first_out, second_out, shard_out, RATE_MATRIX, DECAY_RATE)
    upd_gu = adam_step(w_gu, first_gu, second_gu, sum_gu, RATE_MATRIX, DECAY_RATE)
    upd_down = adam_step(w_down, first_down, second_down, shard_down, RATE_MATRIX, DECAY_RATE)
    upd_gains = adam_step(norm_gains, first_gains, second_gains, shard_gains, RATE_GAIN, 0.0)
    return (layer_out, token_grad, *upd_qkv, *upd_out, *upd_gu, *upd_down, *upd_gains)


def solution(mesh):
    in_specs = (
        P("replica", "group", None),
        P("replica", "group", None),
        P("replica", None),
        P("group", None),
        P("group", None),
        P("group", None),
        P("group", None),
        P("group"),
        P("group", None),
        P("group", None),
        P("group", None),
        P("group", None),
        P("group"),
        P("group", None),
        P("group", None),
        P("group", None),
        P("group", None),
        P("group"),
    )
    out_specs = (
        P("replica", "group", None),
        P("replica", "group", None),
        P("group", None),
        P("group", None),
        P("group", None),
        P("group", None),
        P("group", None),
        P("group", None),
        P("group", None),
        P("group", None),
        P("group", None),
        P("group", None),
        P("group", None),
        P("group", None),
        P("group"),
        P("group"),
        P("group"),
    )
    return jax.shard_map(
        per_device, mesh=mesh, in_specs=in_specs, out_specs=out_specs, check_vma=False
    )
```

```python
import math

import jax
import jax.numpy as jnp
from jax import lax
from jax.experimental import pallas as pl
from jax.experimental.pallas import tpu as pltpu
from jax.sharding import PartitionSpec as P

D = 640
HQ = 4
HD = 256
FF = 2048
SEG = 256
STEP = 10


EPS_NORM = 1e-06
BETA_ONE = 0.9
BETA_TWO = 0.999
ADAM_EPS = 1e-08
RATE_MATRIX = 0.1
RATE_GAIN = 0.5
DECAY_RATE = 0.1
ROPE_BASE = 1000000.0
NEGATIVE = -1e30
SCALE_SCORE = 0.0625


def rms_norm(values, gain_row):
    factor = lax.rsqrt(jnp.mean(values * values, axis=-1, keepdims=True) + EPS_NORM)
    return values * factor * gain_row


def angles(position, width):
    half_width = width // 2
    frequency = jnp.exp(
        jnp.arange(half_width, dtype=jnp.float32) * (-2.0 * math.log(ROPE_BASE) / width)
    )
    angle_table = position.astype(jnp.float32)[:, None] * frequency[None, :]
    return (jnp.cos(angle_table), jnp.sin(angle_table))


def rotate(values, cosine, sine):
    half_width = values.shape[-1] // 2
    leading = values[..., :half_width]
    trailing = values[..., half_width:]
    return jnp.concatenate(
        [leading * cosine - trailing * sine, trailing * cosine + leading * sine], axis=-1
    )


def layout(lengths, total):
    seq_ends = jnp.cumsum(lengths)
    seq_starts = seq_ends - lengths
    stream_index = jnp.arange(total, dtype=jnp.int32)
    segment = jnp.sum((stream_index[:, None] >= seq_ends[None, :]).astype(jnp.int32), axis=1)
    seq_begin = jnp.max(
        jnp.where(stream_index[:, None] >= seq_starts[None, :], seq_starts[None, :], 0), axis=1
    )
    return (segment, stream_index - seq_begin)


def heads_in(qkv_rows, gain_query, gain_key, cosine, sine):
    row_count = qkv_rows.shape[0]
    queries = qkv_rows[:, : HQ * HD].reshape(row_count, HQ, HD)
    keys_pre = qkv_rows[:, HQ * HD : (HQ + 1) * HD]
    values_pre = qkv_rows[:, (HQ + 1) * HD :]
    query_rot = rotate(rms_norm(queries, gain_query), cosine[:, None, :], sine[:, None, :])
    key_rot = rotate(rms_norm(keys_pre, gain_key), cosine, sine)
    return (query_rot, key_rot, values_pre)


def geglu(gate_up):
    return jax.nn.gelu(gate_up[:, :FF], approximate=True) * gate_up[:, FF:]


def split_gains(gain_all):
    return (
        gain_all[0:D],
        gain_all[D : 2 * D],
        gain_all[2 * D : 3 * D],
        gain_all[3 * D : 4 * D],
        gain_all[4 * D : 4 * D + HD],
        gain_all[4 * D + HD : 4 * D + 2 * HD],
    )


def adam_step(master, moment_one, moment_two, gradient, rate, decay):
    moment_new = BETA_ONE * moment_one + (1.0 - BETA_ONE) * gradient
    square_new = BETA_TWO * moment_two + (1.0 - BETA_TWO) * gradient * gradient
    moment_hat = moment_new / (1.0 - BETA_ONE**STEP)
    square_hat = square_new / (1.0 - BETA_TWO**STEP)
    master_new = master * (1.0 - rate * decay) - rate * moment_hat / (
        jnp.sqrt(square_hat) + ADAM_EPS
    )
    return (moment_new, square_new, master_new)


LOG2E = 1.4426950408889634
MEMBERS = 16
REACH = 3
BLOCKS = 4 * REACH
NT = (((1,), (1,)), ((), ()))
TN = (((0,), (0,)), ((), ()))
F32 = jnp.float32
BF16 = jnp.bfloat16


def ring_up(values):
    return lax.ppermute(values, "group", [(i, (i + 4) % MEMBERS) for i in range(MEMBERS)])


def line_up(values, lowest):
    return lax.ppermute(values, "group", [(i, i + 4) for i in range(4 * lowest, MEMBERS - 4)])


def line_down(values, lowest):
    return lax.ppermute(values, "group", [(i, i - 4) for i in range(4 * lowest, MEMBERS)])


def swap_x(values):
    return lax.ppermute(values, "group", [(i, i ^ 2) for i in range(MEMBERS)])


def swap_core(values):
    return lax.ppermute(values, "group", [(i, i ^ 1) for i in range(MEMBERS)])


def spread(lines):
    near = []
    for line in lines:
        near += [line, swap_x(line)]
    return near + [swap_core(block) for block in near]


def gather_ring(own):
    lines = [own]
    for _ in range(3):
        lines.append(ring_up(lines[-1]))
    return spread(lines)


def gather_keys(own):
    first = line_up(own, 0)
    return spread([own, first, line_up(first, 1)])


def scatter_keys(far, near_far, near):
    running = None
    for k in range(REACH - 1, -1, -1):
        came = swap_core(far[k]).astype(F32)
        over = swap_x((near_far[k].astype(F32) + came[1]).astype(BF16))
        total = near[k].astype(F32) + came[0] + over.astype(F32)
        if running is not None:
            total = total + running.astype(F32)
        if k:
            running = line_down(total.astype(BF16), k)
    return total


def scatter_ring(near, far):
    came = swap_core(far)
    running = None
    for k in (3, 2, 1, 0):
        over = swap_x((near[2 * k + 1].astype(F32) + came[2 * k + 1].astype(F32)).astype(BF16))
        total = near[2 * k].astype(F32) + came[2 * k].astype(F32) + over.astype(F32)
        if running is not None:
            total = total + running.astype(F32)
        if k:
            running = ring_up(total.astype(BF16))
    return total


def owner_up(info, place):
    cr, k, xr = place // 8, place // 2 % 4, place % 2
    return ((info[1] + k) & 3) * 4 + (info[2] ^ xr) * 2 + (info[3] ^ cr)


def order_kernel(info, *refs):
    blocks = refs[:MEMBERS]
    full_ref, gains_ref, rows = refs[MEMBERS:]
    count = rows.shape[0] // MEMBERS
    for place in range(MEMBERS):
        cr, k, xr = place // 8, place // 2 % 4, place % 2
        owner = ((info[1] - k) & 3) * 4 + (info[2] ^ xr) * 2 + (info[3] ^ cr)
        values = blocks[place][...].astype(F32)
        rows[pl.ds(pl.multiple_of(owner * count, 8), count)] = values[:count]
        gains_ref[pl.ds(owner, 1)] = values[count : count + 1]
    full_ref[...] = rows[...].astype(BF16)


def order_rows(info, blocks):
    rows, columns = blocks[0].shape
    count = rows // 8 * 8
    vmem = pl.BlockSpec(memory_space=pltpu.VMEM)
    return pl.pallas_call(
        order_kernel,
        out_shape=(
            jax.ShapeDtypeStruct((MEMBERS * count, columns), BF16),
            jax.ShapeDtypeStruct((MEMBERS, columns), F32),
        ),
        in_specs=[pl.BlockSpec(memory_space=pltpu.SMEM)] + [vmem] * MEMBERS,
        out_specs=(vmem, vmem),
        scratch_shapes=[pltpu.VMEM((MEMBERS * count, columns), F32)],
        compiler_params=pltpu.CompilerParams(vmem_limit_bytes=32 * 1024 * 1024),
        cost_estimate=pl.CostEstimate(flops=0, bytes_accessed=4_000_000, transcendentals=0),
        name="order_rows",
    )(info, *blocks)


def gradient_kernel(tile, pairs, extra, info, *refs):
    operands = refs[: 2 * pairs + extra]
    near, far = refs[2 * pairs + extra : 2 * pairs + extra + 2]
    sums = refs[2 * pairs + extra + 2 :]
    columns = near.shape[2]
    for begin in range(0, columns, tile):
        at = slice(begin, begin + tile)
        for pair in range(pairs):
            left, right = operands[2 * pair], operands[2 * pair + 1]
            sums[pair][...] = lax.dot_general(
                left[...], right[:, at], TN, preferred_element_type=F32
            )
        for place in range(MEMBERS):
            owner = owner_up(info, place)
            parts = []
            for pair in range(pairs):
                count = sums[pair].shape[0] // MEMBERS
                parts.append(sums[pair][pl.ds(pl.multiple_of(owner * count, 8), count)])
            if extra:
                row = operands[2 * pairs][pl.ds(owner, 1), at]
                parts.append(jnp.broadcast_to(row, (8, tile)))
            block = jnp.concatenate(parts, axis=0) if len(parts) > 1 else parts[0]
            target = far if place >= 8 else near
            target[place % 8, :, at] = block.astype(BF16)


def weight_gradient(info, pairs, gains, tile, name):
    columns = pairs[0][1].shape[1]
    tokens_here = pairs[0][0].shape[0]
    counts = [left.shape[1] // MEMBERS for left, _ in pairs]
    rows = sum(counts) + (8 if gains is not None else 0)
    operands = [operand for pair in pairs for operand in pair]
    if gains is not None:
        operands.append(gains)
    shape = jax.ShapeDtypeStruct((MEMBERS // 2, rows, columns), BF16)
    vmem = pl.BlockSpec(memory_space=pltpu.VMEM)
    return pl.pallas_call(
        lambda *refs: gradient_kernel(tile, len(pairs), int(gains is not None), *refs),
        out_shape=(shape, shape),
        in_specs=[pl.BlockSpec(memory_space=pltpu.SMEM)] + [vmem] * len(operands),
        out_specs=(vmem, vmem),
        scratch_shapes=[pltpu.VMEM((MEMBERS * count, tile), F32) for count in counts],
        compiler_params=pltpu.CompilerParams(vmem_limit_bytes=48 * 1024 * 1024),
        cost_estimate=pl.CostEstimate(
            flops=2 * tokens_here * columns * MEMBERS * sum(counts),
            bytes_accessed=4 * MEMBERS * rows * columns,
            transcendentals=0,
        ),
        name=name,
    )(info, *operands)


def key_range(info, stream):
    first = info[0]
    bound = info[4 + stream]
    low = jnp.where(first >= bound, bound, 0)
    return first, bound, low // SEG, first // SEG + 1


def load_blocks(info, blocks, kv, sem):
    z, x, c = info[1], info[2], info[3]
    copies = []
    for place in range(len(blocks)):
        cr, k, xr = place // (2 * REACH), place // 2 % REACH, place % 2
        owner = ((z - k) & 3) * 4 + (x ^ xr) * 2 + (c ^ cr)
        copies.append(pltpu.make_async_copy(blocks[place], kv.at[owner], sem.at[place]))
    for copy in copies:
        copy.start()
    return copies


def forward_kernel(info, q_ref, *refs):
    blocks = refs[:BLOCKS]
    o_ref, lse_ref, kv, acc, total, sem = refs[BLOCKS:]
    copies = load_blocks(info, blocks, kv, sem)
    for copy in copies:
        copy.wait()

    def one_stream(stream, carry):
        first, bound, begin, end = key_range(info, stream)
        acc[...] = jnp.zeros_like(acc)
        total[...] = jnp.zeros_like(total)
        mine = pl.ds(pl.multiple_of(stream * SEG, SEG), SEG)
        row = first + lax.broadcasted_iota(jnp.int32, (SEG, SEG), 0)
        start = jnp.where(row >= bound, bound, 0)

        def visit(j, carry):
            keys = kv[j, stream, :, 0:HD]
            values = kv[j, stream, :, HD : 2 * HD]
            col = j * SEG + lax.broadcasted_iota(jnp.int32, (SEG, SEG), 1)
            mask = (col <= row) & (col >= start)
            for head in range(HQ):
                rows = slice(head * SEG, (head + 1) * SEG)
                query = q_ref[mine, head * HD : (head + 1) * HD]
                score = lax.dot_general(query, keys, NT, preferred_element_type=F32)
                prob = jnp.where(mask, jnp.exp2(score * (SCALE_SCORE * LOG2E)), 0.0)
                total[rows] += prob[:, 0:128] + prob[:, 128:256]
                acc[rows] += jnp.dot(prob.astype(BF16), values, preferred_element_type=F32)
            return carry

        lax.fori_loop(begin, end, visit, 0)
        for head in range(HQ):
            rows = slice(head * SEG, (head + 1) * SEG)
            part = total[rows]
            out = acc[rows] / jnp.sum(part, axis=1, keepdims=True)
            o_ref[mine, head * HD : (head + 1) * HD] = out.astype(BF16)
            lse_ref[stream, :, rows] = jnp.log2(jnp.sum(part.T, axis=0, keepdims=True))
        return carry

    lax.fori_loop(0, 2, one_stream, 0)


def attention_forward(info, query, blocks):
    vmem = pl.BlockSpec(memory_space=pltpu.VMEM)
    return pl.pallas_call(
        forward_kernel,
        out_shape=(
            jax.ShapeDtypeStruct((2 * SEG, HQ * HD), BF16),
            jax.ShapeDtypeStruct((2, 1, HQ * SEG), F32),
        ),
        in_specs=[pl.BlockSpec(memory_space=pltpu.SMEM), vmem]
        + [pl.BlockSpec(memory_space=pl.ANY)] * BLOCKS,
        out_specs=(vmem, vmem),
        scratch_shapes=[
            pltpu.VMEM((MEMBERS, 2, SEG, 2 * HD), BF16),
            pltpu.VMEM((HQ * SEG, HD), F32),
            pltpu.VMEM((HQ * SEG, 128), F32),
            pltpu.SemaphoreType.DMA((BLOCKS,)),
        ],
        compiler_params=pltpu.CompilerParams(vmem_limit_bytes=40 * 1024 * 1024),
        cost_estimate=pl.CostEstimate(
            flops=7_000_000_000, bytes_accessed=9_000_000, transcendentals=7_000_000
        ),
        name="attention_forward",
    )(info, query, *blocks)


def backward_kernel(info, q_ref, o_ref, do_ref, lse_ref, *refs):
    blocks = refs[:BLOCKS]
    dq_ref = refs[BLOCKS]
    far = refs[BLOCKS + 1 : BLOCKS + 1 + REACH]
    near_far = refs[BLOCKS + 1 + REACH : BLOCKS + 1 + 2 * REACH]
    near = refs[BLOCKS + 1 + 2 * REACH : BLOCKS + 1 + 3 * REACH]
    kv, dkv, qs, qt, dos, dot_, dqt, delta, sem, out_sem = refs[BLOCKS + 1 + 3 * REACH :]
    copies = load_blocks(info, blocks, kv, sem)
    z, x, c = info[1], info[2], info[3]

    def clean(place, carry):
        dkv[place] = jnp.zeros((2, SEG, 2 * HD), BF16)
        return carry

    lax.fori_loop(0, BLOCKS, clean, 0)
    for copy in copies:
        copy.wait()

    def one_stream(stream, carry):
        first, bound, begin, end = key_range(info, stream)
        mine = pl.ds(pl.multiple_of(stream * SEG, SEG), SEG)
        for head in range(HQ):
            rows = slice(head * SEG, (head + 1) * SEG)
            lanes = slice(head * HD, (head + 1) * HD)
            query = q_ref[mine, lanes]
            grad = do_ref[mine, lanes]
            qs[rows] = query
            dos[rows] = grad
            qt[:, rows] = query.T
            dot_[:, rows] = grad.T
            both = grad.astype(F32) * o_ref[mine, lanes].astype(F32)
            delta[:, rows] = jnp.sum((both[:, 0:128] + both[:, 128:256]).T, axis=0, keepdims=True)
        dqt[...] = jnp.zeros_like(dqt)
        shape = (SEG, HQ * SEG)

        def visit(j, carry):
            keys = kv[j, stream, :, 0:HD]
            values = kv[j, stream, :, HD : 2 * HD]
            score = jnp.dot(keys, qt[...], preferred_element_type=F32)
            prob = jnp.exp2(score * (SCALE_SCORE * LOG2E) - lse_ref[stream])
            row = first + (lax.broadcasted_iota(jnp.int32, (1, HQ * SEG), 1) & (SEG - 1))
            start = jnp.where(row >= bound, bound, 0)
            col = j * SEG + lax.broadcasted_iota(jnp.int32, shape, 0)
            prob = jnp.where((col <= row) & (col >= start), prob, 0.0)
            dprob = jnp.dot(values, dot_[...], preferred_element_type=F32)
            dscore = (prob * (dprob - delta[...])).astype(BF16)
            dv = jnp.dot(prob.astype(BF16), dos[...], preferred_element_type=F32)
            dk = jnp.dot(dscore, qs[...], preferred_element_type=F32)
            dqt[...] += jnp.dot(keys.T, dscore, preferred_element_type=F32)
            place = ((j & 1) ^ c) * (2 * REACH) + (z - (j >> 2)) * 2 + (((j >> 1) & 1) ^ x)
            dkv[place, stream, :, 0:HD] = (dk * SCALE_SCORE).astype(BF16)
            dkv[place, stream, :, HD : 2 * HD] = dv.astype(BF16)
            return carry

        lax.fori_loop(begin, end, visit, 0)
        for head in range(HQ):
            rows = slice(head * SEG, (head + 1) * SEG)
            dq_ref[mine, head * HD : (head + 1) * HD] = dqt[:, rows].T * SCALE_SCORE
        return carry

    lax.fori_loop(0, 2, one_stream, 0)
    outs = []
    for k in range(REACH):
        outs.append((dkv.at[pl.ds(2 * REACH + 2 * k, 2)], far[k]))
        outs.append((dkv.at[2 * k + 1], near_far[k]))
        outs.append((dkv.at[2 * k], near[k]))
    copies = [
        pltpu.make_async_copy(source, target, out_sem.at[n])
        for n, (source, target) in enumerate(outs)
    ]
    for copy in copies:
        copy.start()
    for copy in copies:
        copy.wait()


def attention_backward(info, query, out, grad_out, lse, blocks):
    one = jax.ShapeDtypeStruct((2, SEG, 2 * HD), BF16)
    two = jax.ShapeDtypeStruct((2, 2, SEG, 2 * HD), BF16)
    vmem = pl.BlockSpec(memory_space=pltpu.VMEM)
    anywhere = pl.BlockSpec(memory_space=pl.ANY)
    result = pl.pallas_call(
        backward_kernel,
        out_shape=[jax.ShapeDtypeStruct((2 * SEG, HQ * HD), F32)]
        + [two] * REACH
        + [one] * (2 * REACH),
        in_specs=[pl.BlockSpec(memory_space=pltpu.SMEM)] + [vmem] * 4 + [anywhere] * BLOCKS,
        out_specs=[vmem] + [anywhere] * (3 * REACH),
        scratch_shapes=[
            pltpu.VMEM((MEMBERS, 2, SEG, 2 * HD), BF16),
            pltpu.VMEM((BLOCKS, 2, SEG, 2 * HD), BF16),
            pltpu.VMEM((HQ * SEG, HD), BF16),
            pltpu.VMEM((HD, HQ * SEG), BF16),
            pltpu.VMEM((HQ * SEG, HD), BF16),
            pltpu.VMEM((HD, HQ * SEG), BF16),
            pltpu.VMEM((HD, HQ * SEG), F32),
            pltpu.VMEM((1, HQ * SEG), F32),
            pltpu.SemaphoreType.DMA((BLOCKS,)),
            pltpu.SemaphoreType.DMA((3 * REACH,)),
        ],
        compiler_params=pltpu.CompilerParams(vmem_limit_bytes=52 * 1024 * 1024),
        cost_estimate=pl.CostEstimate(
            flops=17_000_000_000, bytes_accessed=20_000_000, transcendentals=7_000_000
        ),
        name="attention_backward",
    )(info, query, out, grad_out, lse, *blocks)
    return result[0], result[1 : 1 + REACH], result[1 + REACH : 1 + 2 * REACH], result[1 + 2 * REACH :]


def per_device(
    tokens,
    cotangent,
    lengths,
    w_qkv,
    w_out,
    w_gu,
    w_down,
    norm_gains,
    first_qkv,
    first_out,
    first_gu,
    first_down,
    first_gains,
    second_qkv,
    second_out,
    second_gu,
    second_down,
    second_gains,
):
    streams = tokens.shape[0]
    row_count = streams * SEG
    member_index = lax.axis_index("group")
    tok_rows = tokens.reshape(row_count, D).astype(F32)
    grad_out = cotangent.reshape(row_count, D).astype(F32)
    qkv_rows_low = w_qkv.astype(BF16)
    gain_count = norm_gains.shape[0]
    gain_row = jnp.pad(norm_gains.astype(BF16), (0, qkv_rows_low.shape[1] - gain_count))
    start_row = member_index * SEG
    boundary = lengths[:, 0]
    info = jnp.concatenate(
        [
            jnp.stack([start_row, member_index // 4, member_index // 2 % 2, member_index % 2]),
            boundary,
        ]
    ).astype(jnp.int32)
    full_qkv, gain_rows = order_rows(
        info, gather_ring(jnp.concatenate([qkv_rows_low, gain_row[None]], axis=0))
    )
    full_gains = gain_rows[:, :gain_count].reshape(-1)
    out_rows = w_out.shape[0]
    mixed = lax.all_gather(
        jnp.concatenate([w_out.astype(BF16), w_down.astype(BF16)], axis=0),
        "group",
        axis=0,
        tiled=False,
    )
    full_out = mixed[:, :out_rows].reshape(HQ * HD, D)
    full_down = mixed[:, out_rows:].reshape(FF, D)
    full_gu = lax.all_gather(w_gu.astype(BF16), "group", axis=0, tiled=True)
    gain_in, gain_pa, gain_pf, gain_po, gain_query, gain_key = split_gains(full_gains)
    index_mine = start_row + jnp.arange(SEG, dtype=jnp.int32)
    position_mine = index_mine[None, :] - jnp.where(
        index_mine[None, :] >= boundary[:, None], boundary[:, None], 0
    )
    cosine, sine = angles(position_mine.reshape(row_count), HD)
    normed_in, pull_in = jax.vjp(rms_norm, tok_rows, gain_in)
    input_low = normed_in.astype(BF16)
    qkv_rows = jnp.dot(input_low, full_qkv, preferred_element_type=F32)

    def project(rows_in, gain_q_in, gain_k_in):
        return heads_in(rows_in, gain_q_in, gain_k_in, cosine, sine)

    head_outs, pull_heads = jax.vjp(project, qkv_rows, gain_query, gain_key)
    query_low = head_outs[0].astype(BF16).reshape(row_count, HQ * HD)
    kv_low = jnp.concatenate([head_outs[1].astype(BF16), head_outs[2].astype(BF16)], axis=1)
    blocks = gather_keys(kv_low.reshape(streams, SEG, 2 * HD))
    attn_low, lse = attention_forward(info, query_low, blocks)
    attn_proj = jnp.dot(attn_low, full_out, preferred_element_type=F32)
    post_attn, pull_attn = jax.vjp(rms_norm, attn_proj, gain_pa)
    middle = tok_rows + post_attn
    normed_ff, pull_ff = jax.vjp(rms_norm, middle, gain_pf)
    ff_low = normed_ff.astype(BF16)
    gate_up = jnp.dot(ff_low, full_gu, preferred_element_type=F32)
    hidden, pull_geglu = jax.vjp(geglu, gate_up)
    hidden_low = hidden.astype(BF16)
    down_proj = jnp.dot(hidden_low, full_down, preferred_element_type=F32)
    post_ff, pull_post = jax.vjp(rms_norm, down_proj, gain_po)
    layer_out = (middle + post_ff).astype(BF16).reshape(streams, SEG, D)
    grad_down, grad_gain_po = pull_post(grad_out)
    down_low = grad_down.astype(BF16)
    grad_hidden = jnp.dot(down_low, full_down.T, preferred_element_type=F32)
    (grad_gate_up,) = pull_geglu(grad_hidden)
    gate_up_low = grad_gate_up.astype(BF16)
    parts_gu = weight_gradient(info, [(ff_low, gate_up_low)], None, 512, "gradient_gu")
    grad_normed_ff = jnp.dot(gate_up_low, full_gu.T, preferred_element_type=F32)
    grad_middle_ff, grad_gain_pf = pull_ff(grad_normed_ff)
    grad_middle = grad_out + grad_middle_ff
    grad_attn_proj, grad_gain_pa = pull_attn(grad_middle)
    proj_low = grad_attn_proj.astype(BF16)
    grad_attn_low = jnp.dot(proj_low, full_out.T, preferred_element_type=F32).astype(BF16)
    parts_mixed = weight_gradient(
        info, [(attn_low, proj_low), (hidden_low, down_low)], None, 640, "gradient_mixed"
    )
    grad_attn_low, parts_gu, parts_mixed = lax.optimization_barrier(
        (grad_attn_low, parts_gu, parts_mixed)
    )
    shard_gu = scatter_ring(*parts_gu).astype(BF16)
    shard_mixed = scatter_ring(*parts_mixed).astype(BF16)
    grad_query, far, near_far, near = attention_backward(
        info, query_low, attn_low, grad_attn_low, lse, blocks
    )
    grad_kv = scatter_keys(far, near_far, near).reshape(row_count, 2 * HD)
    grad_qkv, grad_gain_q, grad_gain_k = pull_heads(
        (grad_query.reshape(row_count, HQ, HD), grad_kv[:, :HD], grad_kv[:, HD:])
    )
    qkv_low = grad_qkv.astype(BF16)
    grad_normed_in = jnp.dot(qkv_low, full_qkv.T, preferred_element_type=F32)
    grad_tokens_in, grad_gain_in = pull_in(grad_normed_in)
    token_grad = (grad_middle + grad_tokens_in).reshape(streams, SEG, D)
    wgrad_gains = jnp.concatenate(
        [grad_gain_in, grad_gain_pa, grad_gain_pf, grad_gain_po, grad_gain_q, grad_gain_k]
    )
    gains_out = jnp.pad(
        wgrad_gains.reshape(MEMBERS, gain_count), ((0, 0), (0, qkv_low.shape[1] - gain_count))
    )
    parts_first = weight_gradient(info, [(input_low, qkv_low)], gains_out, 512, "gradient_qkv")
    shard_first = scatter_ring(*parts_first).astype(BF16)

    def over_replicas(shard):
        if lax.axis_size("replica") == 2:
            other = lax.ppermute(shard, "replica", [(0, 1), (1, 0)])
            return shard.astype(F32) + other.astype(F32)
        return lax.psum(shard, "replica").astype(F32)

    sum_gu, sum_mixed, sum_first = (
        over_replicas(shard_gu),
        over_replicas(shard_mixed),
        over_replicas(shard_first),
    )
    shard_qkv, shard_gains = sum_first[:-8], sum_first[-1, :gain_count]
    shard_out, shard_down = sum_mixed[:out_rows], sum_mixed[out_rows:]
    upd_qkv = adam_step(w_qkv, first_qkv, second_qkv, shard_qkv, RATE_MATRIX, DECAY_RATE)
    upd_out = adam_step(w_out, first_out, second_out, shard_out, RATE_MATRIX, DECAY_RATE)
    upd_gu = adam_step(w_gu, first_gu, second_gu, sum_gu, RATE_MATRIX, DECAY_RATE)
    upd_down = adam_step(w_down, first_down, second_down, shard_down, RATE_MATRIX, DECAY_RATE)
    upd_gains = adam_step(norm_gains, first_gains, second_gains, shard_gains, RATE_GAIN, 0.0)
    return (layer_out, token_grad, *upd_qkv, *upd_out, *upd_gu, *upd_down, *upd_gains)


def solution(mesh):
    in_specs = (
        P("replica", "group", None),
        P("replica", "group", None),
        P("replica", None),
        P("group", None),
        P("group", None),
        P("group", None),
        P("group", None),
        P("group"),
        P("group", None),
        P("group", None),
        P("group", None),
        P("group", None),
        P("group"),
        P("group", None),
        P("group", None),
        P("group", None),
        P("group", None),
        P("group"),
    )
    out_specs = (
        P("replica", "group", None),
        P("replica", "group", None),
        P("group", None),
        P("group", None),
        P("group", None),
        P("group", None),
        P("group", None),
        P("group", None),
        P("group", None),
        P("group", None),
        P("group", None),
        P("group", None),
        P("group", None),
        P("group", None),
        P("group"),
        P("group"),
        P("group"),
    )
    return jax.shard_map(
        per_device, mesh=mesh, in_specs=in_specs, out_specs=out_specs, check_vma=False
    )
```

```python
import math

import jax
import jax.numpy as jnp
from jax import lax
from jax.experimental import pallas as pl
from jax.experimental.pallas import tpu as pltpu
from jax.sharding import PartitionSpec as P

D = 640
HQ = 4
HD = 256
FF = 2048
SEG = 256
STEP = 10


EPS_NORM = 1e-06
BETA_ONE = 0.9
BETA_TWO = 0.999
ADAM_EPS = 1e-08
RATE_MATRIX = 0.1
RATE_GAIN = 0.5
DECAY_RATE = 0.1
ROPE_BASE = 1000000.0
NEGATIVE = -1e30
SCALE_SCORE = 0.0625


def rms_norm(values, gain_row):
    factor = lax.rsqrt(jnp.mean(values * values, axis=-1, keepdims=True) + EPS_NORM)
    return values * factor * gain_row


def angles(position, width):
    half_width = width // 2
    frequency = jnp.exp(
        jnp.arange(half_width, dtype=jnp.float32) * (-2.0 * math.log(ROPE_BASE) / width)
    )
    angle_table = position.astype(jnp.float32)[:, None] * frequency[None, :]
    return (jnp.cos(angle_table), jnp.sin(angle_table))


def rotate(values, cosine, sine):
    half_width = values.shape[-1] // 2
    leading = values[..., :half_width]
    trailing = values[..., half_width:]
    return jnp.concatenate(
        [leading * cosine - trailing * sine, trailing * cosine + leading * sine], axis=-1
    )


def layout(lengths, total):
    seq_ends = jnp.cumsum(lengths)
    seq_starts = seq_ends - lengths
    stream_index = jnp.arange(total, dtype=jnp.int32)
    segment = jnp.sum((stream_index[:, None] >= seq_ends[None, :]).astype(jnp.int32), axis=1)
    seq_begin = jnp.max(
        jnp.where(stream_index[:, None] >= seq_starts[None, :], seq_starts[None, :], 0), axis=1
    )
    return (segment, stream_index - seq_begin)


def head_in(values, gain_row, cosine, sine):
    return rotate(rms_norm(values, gain_row), cosine, sine)


def geglu(gate_up):
    return jax.nn.gelu(gate_up[:, :FF], approximate=True) * gate_up[:, FF:]


def split_gains(gain_all):
    return (
        gain_all[0:D],
        gain_all[D : 2 * D],
        gain_all[2 * D : 3 * D],
        gain_all[3 * D : 4 * D],
        gain_all[4 * D : 4 * D + HD],
        gain_all[4 * D + HD : 4 * D + 2 * HD],
    )


def adam_step(master, moment_one, moment_two, gradient, rate, decay):
    moment_new = BETA_ONE * moment_one + (1.0 - BETA_ONE) * gradient
    square_new = BETA_TWO * moment_two + (1.0 - BETA_TWO) * gradient * gradient
    moment_hat = moment_new / (1.0 - BETA_ONE**STEP)
    square_hat = square_new / (1.0 - BETA_TWO**STEP)
    master_new = master * (1.0 - rate * decay) - rate * moment_hat / (
        jnp.sqrt(square_hat) + ADAM_EPS
    )
    return (moment_new, square_new, master_new)


LOG2E = 1.4426950408889634
KEYS = 512
MEMBERS = 16
REACH = 3
BLOCKS = 4 * REACH
NT = (((1,), (1,)), ((), ()))
TN = (((0,), (0,)), ((), ()))
F32 = jnp.float32
BF16 = jnp.bfloat16


def shift_z(values, k):
    return lax.ppermute(values, "group", [(i, (i + 4 * k) % MEMBERS) for i in range(MEMBERS)])


def line_up(values, k):
    return lax.ppermute(values, "group", [(i, i + 4 * k) for i in range(MEMBERS - 4 * k)])


def line_down(values, k):
    return lax.ppermute(values, "group", [(i, i - 4 * k) for i in range(4 * k, MEMBERS)])


def swap_x(values):
    return lax.ppermute(values, "group", [(i, i ^ 2) for i in range(MEMBERS)])


def swap_core(values):
    return lax.ppermute(values, "group", [(i, i ^ 1) for i in range(MEMBERS)])


def spread(lines):
    near = lines + [swap_x(line) for line in lines]
    return near + [swap_core(block) for block in near]


def gather_all(own):
    return spread([own] + [shift_z(own, k) for k in (1, 2, 3)])


def gather_keys(own):
    return spread([own] + [line_up(own, k) for k in range(1, REACH)])


def scatter_keys(far, near_far, near):
    totals = [None] * REACH
    for k in range(REACH - 1, -1, -1):
        came = swap_core(far[k]).astype(F32)
        over = swap_x((near_far[k].astype(F32) + came[1]).astype(BF16))
        totals[k] = near[k].astype(F32) + came[0] + over.astype(F32)
        if k:
            totals[k] = line_down(totals[k].astype(BF16), k).astype(F32)
    return totals[0] + totals[1] + totals[2]


def scatter_x(near, came):
    return swap_x((near[4:].astype(F32) + came[4:].astype(F32)).astype(BF16))


def scatter_z(near, came, over):
    total = [near[k].astype(F32) + came[k].astype(F32) + over[k].astype(F32) for k in range(4)]
    for k in (1, 2, 3):
        total[0] = total[0] + shift_z(total[k].astype(BF16), k).astype(F32)
    return total[0].astype(BF16)


def over_replicas(shard):
    if lax.axis_size("replica") == 2:
        other = lax.ppermute(shard, "replica", [(0, 1), (1, 0)])
        return shard.astype(F32) + other.astype(F32)
    return lax.psum(shard, "replica").astype(F32)


def owner_up(info, place):
    cr, xr, k = place // 8, place // 4 % 2, place % 4
    return ((info[1] + k) & 3) * 4 + (info[2] ^ xr) * 2 + (info[3] ^ cr)


def order_kernel(info, *refs):
    blocks = refs[:MEMBERS]
    full_ref, rows = refs[MEMBERS], refs[-1]
    count = rows.shape[0] // MEMBERS
    for place in range(MEMBERS):
        cr, xr, k = place // 8, place // 4 % 2, place % 4
        owner = ((info[1] - k) & 3) * 4 + (info[2] ^ xr) * 2 + (info[3] ^ cr)
        values = blocks[place][...].astype(F32)
        rows[pl.ds(pl.multiple_of(owner * count, 8), count)] = values[:count]
        if len(refs) > MEMBERS + 2:
            refs[MEMBERS + 1][pl.ds(owner, 1)] = values[count : count + 1]
    full_ref[...] = rows[...].astype(BF16)


def order_rows(info, blocks, name):
    rows, columns = blocks[0].shape
    count = rows // 8 * 8
    vmem = pl.BlockSpec(memory_space=pltpu.VMEM)
    shapes = [jax.ShapeDtypeStruct((MEMBERS * count, columns), BF16)]
    if rows > count:
        shapes.append(jax.ShapeDtypeStruct((MEMBERS, columns), F32))
    return pl.pallas_call(
        order_kernel,
        out_shape=shapes,
        in_specs=[pl.BlockSpec(memory_space=pltpu.SMEM)] + [vmem] * MEMBERS,
        out_specs=[vmem] * len(shapes),
        scratch_shapes=[pltpu.VMEM((MEMBERS * count, columns), F32)],
        compiler_params=pltpu.CompilerParams(vmem_limit_bytes=32 * 1024 * 1024),
        cost_estimate=pl.CostEstimate(flops=0, bytes_accessed=4_000_000, transcendentals=0),
        name=name,
    )(info, *blocks)


def gradient_kernel(tile, pairs, extra, info, *refs):
    operands = refs[: 2 * pairs + extra]
    near, far = refs[2 * pairs + extra : 2 * pairs + extra + 2]
    sums = refs[2 * pairs + extra + 2 :]
    columns = near.shape[2]
    for begin in range(0, columns, tile):
        at = slice(begin, begin + tile)
        for pair in range(pairs):
            left, right = operands[2 * pair], operands[2 * pair + 1]
            sums[pair][...] = lax.dot_general(
                left[...], right[:, at], TN, preferred_element_type=F32
            )
        for place in range(MEMBERS):
            owner = owner_up(info, place)
            parts = []
            for pair in range(pairs):
                count = sums[pair].shape[0] // MEMBERS
                parts.append(sums[pair][pl.ds(pl.multiple_of(owner * count, 8), count)])
            if extra:
                row = operands[2 * pairs][pl.ds(owner, 1), at]
                parts.append(jnp.broadcast_to(row, (8, tile)))
            block = jnp.concatenate(parts, axis=0) if len(parts) > 1 else parts[0]
            target = far if place >= 8 else near
            target[place % 8, :, at] = block.astype(BF16)


def weight_gradient(info, pairs, gains, tile, name):
    columns = pairs[0][1].shape[1]
    tokens_here = pairs[0][0].shape[0]
    counts = [left.shape[1] // MEMBERS for left, _ in pairs]
    rows = sum(counts) + (8 if gains is not None else 0)
    operands = [operand for pair in pairs for operand in pair]
    if gains is not None:
        operands.append(gains)
    shape = jax.ShapeDtypeStruct((MEMBERS // 2, rows, columns), BF16)
    vmem = pl.BlockSpec(memory_space=pltpu.VMEM)
    return pl.pallas_call(
        lambda *refs: gradient_kernel(tile, len(pairs), int(gains is not None), *refs),
        out_shape=(shape, shape),
        in_specs=[pl.BlockSpec(memory_space=pltpu.SMEM)] + [vmem] * len(operands),
        out_specs=(vmem, vmem),
        scratch_shapes=[pltpu.VMEM((MEMBERS * count, tile), F32) for count in counts],
        compiler_params=pltpu.CompilerParams(vmem_limit_bytes=48 * 1024 * 1024),
        cost_estimate=pl.CostEstimate(
            flops=2 * tokens_here * columns * MEMBERS * sum(counts),
            bytes_accessed=4 * MEMBERS * rows * columns,
            transcendentals=0,
        ),
        name=name,
    )(info, *operands)


def key_range(info, stream):
    first = info[0]
    bound = info[4 + stream]
    low = jnp.where(first >= bound, bound, 0)
    high = jnp.where(first + SEG - 1 >= bound, bound, 0)
    return first, bound, low, high


def load_blocks(info, blocks, kv, sem):
    z, x, c = info[1], info[2], info[3]
    copies = []
    for place in range(BLOCKS):
        cr, xr, k = place // (2 * REACH), place // REACH % 2, place % REACH
        owner = ((z - k) & 3) * 4 + (x ^ xr) * 2 + (c ^ cr)
        copies.append(pltpu.make_async_copy(blocks[place], kv.at[owner], sem.at[place]))
    for copy in copies:
        copy.start()
    return copies


def forward_kernel(stream, info, q_ref, *refs):
    blocks = refs[:BLOCKS]
    o_ref, lse_ref, kv, acc, total, sem = refs[BLOCKS:]
    copies = load_blocks(info, blocks, kv, sem)
    first, bound, low, high = key_range(info, stream)
    begin = low // KEYS
    diagonal = first // KEYS
    clear = jnp.clip((high + KEYS - 1) // KEYS, begin, diagonal)
    acc[...] = jnp.zeros_like(acc)
    total[...] = jnp.zeros_like(total)
    for copy in copies:
        copy.wait()

    def visit(j, masked):
        keys = kv[pl.ds(2 * j, 2), :, 0:HD].reshape(KEYS, HD)
        values = kv[pl.ds(2 * j, 2), :, HD : 2 * HD].reshape(KEYS, HD)
        if masked:
            row = first + lax.broadcasted_iota(jnp.int32, (SEG, KEYS), 0)
            col = j * KEYS + lax.broadcasted_iota(jnp.int32, (SEG, KEYS), 1)
            mask = (col <= row) & (col >= jnp.where(row >= bound, bound, 0))
        for head in range(HQ):
            rows = slice(head * SEG, (head + 1) * SEG)
            query = q_ref[:, head * HD : (head + 1) * HD]
            score = lax.dot_general(query, keys, NT, preferred_element_type=F32)
            prob = jnp.exp2(score * (SCALE_SCORE * LOG2E))
            if masked:
                prob = jnp.where(mask, prob, 0.0)
            total[rows] += (
                prob[:, 0:128] + prob[:, 128:256] + prob[:, 256:384] + prob[:, 384:512]
            )
            acc[rows] += jnp.dot(prob.astype(BF16), values, preferred_element_type=F32)

    def masked_step(i, carry):
        visit(jnp.where(i < clear, i, diagonal), True)
        return carry

    def clear_step(j, carry):
        visit(j, False)
        return carry

    lax.fori_loop(begin, clear + 1, masked_step, 0)
    lax.fori_loop(clear, diagonal, clear_step, 0)
    for head in range(HQ):
        rows = slice(head * SEG, (head + 1) * SEG)
        part = total[rows]
        out = acc[rows] / jnp.sum(part, axis=1, keepdims=True)
        o_ref[:, head * HD : (head + 1) * HD] = out.astype(BF16)
        lse_ref[:, rows] = jnp.log2(jnp.sum(part.T, axis=0, keepdims=True))


def attention_forward(stream, info, query, blocks):
    vmem = pl.BlockSpec(memory_space=pltpu.VMEM)
    return pl.pallas_call(
        lambda *refs: forward_kernel(stream, *refs),
        out_shape=(
            jax.ShapeDtypeStruct((SEG, HQ * HD), BF16),
            jax.ShapeDtypeStruct((1, HQ * SEG), F32),
        ),
        in_specs=[pl.BlockSpec(memory_space=pltpu.SMEM), vmem]
        + [pl.BlockSpec(memory_space=pl.ANY)] * BLOCKS,
        out_specs=(vmem, vmem),
        scratch_shapes=[
            pltpu.VMEM((MEMBERS, SEG, 2 * HD), BF16),
            pltpu.VMEM((HQ * SEG, HD), F32),
            pltpu.VMEM((HQ * SEG, 128), F32),
            pltpu.SemaphoreType.DMA((BLOCKS,)),
        ],
        compiler_params=pltpu.CompilerParams(vmem_limit_bytes=40 * 1024 * 1024),
        cost_estimate=pl.CostEstimate(
            flops=3_500_000_000, bytes_accessed=5_000_000, transcendentals=3_500_000
        ),
        name=f"attention_forward_{stream}",
    )(info, query, *blocks)


def backward_kernel(stream, info, q_ref, o_ref, do_ref, lse_ref, *refs):
    blocks = refs[:BLOCKS]
    dq_ref = refs[BLOCKS]
    far = refs[BLOCKS + 1 : BLOCKS + 1 + REACH]
    near_far = refs[BLOCKS + 1 + REACH : BLOCKS + 1 + 2 * REACH]
    near = refs[BLOCKS + 1 + 2 * REACH : BLOCKS + 1 + 3 * REACH]
    kv, dkv, qs, qt, dos, dot_, dqt, delta, sem, out_sem = refs[BLOCKS + 1 + 3 * REACH :]
    copies = load_blocks(info, blocks, kv, sem)
    z, x, c = info[1], info[2], info[3]

    def clean(place, carry):
        dkv[place] = jnp.zeros((SEG, 2 * HD), BF16)
        return carry

    lax.fori_loop(0, BLOCKS, clean, 0)
    first, bound, low, _ = key_range(info, stream)
    for head in range(HQ):
        rows = slice(head * SEG, (head + 1) * SEG)
        query = q_ref[:, head * HD : (head + 1) * HD]
        grad = do_ref[:, head * HD : (head + 1) * HD]
        qs[rows] = query
        dos[rows] = grad
        qt[:, rows] = query.T
        dot_[:, rows] = grad.T
        both = grad.astype(F32) * o_ref[:, head * HD : (head + 1) * HD].astype(F32)
        delta[:, rows] = jnp.sum((both[:, 0:128] + both[:, 128:256]).T, axis=0, keepdims=True)
    dqt[...] = jnp.zeros_like(dqt)
    for copy in copies:
        copy.wait()

    def visit(j, carry):
        keys = kv[j, :, 0:HD]
        values = kv[j, :, HD : 2 * HD]
        score = jnp.dot(keys, qt[...], preferred_element_type=F32)
        prob = jnp.exp2(score * (SCALE_SCORE * LOG2E) - lse_ref[...])
        row = first + (lax.broadcasted_iota(jnp.int32, (1, HQ * SEG), 1) & (SEG - 1))
        start = jnp.where(row >= bound, bound, 0)
        col = j * SEG + lax.broadcasted_iota(jnp.int32, (SEG, HQ * SEG), 0)
        prob = jnp.where((col <= row) & (col >= start), prob, 0.0)
        dprob = jnp.dot(values, dot_[...], preferred_element_type=F32)
        dscore = (prob * (dprob - delta[...])).astype(BF16)
        dv = jnp.dot(prob.astype(BF16), dos[...], preferred_element_type=F32)
        dk = jnp.dot(dscore, qs[...], preferred_element_type=F32)
        dqt[...] += jnp.dot(keys.T, dscore, preferred_element_type=F32)
        place = ((j & 1) ^ c) * (2 * REACH) + (z - (j >> 2)) * 2 + (((j >> 1) & 1) ^ x)
        dkv[place, :, 0:HD] = (dk * SCALE_SCORE).astype(BF16)
        dkv[place, :, HD : 2 * HD] = dv.astype(BF16)
        return carry

    lax.fori_loop(low // SEG, first // SEG + 1, visit, 0)
    outs = []
    for k in range(REACH):
        outs.append((dkv.at[pl.ds(2 * REACH + 2 * k, 2)], far[k]))
        outs.append((dkv.at[2 * k + 1], near_far[k]))
        outs.append((dkv.at[2 * k], near[k]))
    copies = [
        pltpu.make_async_copy(source, target, out_sem.at[n])
        for n, (source, target) in enumerate(outs)
    ]
    for copy in copies:
        copy.start()
    for head in range(HQ):
        rows = slice(head * SEG, (head + 1) * SEG)
        dq_ref[:, head * HD : (head + 1) * HD] = dqt[:, rows].T * SCALE_SCORE
    for copy in copies:
        copy.wait()


def attention_backward(stream, info, query, out, grad_out, lse, blocks):
    one = jax.ShapeDtypeStruct((SEG, 2 * HD), BF16)
    two = jax.ShapeDtypeStruct((2, SEG, 2 * HD), BF16)
    vmem = pl.BlockSpec(memory_space=pltpu.VMEM)
    anywhere = pl.BlockSpec(memory_space=pl.ANY)
    result = pl.pallas_call(
        lambda *refs: backward_kernel(stream, *refs),
        out_shape=[jax.ShapeDtypeStruct((SEG, HQ * HD), F32)]
        + [two] * REACH
        + [one] * (2 * REACH),
        in_specs=[pl.BlockSpec(memory_space=pltpu.SMEM)] + [vmem] * 4 + [anywhere] * BLOCKS,
        out_specs=[vmem] + [anywhere] * (3 * REACH),
        scratch_shapes=[
            pltpu.VMEM((MEMBERS, SEG, 2 * HD), BF16),
            pltpu.VMEM((BLOCKS, SEG, 2 * HD), BF16),
            pltpu.VMEM((HQ * SEG, HD), BF16),
            pltpu.VMEM((HD, HQ * SEG), BF16),
            pltpu.VMEM((HQ * SEG, HD), BF16),
            pltpu.VMEM((HD, HQ * SEG), BF16),
            pltpu.VMEM((HD, HQ * SEG), F32),
            pltpu.VMEM((1, HQ * SEG), F32),
            pltpu.SemaphoreType.DMA((BLOCKS,)),
            pltpu.SemaphoreType.DMA((3 * REACH,)),
        ],
        compiler_params=pltpu.CompilerParams(vmem_limit_bytes=40 * 1024 * 1024),
        cost_estimate=pl.CostEstimate(
            flops=8_700_000_000, bytes_accessed=10_000_000, transcendentals=3_500_000
        ),
        name=f"attention_backward_{stream}",
    )(info, query, out, grad_out, lse, *blocks)
    return result[0], result[1 : 1 + REACH], result[1 + REACH : 1 + 2 * REACH], result[1 + 2 * REACH :]


def per_device(
    tokens,
    cotangent,
    lengths,
    w_qkv,
    w_out,
    w_gu,
    w_down,
    norm_gains,
    first_qkv,
    first_out,
    first_gu,
    first_down,
    first_gains,
    second_qkv,
    second_out,
    second_gu,
    second_down,
    second_gains,
):
    streams = tokens.shape[0]
    row_count = streams * SEG
    member_index = lax.axis_index("group")
    tok_rows = tokens.reshape(row_count, D).astype(F32)
    grad_out = cotangent.reshape(row_count, D).astype(F32)
    start_row = member_index * SEG
    boundary = lengths[:, 0]
    info = jnp.concatenate(
        [
            jnp.stack([start_row, member_index // 4, member_index // 2 % 2, member_index % 2]),
            boundary,
        ]
    ).astype(jnp.int32)
    q_width = HQ * HD
    low_qkv = w_qkv.astype(BF16)
    gain_count = norm_gains.shape[0]
    gain_row = jnp.pad(norm_gains.astype(BF16), (0, 2 * HD - gain_count))
    full_kv, gain_rows = order_rows(
        info,
        gather_all(jnp.concatenate([low_qkv[:, q_width:], gain_row[None]], axis=0)),
        "order_kv",
    )
    full_gains = gain_rows[:, :gain_count].reshape(-1)
    gain_in, gain_pa, gain_pf, gain_po, gain_query, gain_key = split_gains(full_gains)
    out_rows = w_out.shape[0]
    mixed = lax.all_gather(
        jnp.concatenate([w_out.astype(BF16), w_down.astype(BF16)], axis=0),
        "group",
        axis=0,
        tiled=False,
    )
    full_out = mixed[:, :out_rows].reshape(HQ * HD, D)
    full_down = mixed[:, out_rows:].reshape(FF, D)
    low_gu, low_q, gain_in = lax.optimization_barrier(
        (w_gu.astype(BF16), low_qkv[:, :q_width], gain_in)
    )
    full_gu = lax.all_gather(low_gu, "group", axis=0, tiled=True)
    index_mine = start_row + jnp.arange(SEG, dtype=jnp.int32)
    position_mine = index_mine[None, :] - jnp.where(
        index_mine[None, :] >= boundary[:, None], boundary[:, None], 0
    )
    cosine, sine = angles(position_mine.reshape(row_count), HD)
    normed_in, pull_in = jax.vjp(rms_norm, tok_rows, gain_in)
    input_low = normed_in.astype(BF16)
    kv_rows = jnp.dot(input_low, full_kv, preferred_element_type=F32)
    key_rot, pull_key = jax.vjp(
        lambda rows, gain: head_in(rows, gain, cosine, sine), kv_rows[:, :HD], gain_key
    )
    kv_low = jnp.concatenate([key_rot.astype(BF16), kv_rows[:, HD:].astype(BF16)], axis=1)
    blocks = [gather_keys(kv_low[s * SEG : (s + 1) * SEG]) for s in range(streams)]
    (full_q,) = order_rows(info, gather_all(low_q), "order_q")
    query_rows = jnp.dot(input_low, full_q, preferred_element_type=F32)
    query_rot, pull_query = [], []
    for head in range(HQ):
        rotated, pull = jax.vjp(
            lambda rows, gain: head_in(rows, gain, cosine, sine),
            query_rows[:, head * HD : (head + 1) * HD],
            gain_query,
        )
        query_rot.append(rotated.astype(BF16))
        pull_query.append(pull)
    query_low = jnp.concatenate(query_rot, axis=1)
    attended = [
        attention_forward(s, info, query_low[s * SEG : (s + 1) * SEG], blocks[s])
        for s in range(streams)
    ]
    attn_low = jnp.concatenate([out for out, _ in attended], axis=0)
    attn_proj = jnp.dot(attn_low, full_out, preferred_element_type=F32)
    post_attn, pull_attn = jax.vjp(rms_norm, attn_proj, gain_pa)
    middle = tok_rows + post_attn
    normed_ff, pull_ff = jax.vjp(rms_norm, middle, gain_pf)
    ff_low = normed_ff.astype(BF16)
    gate_up = jnp.dot(ff_low, full_gu, preferred_element_type=F32)
    hidden, pull_geglu = jax.vjp(geglu, gate_up)
    hidden_low = hidden.astype(BF16)
    down_proj = jnp.dot(hidden_low, full_down, preferred_element_type=F32)
    post_ff, pull_post = jax.vjp(rms_norm, down_proj, gain_po)
    layer_out = (middle + post_ff).astype(BF16).reshape(streams, SEG, D)
    grad_down, grad_gain_po = pull_post(grad_out)
    down_low = grad_down.astype(BF16)
    grad_hidden = jnp.dot(down_low, full_down.T, preferred_element_type=F32)
    (grad_gate_up,) = pull_geglu(grad_hidden)
    gate_up_low = grad_gate_up.astype(BF16)
    near_gu, far_gu = weight_gradient(info, [(ff_low, gate_up_low)], None, 512, "gradient_gu")
    came_gu = swap_core(far_gu)
    grad_normed_ff = jnp.dot(gate_up_low, full_gu.T, preferred_element_type=F32)
    grad_middle_ff, grad_gain_pf = pull_ff(grad_normed_ff)
    grad_middle = grad_out + grad_middle_ff
    grad_attn_proj, grad_gain_pa = pull_attn(grad_middle)
    proj_low = grad_attn_proj.astype(BF16)
    grad_attn_low = jnp.dot(proj_low, full_out.T, preferred_element_type=F32).astype(BF16)
    near_mixed, far_mixed = weight_gradient(
        info, [(attn_low, proj_low), (hidden_low, down_low)], None, 640, "gradient_mixed"
    )
    came_mixed = swap_core(far_mixed)
    over_gu = scatter_x(near_gu, came_gu)
    grad_attn = [grad_attn_low[s * SEG : (s + 1) * SEG] for s in range(streams)]
    grad_attn[0], came_gu, near_mixed = lax.optimization_barrier(
        (grad_attn[0], came_gu, near_mixed)
    )

    def back(s):
        return attention_backward(
            s, info, query_low[s * SEG : (s + 1) * SEG], attended[s][0], grad_attn[s], attended[s][1], blocks[s]
        )

    first_back = back(0)
    grad_attn[1], over_gu, came_mixed, first_back = lax.optimization_barrier(
        (grad_attn[1], over_gu, came_mixed, first_back)
    )
    over_mixed = scatter_x(near_mixed, came_mixed)
    second_back = back(1)
    grad_kv = jnp.concatenate(
        [scatter_keys(*first_back[1:]), scatter_keys(*second_back[1:])], axis=0
    )
    sum_gu = over_replicas(scatter_z(near_gu, came_gu, over_gu))
    grad_query = jnp.concatenate([first_back[0], second_back[0]], axis=0)
    grad_query_rows, grad_gain_q = [], 0.0
    for head in range(HQ):
        rows, gain = pull_query[head](grad_query[:, head * HD : (head + 1) * HD])
        grad_query_rows.append(rows.astype(BF16))
        grad_gain_q = grad_gain_q + gain
    query_grad_low = jnp.concatenate(grad_query_rows, axis=1)
    near_q, far_q = weight_gradient(
        info, [(input_low, query_grad_low)], None, 512, "gradient_q"
    )
    came_q = swap_core(far_q)
    over_q = scatter_x(near_q, came_q)
    grad_kv, over_mixed, over_q = lax.optimization_barrier((grad_kv, over_mixed, over_q))
    sum_mixed = over_replicas(scatter_z(near_mixed, came_mixed, over_mixed))
    sum_q = over_replicas(scatter_z(near_q, came_q, over_q))
    grad_key_rows, grad_gain_k = pull_key(grad_kv[:, :HD])
    kv_grad_low = jnp.concatenate(
        [grad_key_rows.astype(BF16), grad_kv[:, HD:].astype(BF16)], axis=1
    )
    grad_normed_in = jnp.dot(query_grad_low, full_q.T, preferred_element_type=F32) + jnp.dot(
        kv_grad_low, full_kv.T, preferred_element_type=F32
    )
    grad_tokens_in, grad_gain_in = pull_in(grad_normed_in)
    token_grad = (grad_middle + grad_tokens_in).reshape(streams, SEG, D)
    wgrad_gains = jnp.concatenate(
        [grad_gain_in, grad_gain_pa, grad_gain_pf, grad_gain_po, grad_gain_q, grad_gain_k]
    )
    gains_out = jnp.pad(
        wgrad_gains.reshape(MEMBERS, gain_count), ((0, 0), (0, 2 * HD - gain_count))
    )
    near_kv, far_kv = weight_gradient(
        info, [(input_low, kv_grad_low)], gains_out, 2 * HD, "gradient_kv"
    )
    came_kv = swap_core(far_kv)
    sum_kv = over_replicas(scatter_z(near_kv, came_kv, scatter_x(near_kv, came_kv)))
    shard_qkv = jnp.concatenate([sum_q, sum_kv[:-8]], axis=1)
    shard_gains = sum_kv[-1, :gain_count]
    shard_out, shard_down = sum_mixed[:out_rows], sum_mixed[out_rows:]
    upd_qkv = adam_step(w_qkv, first_qkv, second_qkv, shard_qkv, RATE_MATRIX, DECAY_RATE)
    upd_out = adam_step(w_out, first_out, second_out, shard_out, RATE_MATRIX, DECAY_RATE)
    upd_gu = adam_step(w_gu, first_gu, second_gu, sum_gu, RATE_MATRIX, DECAY_RATE)
    upd_down = adam_step(w_down, first_down, second_down, shard_down, RATE_MATRIX, DECAY_RATE)
    upd_gains = adam_step(norm_gains, first_gains, second_gains, shard_gains, RATE_GAIN, 0.0)
    return (layer_out, token_grad, *upd_qkv, *upd_out, *upd_gu, *upd_down, *upd_gains)


def solution(mesh):
    in_specs = (
        P("replica", "group", None),
        P("replica", "group", None),
        P("replica", None),
        P("group", None),
        P("group", None),
        P("group", None),
        P("group", None),
        P("group"),
        P("group", None),
        P("group", None),
        P("group", None),
        P("group", None),
        P("group"),
        P("group", None),
        P("group", None),
        P("group", None),
        P("group", None),
        P("group"),
    )
    out_specs = (
        P("replica", "group", None),
        P("replica", "group", None),
        P("group", None),
        P("group", None),
        P("group", None),
        P("group", None),
        P("group", None),
        P("group", None),
        P("group", None),
        P("group", None),
        P("group", None),
        P("group", None),
        P("group", None),
        P("group", None),
        P("group"),
        P("group"),
        P("group"),
    )
    return jax.shard_map(
        per_device, mesh=mesh, in_specs=in_specs, out_specs=out_specs, check_vma=False
    )
```

```python
import math

import jax
import jax.numpy as jnp
from jax import lax
from jax.experimental import pallas as pl
from jax.experimental.pallas import tpu as pltpu
from jax.sharding import PartitionSpec as P

D = 640
HQ = 4
HD = 256
FF = 2048
SEG = 256
STEP = 10


EPS_NORM = 1e-06
BETA_ONE = 0.9
BETA_TWO = 0.999
ADAM_EPS = 1e-08
RATE_MATRIX = 0.1
RATE_GAIN = 0.5
DECAY_RATE = 0.1
ROPE_BASE = 1000000.0
NEGATIVE = -1e30
SCALE_SCORE = 0.0625


def rms_norm(values, gain_row):
    factor = lax.rsqrt(jnp.mean(values * values, axis=-1, keepdims=True) + EPS_NORM)
    return values * factor * gain_row


def angles(position, width):
    half_width = width // 2
    frequency = jnp.exp(
        jnp.arange(half_width, dtype=jnp.float32) * (-2.0 * math.log(ROPE_BASE) / width)
    )
    angle_table = position.astype(jnp.float32)[:, None] * frequency[None, :]
    return (jnp.cos(angle_table), jnp.sin(angle_table))


def rotate(values, cosine, sine):
    half_width = values.shape[-1] // 2
    leading = values[..., :half_width]
    trailing = values[..., half_width:]
    return jnp.concatenate(
        [leading * cosine - trailing * sine, trailing * cosine + leading * sine], axis=-1
    )


def layout(lengths, total):
    seq_ends = jnp.cumsum(lengths)
    seq_starts = seq_ends - lengths
    stream_index = jnp.arange(total, dtype=jnp.int32)
    segment = jnp.sum((stream_index[:, None] >= seq_ends[None, :]).astype(jnp.int32), axis=1)
    seq_begin = jnp.max(
        jnp.where(stream_index[:, None] >= seq_starts[None, :], seq_starts[None, :], 0), axis=1
    )
    return (segment, stream_index - seq_begin)


def head_in(values, gain_row, cosine, sine):
    return rotate(rms_norm(values, gain_row), cosine, sine)


def geglu(gate_up):
    return jax.nn.gelu(gate_up[:, :FF], approximate=True) * gate_up[:, FF:]


def split_gains(gain_all):
    return (
        gain_all[0:D],
        gain_all[D : 2 * D],
        gain_all[2 * D : 3 * D],
        gain_all[3 * D : 4 * D],
        gain_all[4 * D : 4 * D + HD],
        gain_all[4 * D + HD : 4 * D + 2 * HD],
    )


def adam_step(master, moment_one, moment_two, gradient, rate, decay):
    moment_new = BETA_ONE * moment_one + (1.0 - BETA_ONE) * gradient
    square_new = BETA_TWO * moment_two + (1.0 - BETA_TWO) * gradient * gradient
    moment_hat = moment_new / (1.0 - BETA_ONE**STEP)
    square_hat = square_new / (1.0 - BETA_TWO**STEP)
    master_new = master * (1.0 - rate * decay) - rate * moment_hat / (
        jnp.sqrt(square_hat) + ADAM_EPS
    )
    return (moment_new, square_new, master_new)


LOG2E = 1.4426950408889634
KEYS = 512
MEMBERS = 16
REACH = 3
BLOCKS = 4 * REACH
NT = (((1,), (1,)), ((), ()))
TN = (((0,), (0,)), ((), ()))
F32 = jnp.float32
BF16 = jnp.bfloat16


def shift_z(values, k):
    return lax.ppermute(values, "group", [(i, (i + 4 * k) % MEMBERS) for i in range(MEMBERS)])


def line_up(values, lowest):
    return lax.ppermute(values, "group", [(i, i + 4) for i in range(4 * lowest, MEMBERS - 4)])


def line_down(values, lowest):
    return lax.ppermute(values, "group", [(i, i - 4) for i in range(4 * lowest, MEMBERS)])


def swap_x(values):
    return lax.ppermute(values, "group", [(i, i ^ 2) for i in range(MEMBERS)])


def swap_core(values):
    return lax.ppermute(values, "group", [(i, i ^ 1) for i in range(MEMBERS)])


def spread(lines):
    near = lines + [swap_x(line) for line in lines]
    return near + [swap_core(block) for block in near]


def gather_all(own):
    return spread([own] + [shift_z(own, k) for k in (1, 2, 3)])


def gather_keys(own, later):
    first = line_up(own, 0)
    first, later = lax.optimization_barrier((first, later))
    return spread([own, first, line_up(first, 1)]), later


def scatter_keys(far, near_far, near):
    running = None
    for k in range(REACH - 1, -1, -1):
        came = swap_core(far[k]).astype(F32)
        over = swap_x((near_far[k].astype(F32) + came[1]).astype(BF16))
        total = near[k].astype(F32) + came[0] + over.astype(F32)
        if running is not None:
            total = total + running.astype(F32)
        if k:
            running = line_down(total.astype(BF16), k)
    return total


def gather_halves(shard):
    if lax.axis_size("replica") != 2:
        full = lax.all_gather(shard, "group", axis=0, tiled=False)
        return jnp.split(full, 2, axis=2)
    half = shard.shape[1] // 2
    mine = lax.dynamic_slice_in_dim(shard, lax.axis_index("replica") * half, half, 1)
    full = lax.all_gather(mine, ("replica", "group"), axis=0, tiled=False)
    return [full[:MEMBERS], full[MEMBERS:]]


def scatter_halves(halves):
    if lax.axis_size("replica") != 2:
        return lax.psum_scatter(halves, "group", scatter_dimension=1, tiled=True)
    flat = halves.reshape(-1, halves.shape[2])
    return lax.psum_scatter(flat, ("replica", "group"), scatter_dimension=0, tiled=True)


def join_halves(mine):
    if lax.axis_size("replica") != 2:
        own = lax.psum(mine, "replica").astype(F32)
        return jnp.concatenate([own[0], own[1]], axis=1)
    other = lax.ppermute(mine, "replica", [(0, 1), (1, 0)])
    first = lax.axis_index("replica") == 0
    return jnp.concatenate(
        [jnp.where(first, mine, other), jnp.where(first, other, mine)], axis=1
    ).astype(F32)


def scatter_x(near, came):
    return swap_x((near[4:].astype(F32) + came[4:].astype(F32)).astype(BF16))


def scatter_z(near, came, over):
    total = [near[k].astype(F32) + came[k].astype(F32) + over[k].astype(F32) for k in range(4)]
    for k in (1, 2, 3):
        total[0] = total[0] + shift_z(total[k].astype(BF16), k).astype(F32)
    return total[0].astype(BF16)


def over_replicas(shard):
    if lax.axis_size("replica") == 2:
        other = lax.ppermute(shard, "replica", [(0, 1), (1, 0)])
        return shard.astype(F32) + other.astype(F32)
    return lax.psum(shard, "replica").astype(F32)


def owner_up(info, place):
    cr, xr, k = place // 8, place // 4 % 2, place % 4
    return ((info[1] + k) & 3) * 4 + (info[2] ^ xr) * 2 + (info[3] ^ cr)


def order_kernel(info, *refs):
    blocks = refs[:MEMBERS]
    full_ref, rows = refs[MEMBERS], refs[-1]
    count = rows.shape[0] // MEMBERS
    for place in range(MEMBERS):
        cr, xr, k = place // 8, place // 4 % 2, place % 4
        owner = ((info[1] - k) & 3) * 4 + (info[2] ^ xr) * 2 + (info[3] ^ cr)
        values = blocks[place][...].astype(F32)
        rows[pl.ds(pl.multiple_of(owner * count, 8), count)] = values[:count]
        if len(refs) > MEMBERS + 2:
            refs[MEMBERS + 1][pl.ds(owner, 1)] = values[count : count + 1]
    full_ref[...] = rows[...].astype(BF16)


def order_rows(info, blocks, name):
    rows, columns = blocks[0].shape
    count = rows // 8 * 8
    vmem = pl.BlockSpec(memory_space=pltpu.VMEM)
    shapes = [jax.ShapeDtypeStruct((MEMBERS * count, columns), BF16)]
    if rows > count:
        shapes.append(jax.ShapeDtypeStruct((MEMBERS, columns), F32))
    return pl.pallas_call(
        order_kernel,
        out_shape=shapes,
        in_specs=[pl.BlockSpec(memory_space=pltpu.SMEM)] + [vmem] * MEMBERS,
        out_specs=[vmem] * len(shapes),
        scratch_shapes=[pltpu.VMEM((MEMBERS * count, columns), F32)],
        compiler_params=pltpu.CompilerParams(vmem_limit_bytes=32 * 1024 * 1024),
        cost_estimate=pl.CostEstimate(flops=0, bytes_accessed=4_000_000, transcendentals=0),
        name=name,
    )(info, *blocks)


def gradient_kernel(tile, pairs, extra, info, *refs):
    operands = refs[: 2 * pairs + extra]
    near, far = refs[2 * pairs + extra : 2 * pairs + extra + 2]
    sums = refs[2 * pairs + extra + 2 :]
    columns = near.shape[2]
    for begin in range(0, columns, tile):
        at = slice(begin, begin + tile)
        for pair in range(pairs):
            left, right = operands[2 * pair], operands[2 * pair + 1]
            sums[pair][...] = lax.dot_general(
                left[...], right[:, at], TN, preferred_element_type=F32
            )
        for place in range(MEMBERS):
            owner = owner_up(info, place)
            parts = []
            for pair in range(pairs):
                count = sums[pair].shape[0] // MEMBERS
                parts.append(sums[pair][pl.ds(pl.multiple_of(owner * count, 8), count)])
            if extra:
                row = operands[2 * pairs][pl.ds(owner, 1), at]
                parts.append(jnp.broadcast_to(row, (8, tile)))
            block = jnp.concatenate(parts, axis=0) if len(parts) > 1 else parts[0]
            target = far if place >= 8 else near
            target[place % 8, :, at] = block.astype(BF16)


def weight_gradient(info, pairs, gains, tile, name):
    columns = pairs[0][1].shape[1]
    tokens_here = pairs[0][0].shape[0]
    counts = [left.shape[1] // MEMBERS for left, _ in pairs]
    rows = sum(counts) + (8 if gains is not None else 0)
    operands = [operand for pair in pairs for operand in pair]
    if gains is not None:
        operands.append(gains)
    shape = jax.ShapeDtypeStruct((MEMBERS // 2, rows, columns), BF16)
    vmem = pl.BlockSpec(memory_space=pltpu.VMEM)
    return pl.pallas_call(
        lambda *refs: gradient_kernel(tile, len(pairs), int(gains is not None), *refs),
        out_shape=(shape, shape),
        in_specs=[pl.BlockSpec(memory_space=pltpu.SMEM)] + [vmem] * len(operands),
        out_specs=(vmem, vmem),
        scratch_shapes=[pltpu.VMEM((MEMBERS * count, tile), F32) for count in counts],
        compiler_params=pltpu.CompilerParams(vmem_limit_bytes=48 * 1024 * 1024),
        cost_estimate=pl.CostEstimate(
            flops=2 * tokens_here * columns * MEMBERS * sum(counts),
            bytes_accessed=4 * MEMBERS * rows * columns,
            transcendentals=0,
        ),
        name=name,
    )(info, *operands)


def halves_kernel(left, right, out):
    half, tile = out.shape[2], 512
    for part in range(2):
        for begin in range(0, half, tile):
            out[part, :, begin : begin + tile] = lax.dot_general(
                left[...],
                right[:, part * half + begin : part * half + begin + tile],
                TN,
                preferred_element_type=F32,
            ).astype(BF16)


def halves_gradient(left, right):
    vmem = pl.BlockSpec(memory_space=pltpu.VMEM)
    rows, columns = left.shape[1], right.shape[1]
    return pl.pallas_call(
        halves_kernel,
        out_shape=jax.ShapeDtypeStruct((2, rows, columns // 2), BF16),
        in_specs=[vmem, vmem],
        out_specs=vmem,
        compiler_params=pltpu.CompilerParams(vmem_limit_bytes=40 * 1024 * 1024),
        cost_estimate=pl.CostEstimate(
            flops=2 * left.shape[0] * rows * columns,
            bytes_accessed=4 * rows * columns,
            transcendentals=0,
        ),
        name="gradient_gu",
    )(left, right)


def key_range(info, stream):
    first = info[0]
    bound = info[4 + stream]
    low = jnp.where(first >= bound, bound, 0)
    high = jnp.where(first + SEG - 1 >= bound, bound, 0)
    return first, bound, low, high


def load_blocks(info, blocks, kv, sem):
    z, x, c = info[1], info[2], info[3]
    copies = []
    for place in range(len(blocks)):
        cr, xr, k = place // (2 * REACH), place // REACH % 2, place % REACH
        owner = ((z - k) & 3) * 4 + (x ^ xr) * 2 + (c ^ cr)
        copies.append(pltpu.make_async_copy(blocks[place], kv.at[owner], sem.at[place]))
    for copy in copies:
        copy.start()
    return copies


def forward_kernel(info, q_ref, *refs):
    blocks = refs[:BLOCKS]
    o_ref, lse_ref, kv, acc, total, sem = refs[BLOCKS:]
    copies = load_blocks(info, blocks, kv, sem)
    for copy in copies:
        copy.wait()

    def one_stream(stream, carry):
        mine = pl.ds(pl.multiple_of(stream * SEG, SEG), SEG)
        first, bound, low, high = key_range(info, stream)
        begin = low // KEYS
        diagonal = first // KEYS
        clear = jnp.clip((high + KEYS - 1) // KEYS, begin, diagonal)
        acc[...] = jnp.zeros_like(acc)
        total[...] = jnp.zeros_like(total)

        def visit(j, masked):
            keys = kv[pl.ds(2 * j, 2), stream, :, 0:HD].reshape(KEYS, HD)
            values = kv[pl.ds(2 * j, 2), stream, :, HD : 2 * HD].reshape(KEYS, HD)
            if masked:
                row = first + lax.broadcasted_iota(jnp.int32, (SEG, KEYS), 0)
                col = j * KEYS + lax.broadcasted_iota(jnp.int32, (SEG, KEYS), 1)
                mask = (col <= row) & (col >= jnp.where(row >= bound, bound, 0))
            for head in range(HQ):
                rows = slice(head * SEG, (head + 1) * SEG)
                query = q_ref[mine, head * HD : (head + 1) * HD]
                score = lax.dot_general(query, keys, NT, preferred_element_type=F32)
                prob = jnp.exp2(score * (SCALE_SCORE * LOG2E))
                if masked:
                    prob = jnp.where(mask, prob, 0.0)
                total[rows] += (
                    prob[:, 0:128] + prob[:, 128:256] + prob[:, 256:384] + prob[:, 384:512]
                )
                acc[rows] += jnp.dot(prob.astype(BF16), values, preferred_element_type=F32)

        def masked_step(i, carry):
            visit(jnp.where(i < clear, i, diagonal), True)
            return carry

        def clear_step(j, carry):
            visit(j, False)
            return carry

        lax.fori_loop(begin, clear + 1, masked_step, 0)
        lax.fori_loop(clear, diagonal, clear_step, 0)
        for head in range(HQ):
            rows = slice(head * SEG, (head + 1) * SEG)
            part = total[rows]
            out = acc[rows] / jnp.sum(part, axis=1, keepdims=True)
            o_ref[mine, head * HD : (head + 1) * HD] = out.astype(BF16)
            lse_ref[stream, :, rows] = jnp.log2(jnp.sum(part.T, axis=0, keepdims=True))
        return carry

    lax.fori_loop(0, 2, one_stream, 0)


def attention_forward(info, query, blocks):
    vmem = pl.BlockSpec(memory_space=pltpu.VMEM)
    return pl.pallas_call(
        forward_kernel,
        out_shape=(
            jax.ShapeDtypeStruct((2 * SEG, HQ * HD), BF16),
            jax.ShapeDtypeStruct((2, 1, HQ * SEG), F32),
        ),
        in_specs=[pl.BlockSpec(memory_space=pltpu.SMEM), vmem]
        + [pl.BlockSpec(memory_space=pl.ANY)] * BLOCKS,
        out_specs=(vmem, vmem),
        scratch_shapes=[
            pltpu.VMEM((MEMBERS, 2, SEG, 2 * HD), BF16),
            pltpu.VMEM((HQ * SEG, HD), F32),
            pltpu.VMEM((HQ * SEG, 128), F32),
            pltpu.SemaphoreType.DMA((BLOCKS,)),
        ],
        compiler_params=pltpu.CompilerParams(vmem_limit_bytes=40 * 1024 * 1024),
        cost_estimate=pl.CostEstimate(
            flops=7_000_000_000, bytes_accessed=9_000_000, transcendentals=7_000_000
        ),
        name="attention_forward",
    )(info, query, *blocks)


def backward_kernel(info, q_ref, o_ref, do_ref, lse_ref, *refs):
    blocks = refs[:BLOCKS]
    dq_ref = refs[BLOCKS]
    far = refs[BLOCKS + 1 : BLOCKS + 1 + REACH]
    near_far = refs[BLOCKS + 1 + REACH : BLOCKS + 1 + 2 * REACH]
    near = refs[BLOCKS + 1 + 2 * REACH : BLOCKS + 1 + 3 * REACH]
    kv, dkv, qs, qt, dos, dot_, dqt, delta, sem, out_sem = refs[BLOCKS + 1 + 3 * REACH :]
    copies = load_blocks(info, blocks, kv, sem)
    z, x, c = info[1], info[2], info[3]

    def clean(place, carry):
        dkv[place] = jnp.zeros((2, SEG, 2 * HD), BF16)
        return carry

    lax.fori_loop(0, BLOCKS, clean, 0)
    for copy in copies:
        copy.wait()

    def one_stream(stream, carry):
        first, bound, low, _ = key_range(info, stream)
        mine = pl.ds(pl.multiple_of(stream * SEG, SEG), SEG)
        for head in range(HQ):
            rows = slice(head * SEG, (head + 1) * SEG)
            lanes = slice(head * HD, (head + 1) * HD)
            query = q_ref[mine, lanes]
            grad = do_ref[mine, lanes]
            qs[rows] = query
            dos[rows] = grad
            qt[:, rows] = query.T
            dot_[:, rows] = grad.T
            both = grad.astype(F32) * o_ref[mine, lanes].astype(F32)
            delta[:, rows] = jnp.sum((both[:, 0:128] + both[:, 128:256]).T, axis=0, keepdims=True)
        dqt[...] = jnp.zeros_like(dqt)
        shape = (SEG, HQ * SEG)

        def visit(j, carry):
            keys = kv[j, stream, :, 0:HD]
            values = kv[j, stream, :, HD : 2 * HD]
            score = jnp.dot(keys, qt[...], preferred_element_type=F32)
            prob = jnp.exp2(score * (SCALE_SCORE * LOG2E) - lse_ref[stream])
            row = first + (lax.broadcasted_iota(jnp.int32, (1, HQ * SEG), 1) & (SEG - 1))
            start = jnp.where(row >= bound, bound, 0)
            col = j * SEG + lax.broadcasted_iota(jnp.int32, shape, 0)
            prob = jnp.where((col <= row) & (col >= start), prob, 0.0)
            dprob = jnp.dot(values, dot_[...], preferred_element_type=F32)
            dscore = (prob * (dprob - delta[...])).astype(BF16)
            dv = jnp.dot(prob.astype(BF16), dos[...], preferred_element_type=F32)
            dk = jnp.dot(dscore, qs[...], preferred_element_type=F32)
            dqt[...] += jnp.dot(keys.T, dscore, preferred_element_type=F32)
            place = ((j & 1) ^ c) * (2 * REACH) + (z - (j >> 2)) * 2 + (((j >> 1) & 1) ^ x)
            dkv[place, stream, :, 0:HD] = (dk * SCALE_SCORE).astype(BF16)
            dkv[place, stream, :, HD : 2 * HD] = dv.astype(BF16)
            return carry

        lax.fori_loop(low // SEG, first // SEG + 1, visit, 0)
        for head in range(HQ):
            rows = slice(head * SEG, (head + 1) * SEG)
            dq_ref[mine, head * HD : (head + 1) * HD] = dqt[:, rows].T * SCALE_SCORE
        return carry

    lax.fori_loop(0, 2, one_stream, 0)
    outs = []
    for k in range(REACH):
        outs.append((dkv.at[pl.ds(2 * REACH + 2 * k, 2)], far[k]))
        outs.append((dkv.at[2 * k + 1], near_far[k]))
        outs.append((dkv.at[2 * k], near[k]))
    copies = [
        pltpu.make_async_copy(source, target, out_sem.at[n])
        for n, (source, target) in enumerate(outs)
    ]
    for copy in copies:
        copy.start()
    for copy in copies:
        copy.wait()


def attention_backward(info, query, out, grad_out, lse, blocks):
    one = jax.ShapeDtypeStruct((2, SEG, 2 * HD), BF16)
    two = jax.ShapeDtypeStruct((2, 2, SEG, 2 * HD), BF16)
    vmem = pl.BlockSpec(memory_space=pltpu.VMEM)
    anywhere = pl.BlockSpec(memory_space=pl.ANY)
    result = pl.pallas_call(
        backward_kernel,
        out_shape=[jax.ShapeDtypeStruct((2 * SEG, HQ * HD), F32)]
        + [two] * REACH
        + [one] * (2 * REACH),
        in_specs=[pl.BlockSpec(memory_space=pltpu.SMEM)] + [vmem] * 4 + [anywhere] * BLOCKS,
        out_specs=[vmem] + [anywhere] * (3 * REACH),
        scratch_shapes=[
            pltpu.VMEM((MEMBERS, 2, SEG, 2 * HD), BF16),
            pltpu.VMEM((BLOCKS, 2, SEG, 2 * HD), BF16),
            pltpu.VMEM((HQ * SEG, HD), BF16),
            pltpu.VMEM((HD, HQ * SEG), BF16),
            pltpu.VMEM((HQ * SEG, HD), BF16),
            pltpu.VMEM((HD, HQ * SEG), BF16),
            pltpu.VMEM((HD, HQ * SEG), F32),
            pltpu.VMEM((1, HQ * SEG), F32),
            pltpu.SemaphoreType.DMA((BLOCKS,)),
            pltpu.SemaphoreType.DMA((3 * REACH,)),
        ],
        compiler_params=pltpu.CompilerParams(vmem_limit_bytes=52 * 1024 * 1024),
        cost_estimate=pl.CostEstimate(
            flops=17_000_000_000, bytes_accessed=20_000_000, transcendentals=7_000_000
        ),
        name="attention_backward",
    )(info, query, out, grad_out, lse, *blocks)
    return result[0], result[1 : 1 + REACH], result[1 + REACH : 1 + 2 * REACH], result[1 + 2 * REACH :]


def per_device(
    tokens,
    cotangent,
    lengths,
    w_qkv,
    w_out,
    w_gu,
    w_down,
    norm_gains,
    first_qkv,
    first_out,
    first_gu,
    first_down,
    first_gains,
    second_qkv,
    second_out,
    second_gu,
    second_down,
    second_gains,
):
    streams = tokens.shape[0]
    row_count = streams * SEG
    member_index = lax.axis_index("group")
    tok_rows = tokens.reshape(row_count, D).astype(F32)
    grad_out = cotangent.reshape(row_count, D).astype(F32)
    start_row = member_index * SEG
    boundary = lengths[:, 0]
    info = jnp.concatenate(
        [
            jnp.stack([start_row, member_index // 4, member_index // 2 % 2, member_index % 2]),
            boundary,
        ]
    ).astype(jnp.int32)
    q_width = HQ * HD
    low_qkv = w_qkv.astype(BF16)
    gain_count = norm_gains.shape[0]
    gain_row = jnp.pad(norm_gains.astype(BF16), (0, 2 * HD - gain_count))
    full_kv, gain_rows = order_rows(
        info,
        gather_all(jnp.concatenate([low_qkv[:, q_width:], gain_row[None]], axis=0)),
        "order_kv",
    )
    full_gains = gain_rows[:, :gain_count].reshape(-1)
    gain_in, gain_pa, gain_pf, gain_po, gain_query, gain_key = split_gains(full_gains)
    out_rows = w_out.shape[0]
    mixed = jnp.concatenate(
        gather_halves(jnp.concatenate([w_out.astype(BF16), w_down.astype(BF16)], axis=0)), axis=2
    )
    full_out = mixed[:, :out_rows].reshape(HQ * HD, D)
    full_down = mixed[:, out_rows:].reshape(FF, D)
    full_gate, full_up = [half.reshape(D, FF) for half in gather_halves(w_gu.astype(BF16))]
    index_mine = start_row + jnp.arange(SEG, dtype=jnp.int32)
    position_mine = index_mine[None, :] - jnp.where(
        index_mine[None, :] >= boundary[:, None], boundary[:, None], 0
    )
    cosine, sine = angles(position_mine.reshape(row_count), HD)
    normed_in, pull_in = jax.vjp(rms_norm, tok_rows, gain_in)
    input_low = normed_in.astype(BF16)
    kv_rows = jnp.dot(input_low, full_kv, preferred_element_type=F32)
    key_rot, pull_key = jax.vjp(
        lambda rows, gain: head_in(rows, gain, cosine, sine), kv_rows[:, :HD], gain_key
    )
    kv_low = jnp.concatenate([key_rot.astype(BF16), kv_rows[:, HD:].astype(BF16)], axis=1)
    blocks, low_q = gather_keys(kv_low.reshape(streams, SEG, 2 * HD), low_qkv[:, :q_width])
    (full_q,) = order_rows(info, gather_all(low_q), "order_q")
    query_rows = jnp.dot(input_low, full_q, preferred_element_type=F32)
    query_rot, pull_query = [], []
    for head in range(HQ):
        rotated, pull = jax.vjp(
            lambda rows, gain: head_in(rows, gain, cosine, sine),
            query_rows[:, head * HD : (head + 1) * HD],
            gain_query,
        )
        query_rot.append(rotated.astype(BF16))
        pull_query.append(pull)
    query_low = jnp.concatenate(query_rot, axis=1)
    attn_low, lse = attention_forward(info, query_low, blocks)
    attn_proj = jnp.dot(attn_low, full_out, preferred_element_type=F32)
    post_attn, pull_attn = jax.vjp(rms_norm, attn_proj, gain_pa)
    middle = tok_rows + post_attn
    normed_ff, pull_ff = jax.vjp(rms_norm, middle, gain_pf)
    ff_low = normed_ff.astype(BF16)
    gate_up = jnp.concatenate(
        [
            jnp.dot(ff_low, full_gate, preferred_element_type=F32),
            jnp.dot(ff_low, full_up, preferred_element_type=F32),
        ],
        axis=1,
    )
    hidden, pull_geglu = jax.vjp(geglu, gate_up)
    hidden_low = hidden.astype(BF16)
    down_proj = jnp.dot(hidden_low, full_down, preferred_element_type=F32)
    post_ff, pull_post = jax.vjp(rms_norm, down_proj, gain_po)
    layer_out = (middle + post_ff).astype(BF16).reshape(streams, SEG, D)
    grad_down, grad_gain_po = pull_post(grad_out)
    down_low = grad_down.astype(BF16)
    grad_hidden = jnp.dot(down_low, full_down.T, preferred_element_type=F32)
    (grad_gate_up,) = pull_geglu(grad_hidden)
    gate_up_low = grad_gate_up.astype(BF16)
    grad_gu = halves_gradient(ff_low, gate_up_low)
    grad_normed_ff = jnp.dot(
        gate_up_low[:, :FF], full_gate.T, preferred_element_type=F32
    ) + jnp.dot(gate_up_low[:, FF:], full_up.T, preferred_element_type=F32)
    grad_middle_ff, grad_gain_pf = pull_ff(grad_normed_ff)
    grad_middle = grad_out + grad_middle_ff
    grad_attn_proj, grad_gain_pa = pull_attn(grad_middle)
    proj_low = grad_attn_proj.astype(BF16)
    grad_attn_low = jnp.dot(proj_low, full_out.T, preferred_element_type=F32).astype(BF16)
    near_mixed, far_mixed = weight_gradient(
        info, [(attn_low, proj_low), (hidden_low, down_low)], None, 640, "gradient_mixed"
    )
    came_mixed = swap_core(far_mixed)
    grad_attn_low, grad_gu, near_mixed = lax.optimization_barrier(
        (grad_attn_low, grad_gu, near_mixed)
    )
    mine_gu = scatter_halves(grad_gu)
    over_mixed = scatter_x(near_mixed, came_mixed)
    grad_query, far, near_far, near = attention_backward(
        info, query_low, attn_low, grad_attn_low, lse, blocks
    )
    grad_kv = scatter_keys(far, near_far, near).reshape(row_count, 2 * HD)
    grad_query_rows, grad_gain_q = [], 0.0
    for head in range(HQ):
        rows, gain = pull_query[head](grad_query[:, head * HD : (head + 1) * HD])
        grad_query_rows.append(rows.astype(BF16))
        grad_gain_q = grad_gain_q + gain
    query_grad_low = jnp.concatenate(grad_query_rows, axis=1)
    near_q, far_q = weight_gradient(
        info, [(input_low, query_grad_low)], None, 512, "gradient_q"
    )
    came_q = swap_core(far_q)
    over_q = scatter_x(near_q, came_q)
    grad_kv, over_mixed, over_q, mine_gu = lax.optimization_barrier(
        (grad_kv, over_mixed, over_q, mine_gu)
    )
    sum_gu = join_halves(mine_gu)
    sum_mixed = over_replicas(scatter_z(near_mixed, came_mixed, over_mixed))
    sum_q = over_replicas(scatter_z(near_q, came_q, over_q))
    grad_key_rows, grad_gain_k = pull_key(grad_kv[:, :HD])
    kv_grad_low = jnp.concatenate(
        [grad_key_rows.astype(BF16), grad_kv[:, HD:].astype(BF16)], axis=1
    )
    grad_normed_in = jnp.dot(query_grad_low, full_q.T, preferred_element_type=F32) + jnp.dot(
        kv_grad_low, full_kv.T, preferred_element_type=F32
    )
    grad_tokens_in, grad_gain_in = pull_in(grad_normed_in)
    token_grad = (grad_middle + grad_tokens_in).reshape(streams, SEG, D)
    wgrad_gains = jnp.concatenate(
        [grad_gain_in, grad_gain_pa, grad_gain_pf, grad_gain_po, grad_gain_q, grad_gain_k]
    )
    gains_out = jnp.pad(
        wgrad_gains.reshape(MEMBERS, gain_count), ((0, 0), (0, 2 * HD - gain_count))
    )
    near_kv, far_kv = weight_gradient(
        info, [(input_low, kv_grad_low)], gains_out, 2 * HD, "gradient_kv"
    )
    came_kv = swap_core(far_kv)
    sum_kv = over_replicas(scatter_z(near_kv, came_kv, scatter_x(near_kv, came_kv)))
    shard_qkv = jnp.concatenate([sum_q, sum_kv[:-8]], axis=1)
    shard_gains = sum_kv[-1, :gain_count]
    shard_out, shard_down = sum_mixed[:out_rows], sum_mixed[out_rows:]
    upd_qkv = adam_step(w_qkv, first_qkv, second_qkv, shard_qkv, RATE_MATRIX, DECAY_RATE)
    upd_out = adam_step(w_out, first_out, second_out, shard_out, RATE_MATRIX, DECAY_RATE)
    upd_gu = adam_step(w_gu, first_gu, second_gu, sum_gu, RATE_MATRIX, DECAY_RATE)
    upd_down = adam_step(w_down, first_down, second_down, shard_down, RATE_MATRIX, DECAY_RATE)
    upd_gains = adam_step(norm_gains, first_gains, second_gains, shard_gains, RATE_GAIN, 0.0)
    return (layer_out, token_grad, *upd_qkv, *upd_out, *upd_gu, *upd_down, *upd_gains)


def solution(mesh):
    in_specs = (
        P("replica", "group", None),
        P("replica", "group", None),
        P("replica", None),
        P("group", None),
        P("group", None),
        P("group", None),
        P("group", None),
        P("group"),
        P("group", None),
        P("group", None),
        P("group", None),
        P("group", None),
        P("group"),
        P("group", None),
        P("group", None),
        P("group", None),
        P("group", None),
        P("group"),
    )
    out_specs = (
        P("replica", "group", None),
        P("replica", "group", None),
        P("group", None),
        P("group", None),
        P("group", None),
        P("group", None),
        P("group", None),
        P("group", None),
        P("group", None),
        P("group", None),
        P("group", None),
        P("group", None),
        P("group", None),
        P("group", None),
        P("group"),
        P("group"),
        P("group"),
    )
    return jax.shard_map(
        per_device, mesh=mesh, in_specs=in_specs, out_specs=out_specs, check_vma=False
    )
```

```python
import math

import jax
import jax.numpy as jnp
from jax import lax
from jax.experimental import pallas as pl
from jax.experimental.pallas import tpu as pltpu
from jax.sharding import PartitionSpec as P

D = 640
HQ = 4
HD = 256
FF = 2048
SEG = 256
STEP = 10


EPS_NORM = 1e-06
BETA_ONE = 0.9
BETA_TWO = 0.999
ADAM_EPS = 1e-08
RATE_MATRIX = 0.1
RATE_GAIN = 0.5
DECAY_RATE = 0.1
ROPE_BASE = 1000000.0
NEGATIVE = -1e30
SCALE_SCORE = 0.0625


def rms_norm(values, gain_row):
    factor = lax.rsqrt(jnp.mean(values * values, axis=-1, keepdims=True) + EPS_NORM)
    return values * factor * gain_row


def angles(position, width):
    half_width = width // 2
    frequency = jnp.exp(
        jnp.arange(half_width, dtype=jnp.float32) * (-2.0 * math.log(ROPE_BASE) / width)
    )
    angle_table = position.astype(jnp.float32)[:, None] * frequency[None, :]
    return (jnp.cos(angle_table), jnp.sin(angle_table))


def rotate(values, cosine, sine):
    half_width = values.shape[-1] // 2
    leading = values[..., :half_width]
    trailing = values[..., half_width:]
    return jnp.concatenate(
        [leading * cosine - trailing * sine, trailing * cosine + leading * sine], axis=-1
    )


def layout(lengths, total):
    seq_ends = jnp.cumsum(lengths)
    seq_starts = seq_ends - lengths
    stream_index = jnp.arange(total, dtype=jnp.int32)
    segment = jnp.sum((stream_index[:, None] >= seq_ends[None, :]).astype(jnp.int32), axis=1)
    seq_begin = jnp.max(
        jnp.where(stream_index[:, None] >= seq_starts[None, :], seq_starts[None, :], 0), axis=1
    )
    return (segment, stream_index - seq_begin)


def head_in(values, gain_row, cosine, sine):
    return rotate(rms_norm(values, gain_row), cosine, sine)


def geglu(gate_up):
    return jax.nn.gelu(gate_up[:, :FF], approximate=True) * gate_up[:, FF:]


def split_gains(gain_all):
    return (
        gain_all[0:D],
        gain_all[D : 2 * D],
        gain_all[2 * D : 3 * D],
        gain_all[3 * D : 4 * D],
        gain_all[4 * D : 4 * D + HD],
        gain_all[4 * D + HD : 4 * D + 2 * HD],
    )


def adam_step(master, moment_one, moment_two, gradient, rate, decay):
    moment_new = BETA_ONE * moment_one + (1.0 - BETA_ONE) * gradient
    square_new = BETA_TWO * moment_two + (1.0 - BETA_TWO) * gradient * gradient
    moment_hat = moment_new / (1.0 - BETA_ONE**STEP)
    square_hat = square_new / (1.0 - BETA_TWO**STEP)
    master_new = master * (1.0 - rate * decay) - rate * moment_hat / (
        jnp.sqrt(square_hat) + ADAM_EPS
    )
    return (moment_new, square_new, master_new)


LOG2E = 1.4426950408889634
KEYS = 512
MEMBERS = 16
PACK = 32
REACH = 3
BLOCKS = 4 * REACH
NT = (((1,), (1,)), ((), ()))
TN = (((0,), (0,)), ((), ()))
F32 = jnp.float32
BF16 = jnp.bfloat16


def shift_z(values, k):
    return lax.ppermute(values, "group", [(i, (i + 4 * k) % MEMBERS) for i in range(MEMBERS)])


def line_up(values, lowest):
    return lax.ppermute(values, "group", [(i, i + 4) for i in range(4 * lowest, MEMBERS - 4)])


def line_down(values, lowest):
    return lax.ppermute(values, "group", [(i, i - 4) for i in range(4 * lowest, MEMBERS)])


def swap_x(values):
    return lax.ppermute(values, "group", [(i, i ^ 2) for i in range(MEMBERS)])


def swap_core(values):
    return lax.ppermute(values, "group", [(i, i ^ 1) for i in range(MEMBERS)])


def spread(lines):
    near = lines + [swap_x(line) for line in lines]
    return near + [swap_core(block) for block in near]


def gather_all(own):
    return spread([own] + [shift_z(own, k) for k in (1, 2, 3)])


def gather_keys(own, later):
    first = line_up(own, 0)
    first, later = lax.optimization_barrier((first, later))
    return spread([own, first, line_up(first, 1)]), later


def scatter_keys(far, near_far, near):
    running = None
    for k in range(REACH - 1, -1, -1):
        came = swap_core(far[k]).astype(F32)
        over = swap_x((near_far[k].astype(F32) + came[1]).astype(BF16))
        total = near[k].astype(F32) + came[0] + over.astype(F32)
        if running is not None:
            total = total + running.astype(F32)
        if k:
            running = line_down(total.astype(BF16), k)
    return total


def scatter_x(near, came):
    return swap_x((near[4:].astype(F32) + came[4:].astype(F32)).astype(BF16))


def scatter_z(near, came, over):
    total = [near[k].astype(F32) + came[k].astype(F32) + over[k].astype(F32) for k in range(4)]
    for k in (1, 2, 3):
        total[0] = total[0] + shift_z(total[k].astype(BF16), k).astype(F32)
    return total[0].astype(BF16)


def over_replicas(shard):
    if lax.axis_size("replica") == 2:
        other = lax.ppermute(shard, "replica", [(0, 1), (1, 0)])
        return shard.astype(F32) + other.astype(F32)
    return lax.psum(shard, "replica").astype(F32)


def owner_up(info, place):
    cr, xr, k = place // 8, place // 4 % 2, place % 4
    return ((info[1] + k) & 3) * 4 + (info[2] ^ xr) * 2 + (info[3] ^ cr)


def order_kernel(info, *refs):
    blocks = refs[:MEMBERS]
    full_ref, rows = refs[MEMBERS], refs[-1]
    count = rows.shape[0] // MEMBERS
    for place in range(MEMBERS):
        cr, xr, k = place // 8, place // 4 % 2, place % 4
        owner = ((info[1] - k) & 3) * 4 + (info[2] ^ xr) * 2 + (info[3] ^ cr)
        values = blocks[place][...].astype(F32)
        rows[pl.ds(pl.multiple_of(owner * count, 8), count)] = values[:count]
        if len(refs) > MEMBERS + 2:
            refs[MEMBERS + 1][pl.ds(owner, 1)] = values[count : count + 1]
    full_ref[...] = rows[...].astype(BF16)


def order_rows(info, blocks, name):
    rows, columns = blocks[0].shape
    count = rows // 8 * 8
    vmem = pl.BlockSpec(memory_space=pltpu.VMEM)
    shapes = [jax.ShapeDtypeStruct((MEMBERS * count, columns), BF16)]
    if rows > count:
        shapes.append(jax.ShapeDtypeStruct((MEMBERS, columns), F32))
    return pl.pallas_call(
        order_kernel,
        out_shape=shapes,
        in_specs=[pl.BlockSpec(memory_space=pltpu.SMEM)] + [vmem] * MEMBERS,
        out_specs=[vmem] * len(shapes),
        scratch_shapes=[pltpu.VMEM((MEMBERS * count, columns), F32)],
        compiler_params=pltpu.CompilerParams(vmem_limit_bytes=32 * 1024 * 1024),
        cost_estimate=pl.CostEstimate(flops=0, bytes_accessed=4_000_000, transcendentals=0),
        name=name,
    )(info, *blocks)


def gradient_kernel(tile, pairs, extra, info, *refs):
    operands = refs[: 2 * pairs + extra]
    near, far = refs[2 * pairs + extra : 2 * pairs + extra + 2]
    sums = refs[2 * pairs + extra + 2 :]
    columns = near.shape[2]
    for begin in range(0, columns, tile):
        at = slice(begin, begin + tile)
        for pair in range(pairs):
            left, right = operands[2 * pair], operands[2 * pair + 1]
            sums[pair][...] = lax.dot_general(
                left[...], right[:, at], TN, preferred_element_type=F32
            )
        for place in range(MEMBERS):
            owner = owner_up(info, place)
            parts = []
            for pair in range(pairs):
                count = sums[pair].shape[0] // MEMBERS
                parts.append(sums[pair][pl.ds(pl.multiple_of(owner * count, 8), count)])
            if extra:
                row = operands[2 * pairs][pl.ds(owner, 1), at]
                parts.append(jnp.broadcast_to(row, (8, tile)))
            block = jnp.concatenate(parts, axis=0) if len(parts) > 1 else parts[0]
            target = far if place >= 8 else near
            target[place % 8, :, at] = block.astype(BF16)


def weight_gradient(info, pairs, gains, tile, name):
    columns = pairs[0][1].shape[1]
    tokens_here = pairs[0][0].shape[0]
    counts = [left.shape[1] // MEMBERS for left, _ in pairs]
    rows = sum(counts) + (8 if gains is not None else 0)
    operands = [operand for pair in pairs for operand in pair]
    if gains is not None:
        operands.append(gains)
    shape = jax.ShapeDtypeStruct((MEMBERS // 2, rows, columns), BF16)
    vmem = pl.BlockSpec(memory_space=pltpu.VMEM)
    return pl.pallas_call(
        lambda *refs: gradient_kernel(tile, len(pairs), int(gains is not None), *refs),
        out_shape=(shape, shape),
        in_specs=[pl.BlockSpec(memory_space=pltpu.SMEM)] + [vmem] * len(operands),
        out_specs=(vmem, vmem),
        scratch_shapes=[pltpu.VMEM((MEMBERS * count, tile), F32) for count in counts],
        compiler_params=pltpu.CompilerParams(vmem_limit_bytes=48 * 1024 * 1024),
        cost_estimate=pl.CostEstimate(
            flops=2 * tokens_here * columns * MEMBERS * sum(counts),
            bytes_accessed=4 * MEMBERS * rows * columns,
            transcendentals=0,
        ),
        name=name,
    )(info, *operands)


def pack_shards(out_shard, down_shard, gu_shard):
    mixed = jnp.concatenate([out_shard, down_shard], axis=0)
    rows, columns = mixed.shape
    tiles = mixed.reshape(rows // PACK, PACK, columns // 128, 128).transpose(1, 0, 2, 3)
    flat = tiles.reshape(PACK, -1)
    flat = jnp.pad(flat, ((0, 0), (0, gu_shard.shape[1] - flat.shape[1])))
    return jnp.concatenate([flat, gu_shard], axis=0)


def unpack_mixed(packed, rows):
    tiles = packed[:PACK, : rows // PACK * D].reshape(PACK, rows // PACK, D // 128, 128)
    return tiles.transpose(1, 0, 2, 3).reshape(rows, D)


def unpack_kernel(packed, out_ref, down_ref, gu_ref):
    out_rows, down_rows = out_ref.shape[0] // 2, down_ref.shape[0] // 2
    for member in range(2):
        for i in range((out_rows + down_rows) // PACK):
            for j in range(D // 128):
                tile = 128 * (i * (D // 128) + j)
                values = packed[member, 0:PACK, tile : tile + 128]
                if i < out_rows // PACK:
                    row = member * out_rows + i * PACK
                    out_ref[row : row + PACK, 128 * j : 128 * j + 128] = values
                else:
                    row = member * down_rows + i * PACK - out_rows
                    down_ref[row : row + PACK, 128 * j : 128 * j + 128] = values
    for begin in range(0, 2 * FF, 1024):
        at = slice(begin, begin + 1024)
        both = [packed[member, PACK:, at].astype(F32) for member in range(2)]
        gu_ref[:, at] = jnp.concatenate(both, axis=0).astype(BF16)


def unpack_weights(packed):
    rows = packed.shape[1]
    out_rows, down_rows, gu_rows = HQ * HD // MEMBERS, FF // MEMBERS, rows - PACK
    return pl.pallas_call(
        unpack_kernel,
        grid=(MEMBERS // 2,),
        out_shape=(
            jax.ShapeDtypeStruct((HQ * HD, D), BF16),
            jax.ShapeDtypeStruct((FF, D), BF16),
            jax.ShapeDtypeStruct((MEMBERS * gu_rows, 2 * FF), BF16),
        ),
        in_specs=[pl.BlockSpec((2, rows, 2 * FF), lambda i: (i, 0, 0))],
        out_specs=(
            pl.BlockSpec((2 * out_rows, D), lambda i: (i, 0)),
            pl.BlockSpec((2 * down_rows, D), lambda i: (i, 0)),
            pl.BlockSpec((2 * gu_rows, 2 * FF), lambda i: (i, 0)),
        ),
        compiler_params=pltpu.CompilerParams(vmem_limit_bytes=32 * 1024 * 1024),
        cost_estimate=pl.CostEstimate(flops=0, bytes_accessed=19_000_000, transcendentals=0),
        name="unpack_weights",
    )(packed)


def packed_kernel(ff, gate_up, attn, proj, hidden, down, packed):
    gu_rows = packed.shape[1] - PACK
    out_rows, down_rows = HQ * HD // MEMBERS, FF // MEMBERS
    for begin in range(0, 2 * FF, 512):
        at = slice(begin, begin + 512)
        block = lax.dot_general(ff[...], gate_up[:, at], TN, preferred_element_type=F32)
        for member in range(MEMBERS):
            rows = slice(member * gu_rows, (member + 1) * gu_rows)
            packed[member, PACK:, at] = block[rows].astype(BF16)
    for left, right, count, offset in ((attn, proj, out_rows, 0), (hidden, down, down_rows, out_rows)):
        for begin in range(0, MEMBERS * count, 512):
            block = lax.dot_general(
                left[:, begin : begin + 512], right[...], TN, preferred_element_type=F32
            ).astype(BF16)
            for row in range(begin, begin + 512, PACK):
                i = (offset + row % count) // PACK
                for j in range(D // 128):
                    tile = 128 * (i * (D // 128) + j)
                    packed[row // count, 0:PACK, tile : tile + 128] = block[
                        row - begin : row - begin + PACK, 128 * j : 128 * j + 128
                    ]
    used = D // 128 * 128 * ((out_rows + down_rows) // PACK)
    packed[:, 0:PACK, used:] = jnp.zeros((MEMBERS, PACK, 2 * FF - used), BF16)


def packed_gradient(ff, gate_up, attn, proj, hidden, down):
    vmem = pl.BlockSpec(memory_space=pltpu.VMEM)
    rows = PACK + D // MEMBERS
    return pl.pallas_call(
        packed_kernel,
        out_shape=jax.ShapeDtypeStruct((MEMBERS, rows, 2 * FF), BF16),
        in_specs=[vmem] * 6,
        out_specs=vmem,
        compiler_params=pltpu.CompilerParams(vmem_limit_bytes=48 * 1024 * 1024),
        cost_estimate=pl.CostEstimate(
            flops=2 * ff.shape[0] * (D * 2 * FF + D * FF + D * HQ * HD),
            bytes_accessed=19_000_000,
            transcendentals=0,
        ),
        name="packed_gradient",
    )(ff, gate_up, attn, proj, hidden, down)


def key_range(info, stream):
    first = info[0]
    bound = info[4 + stream]
    low = jnp.where(first >= bound, bound, 0)
    high = jnp.where(first + SEG - 1 >= bound, bound, 0)
    return first, bound, low, high


def load_blocks(info, blocks, kv, sem):
    z, x, c = info[1], info[2], info[3]
    copies = []
    for place in range(len(blocks)):
        cr, xr, k = place // (2 * REACH), place // REACH % 2, place % REACH
        owner = ((z - k) & 3) * 4 + (x ^ xr) * 2 + (c ^ cr)
        copies.append(pltpu.make_async_copy(blocks[place], kv.at[owner], sem.at[place]))
    for copy in copies:
        copy.start()
    return copies


def forward_kernel(info, q_ref, *refs):
    blocks = refs[:BLOCKS]
    o_ref, lse_ref, kv, acc, total, sem = refs[BLOCKS:]
    copies = load_blocks(info, blocks, kv, sem)
    for copy in copies:
        copy.wait()

    def one_stream(stream, carry):
        mine = pl.ds(pl.multiple_of(stream * SEG, SEG), SEG)
        first, bound, low, high = key_range(info, stream)
        begin = low // KEYS
        diagonal = first // KEYS
        clear = jnp.clip((high + KEYS - 1) // KEYS, begin, diagonal)
        acc[...] = jnp.zeros_like(acc)
        total[...] = jnp.zeros_like(total)

        def visit(j, masked):
            keys = kv[pl.ds(2 * j, 2), stream, :, 0:HD].reshape(KEYS, HD)
            values = kv[pl.ds(2 * j, 2), stream, :, HD : 2 * HD].reshape(KEYS, HD)
            if masked:
                row = first + lax.broadcasted_iota(jnp.int32, (SEG, KEYS), 0)
                col = j * KEYS + lax.broadcasted_iota(jnp.int32, (SEG, KEYS), 1)
                mask = (col <= row) & (col >= jnp.where(row >= bound, bound, 0))
            for head in range(HQ):
                rows = slice(head * SEG, (head + 1) * SEG)
                query = q_ref[mine, head * HD : (head + 1) * HD]
                score = lax.dot_general(query, keys, NT, preferred_element_type=F32)
                prob = jnp.exp2(score * (SCALE_SCORE * LOG2E))
                if masked:
                    prob = jnp.where(mask, prob, 0.0)
                total[rows] += (
                    prob[:, 0:128] + prob[:, 128:256] + prob[:, 256:384] + prob[:, 384:512]
                )
                acc[rows] += jnp.dot(prob.astype(BF16), values, preferred_element_type=F32)

        def masked_step(i, carry):
            visit(jnp.where(i < clear, i, diagonal), True)
            return carry

        def clear_step(j, carry):
            visit(j, False)
            return carry

        lax.fori_loop(begin, clear + 1, masked_step, 0)
        lax.fori_loop(clear, diagonal, clear_step, 0)
        for head in range(HQ):
            rows = slice(head * SEG, (head + 1) * SEG)
            part = total[rows]
            out = acc[rows] / jnp.sum(part, axis=1, keepdims=True)
            o_ref[mine, head * HD : (head + 1) * HD] = out.astype(BF16)
            lse_ref[stream, :, rows] = jnp.log2(jnp.sum(part.T, axis=0, keepdims=True))
        return carry

    lax.fori_loop(0, 2, one_stream, 0)


def attention_forward(info, query, blocks):
    vmem = pl.BlockSpec(memory_space=pltpu.VMEM)
    return pl.pallas_call(
        forward_kernel,
        out_shape=(
            jax.ShapeDtypeStruct((2 * SEG, HQ * HD), BF16),
            jax.ShapeDtypeStruct((2, 1, HQ * SEG), F32),
        ),
        in_specs=[pl.BlockSpec(memory_space=pltpu.SMEM), vmem]
        + [pl.BlockSpec(memory_space=pl.ANY)] * BLOCKS,
        out_specs=(vmem, vmem),
        scratch_shapes=[
            pltpu.VMEM((MEMBERS, 2, SEG, 2 * HD), BF16),
            pltpu.VMEM((HQ * SEG, HD), F32),
            pltpu.VMEM((HQ * SEG, 128), F32),
            pltpu.SemaphoreType.DMA((BLOCKS,)),
        ],
        compiler_params=pltpu.CompilerParams(vmem_limit_bytes=40 * 1024 * 1024),
        cost_estimate=pl.CostEstimate(
            flops=7_000_000_000, bytes_accessed=9_000_000, transcendentals=7_000_000
        ),
        name="attention_forward",
    )(info, query, *blocks)


def backward_kernel(info, q_ref, o_ref, do_ref, lse_ref, *refs):
    blocks = refs[:BLOCKS]
    dq_ref = refs[BLOCKS]
    far = refs[BLOCKS + 1 : BLOCKS + 1 + REACH]
    near_far = refs[BLOCKS + 1 + REACH : BLOCKS + 1 + 2 * REACH]
    near = refs[BLOCKS + 1 + 2 * REACH : BLOCKS + 1 + 3 * REACH]
    kv, dkv, qs, qt, dos, dot_, dqt, delta, sem, out_sem = refs[BLOCKS + 1 + 3 * REACH :]
    copies = load_blocks(info, blocks, kv, sem)
    z, x, c = info[1], info[2], info[3]

    def clean(place, carry):
        dkv[place] = jnp.zeros((2, SEG, 2 * HD), BF16)
        return carry

    lax.fori_loop(0, BLOCKS, clean, 0)
    for copy in copies:
        copy.wait()

    def one_stream(stream, carry):
        first, bound, low, _ = key_range(info, stream)
        mine = pl.ds(pl.multiple_of(stream * SEG, SEG), SEG)
        for head in range(HQ):
            rows = slice(head * SEG, (head + 1) * SEG)
            lanes = slice(head * HD, (head + 1) * HD)
            query = q_ref[mine, lanes]
            grad = do_ref[mine, lanes]
            qs[rows] = query
            dos[rows] = grad
            qt[:, rows] = query.T
            dot_[:, rows] = grad.T
            both = grad.astype(F32) * o_ref[mine, lanes].astype(F32)
            delta[:, rows] = jnp.sum((both[:, 0:128] + both[:, 128:256]).T, axis=0, keepdims=True)
        dqt[...] = jnp.zeros_like(dqt)
        shape = (SEG, HQ * SEG)

        def visit(j, carry):
            keys = kv[j, stream, :, 0:HD]
            values = kv[j, stream, :, HD : 2 * HD]
            score = jnp.dot(keys, qt[...], preferred_element_type=F32)
            prob = jnp.exp2(score * (SCALE_SCORE * LOG2E) - lse_ref[stream])
            row = first + (lax.broadcasted_iota(jnp.int32, (1, HQ * SEG), 1) & (SEG - 1))
            start = jnp.where(row >= bound, bound, 0)
            col = j * SEG + lax.broadcasted_iota(jnp.int32, shape, 0)
            prob = jnp.where((col <= row) & (col >= start), prob, 0.0)
            dprob = jnp.dot(values, dot_[...], preferred_element_type=F32)
            dscore = (prob * (dprob - delta[...])).astype(BF16)
            dv = jnp.dot(prob.astype(BF16), dos[...], preferred_element_type=F32)
            dk = jnp.dot(dscore, qs[...], preferred_element_type=F32)
            dqt[...] += jnp.dot(keys.T, dscore, preferred_element_type=F32)
            place = ((j & 1) ^ c) * (2 * REACH) + (z - (j >> 2)) * 2 + (((j >> 1) & 1) ^ x)
            dkv[place, stream, :, 0:HD] = (dk * SCALE_SCORE).astype(BF16)
            dkv[place, stream, :, HD : 2 * HD] = dv.astype(BF16)
            return carry

        lax.fori_loop(low // SEG, first // SEG + 1, visit, 0)
        for head in range(HQ):
            rows = slice(head * SEG, (head + 1) * SEG)
            dq_ref[mine, head * HD : (head + 1) * HD] = dqt[:, rows].T * SCALE_SCORE
        return carry

    lax.fori_loop(0, 2, one_stream, 0)
    outs = []
    for k in range(REACH):
        outs.append((dkv.at[pl.ds(2 * REACH + 2 * k, 2)], far[k]))
        outs.append((dkv.at[2 * k + 1], near_far[k]))
        outs.append((dkv.at[2 * k], near[k]))
    copies = [
        pltpu.make_async_copy(source, target, out_sem.at[n])
        for n, (source, target) in enumerate(outs)
    ]
    for copy in copies:
        copy.start()
    for copy in copies:
        copy.wait()


def attention_backward(info, query, out, grad_out, lse, blocks):
    one = jax.ShapeDtypeStruct((2, SEG, 2 * HD), BF16)
    two = jax.ShapeDtypeStruct((2, 2, SEG, 2 * HD), BF16)
    vmem = pl.BlockSpec(memory_space=pltpu.VMEM)
    anywhere = pl.BlockSpec(memory_space=pl.ANY)
    result = pl.pallas_call(
        backward_kernel,
        out_shape=[jax.ShapeDtypeStruct((2 * SEG, HQ * HD), F32)]
        + [two] * REACH
        + [one] * (2 * REACH),
        in_specs=[pl.BlockSpec(memory_space=pltpu.SMEM)] + [vmem] * 4 + [anywhere] * BLOCKS,
        out_specs=[vmem] + [anywhere] * (3 * REACH),
        scratch_shapes=[
            pltpu.VMEM((MEMBERS, 2, SEG, 2 * HD), BF16),
            pltpu.VMEM((BLOCKS, 2, SEG, 2 * HD), BF16),
            pltpu.VMEM((HQ * SEG, HD), BF16),
            pltpu.VMEM((HD, HQ * SEG), BF16),
            pltpu.VMEM((HQ * SEG, HD), BF16),
            pltpu.VMEM((HD, HQ * SEG), BF16),
            pltpu.VMEM((HD, HQ * SEG), F32),
            pltpu.VMEM((1, HQ * SEG), F32),
            pltpu.SemaphoreType.DMA((BLOCKS,)),
            pltpu.SemaphoreType.DMA((3 * REACH,)),
        ],
        compiler_params=pltpu.CompilerParams(vmem_limit_bytes=52 * 1024 * 1024),
        cost_estimate=pl.CostEstimate(
            flops=17_000_000_000, bytes_accessed=20_000_000, transcendentals=7_000_000
        ),
        name="attention_backward",
    )(info, query, out, grad_out, lse, *blocks)
    return result[0], result[1 : 1 + REACH], result[1 + REACH : 1 + 2 * REACH], result[1 + 2 * REACH :]


def per_device(
    tokens,
    cotangent,
    lengths,
    w_qkv,
    w_out,
    w_gu,
    w_down,
    norm_gains,
    first_qkv,
    first_out,
    first_gu,
    first_down,
    first_gains,
    second_qkv,
    second_out,
    second_gu,
    second_down,
    second_gains,
):
    streams = tokens.shape[0]
    row_count = streams * SEG
    member_index = lax.axis_index("group")
    tok_rows = tokens.reshape(row_count, D).astype(F32)
    grad_out = cotangent.reshape(row_count, D).astype(F32)
    start_row = member_index * SEG
    boundary = lengths[:, 0]
    info = jnp.concatenate(
        [
            jnp.stack([start_row, member_index // 4, member_index // 2 % 2, member_index % 2]),
            boundary,
        ]
    ).astype(jnp.int32)
    q_width = HQ * HD
    low_qkv = w_qkv.astype(BF16)
    gain_count = norm_gains.shape[0]
    gain_row = jnp.pad(norm_gains.astype(BF16), (0, 2 * HD - gain_count))
    full_kv, gain_rows = order_rows(
        info,
        gather_all(jnp.concatenate([low_qkv[:, q_width:], gain_row[None]], axis=0)),
        "order_kv",
    )
    full_gains = gain_rows[:, :gain_count].reshape(-1)
    gain_in, gain_pa, gain_pf, gain_po, gain_query, gain_key = split_gains(full_gains)
    out_rows = w_out.shape[0]
    down_rows = w_down.shape[0]
    full_out, full_down, full_gu = unpack_weights(
        lax.all_gather(
            pack_shards(w_out.astype(BF16), w_down.astype(BF16), w_gu.astype(BF16)),
            "group",
            axis=0,
            tiled=False,
        )
    )
    index_mine = start_row + jnp.arange(SEG, dtype=jnp.int32)
    position_mine = index_mine[None, :] - jnp.where(
        index_mine[None, :] >= boundary[:, None], boundary[:, None], 0
    )
    cosine, sine = angles(position_mine.reshape(row_count), HD)
    normed_in, pull_in = jax.vjp(rms_norm, tok_rows, gain_in)
    input_low = normed_in.astype(BF16)
    kv_rows = jnp.dot(input_low, full_kv, preferred_element_type=F32)
    key_rot, pull_key = jax.vjp(
        lambda rows, gain: head_in(rows, gain, cosine, sine), kv_rows[:, :HD], gain_key
    )
    kv_low = jnp.concatenate([key_rot.astype(BF16), kv_rows[:, HD:].astype(BF16)], axis=1)
    blocks, low_q = gather_keys(kv_low.reshape(streams, SEG, 2 * HD), low_qkv[:, :q_width])
    (full_q,) = order_rows(info, gather_all(low_q), "order_q")
    query_rows = jnp.dot(input_low, full_q, preferred_element_type=F32)
    query_rot, pull_query = [], []
    for head in range(HQ):
        rotated, pull = jax.vjp(
            lambda rows, gain: head_in(rows, gain, cosine, sine),
            query_rows[:, head * HD : (head + 1) * HD],
            gain_query,
        )
        query_rot.append(rotated.astype(BF16))
        pull_query.append(pull)
    query_low = jnp.concatenate(query_rot, axis=1)
    attn_low, lse = attention_forward(info, query_low, blocks)
    attn_proj = jnp.dot(attn_low, full_out, preferred_element_type=F32)
    post_attn, pull_attn = jax.vjp(rms_norm, attn_proj, gain_pa)
    middle = tok_rows + post_attn
    normed_ff, pull_ff = jax.vjp(rms_norm, middle, gain_pf)
    ff_low = normed_ff.astype(BF16)
    gate_up = jnp.dot(ff_low, full_gu, preferred_element_type=F32)
    hidden, pull_geglu = jax.vjp(geglu, gate_up)
    hidden_low = hidden.astype(BF16)
    down_proj = jnp.dot(hidden_low, full_down, preferred_element_type=F32)
    post_ff, pull_post = jax.vjp(rms_norm, down_proj, gain_po)
    layer_out = (middle + post_ff).astype(BF16).reshape(streams, SEG, D)
    grad_down, grad_gain_po = pull_post(grad_out)
    down_low = grad_down.astype(BF16)
    grad_hidden = jnp.dot(down_low, full_down.T, preferred_element_type=F32)
    (grad_gate_up,) = pull_geglu(grad_hidden)
    gate_up_low = grad_gate_up.astype(BF16)
    grad_normed_ff = jnp.dot(gate_up_low, full_gu.T, preferred_element_type=F32)
    grad_middle_ff, grad_gain_pf = pull_ff(grad_normed_ff)
    grad_middle = grad_out + grad_middle_ff
    grad_attn_proj, grad_gain_pa = pull_attn(grad_middle)
    proj_low = grad_attn_proj.astype(BF16)
    grad_attn_low = jnp.dot(proj_low, full_out.T, preferred_element_type=F32).astype(BF16)
    packed = packed_gradient(ff_low, gate_up_low, attn_low, proj_low, hidden_low, down_low)
    grad_attn_low, packed = lax.optimization_barrier((grad_attn_low, packed))
    mine = lax.psum_scatter(packed, "group", scatter_dimension=0, tiled=False)
    grad_query, far, near_far, near = attention_backward(
        info, query_low, attn_low, grad_attn_low, lse, blocks
    )
    grad_kv = scatter_keys(far, near_far, near).reshape(row_count, 2 * HD)
    grad_query_rows, grad_gain_q = [], 0.0
    for head in range(HQ):
        rows, gain = pull_query[head](grad_query[:, head * HD : (head + 1) * HD])
        grad_query_rows.append(rows.astype(BF16))
        grad_gain_q = grad_gain_q + gain
    query_grad_low = jnp.concatenate(grad_query_rows, axis=1)
    near_q, far_q = weight_gradient(
        info, [(input_low, query_grad_low)], None, 512, "gradient_q"
    )
    came_q = swap_core(far_q)
    over_q = scatter_x(near_q, came_q)
    grad_kv, over_q = lax.optimization_barrier((grad_kv, over_q))
    sum_q = over_replicas(scatter_z(near_q, came_q, over_q))
    grad_key_rows, grad_gain_k = pull_key(grad_kv[:, :HD])
    kv_grad_low = jnp.concatenate(
        [grad_key_rows.astype(BF16), grad_kv[:, HD:].astype(BF16)], axis=1
    )
    grad_normed_in = jnp.dot(query_grad_low, full_q.T, preferred_element_type=F32) + jnp.dot(
        kv_grad_low, full_kv.T, preferred_element_type=F32
    )
    grad_tokens_in, grad_gain_in = pull_in(grad_normed_in)
    token_grad = (grad_middle + grad_tokens_in).reshape(streams, SEG, D)
    wgrad_gains = jnp.concatenate(
        [grad_gain_in, grad_gain_pa, grad_gain_pf, grad_gain_po, grad_gain_q, grad_gain_k]
    )
    gains_out = jnp.pad(
        wgrad_gains.reshape(MEMBERS, gain_count), ((0, 0), (0, 2 * HD - gain_count))
    )
    near_kv, far_kv = weight_gradient(
        info, [(input_low, kv_grad_low)], gains_out, 2 * HD, "gradient_kv"
    )
    came_kv, mine = lax.optimization_barrier((swap_core(far_kv), mine))
    sum_kv = over_replicas(scatter_z(near_kv, came_kv, scatter_x(near_kv, came_kv)))
    shard_qkv = jnp.concatenate([sum_q, sum_kv[:-8]], axis=1)
    shard_gains = sum_kv[-1, :gain_count]
    sum_packed = over_replicas(mine)
    sum_gu = sum_packed[PACK:]
    sum_mixed = unpack_mixed(sum_packed, out_rows + down_rows)
    shard_out, shard_down = sum_mixed[:out_rows], sum_mixed[out_rows:]
    upd_qkv = adam_step(w_qkv, first_qkv, second_qkv, shard_qkv, RATE_MATRIX, DECAY_RATE)
    upd_out = adam_step(w_out, first_out, second_out, shard_out, RATE_MATRIX, DECAY_RATE)
    upd_gu = adam_step(w_gu, first_gu, second_gu, sum_gu, RATE_MATRIX, DECAY_RATE)
    upd_down = adam_step(w_down, first_down, second_down, shard_down, RATE_MATRIX, DECAY_RATE)
    upd_gains = adam_step(norm_gains, first_gains, second_gains, shard_gains, RATE_GAIN, 0.0)
    return (layer_out, token_grad, *upd_qkv, *upd_out, *upd_gu, *upd_down, *upd_gains)


def solution(mesh):
    in_specs = (
        P("replica", "group", None),
        P("replica", "group", None),
        P("replica", None),
        P("group", None),
        P("group", None),
        P("group", None),
        P("group", None),
        P("group"),
        P("group", None),
        P("group", None),
        P("group", None),
        P("group", None),
        P("group"),
        P("group", None),
        P("group", None),
        P("group", None),
        P("group", None),
        P("group"),
    )
    out_specs = (
        P("replica", "group", None),
        P("replica", "group", None),
        P("group", None),
        P("group", None),
        P("group", None),
        P("group", None),
        P("group", None),
        P("group", None),
        P("group", None),
        P("group", None),
        P("group", None),
        P("group", None),
        P("group", None),
        P("group", None),
        P("group"),
        P("group"),
        P("group"),
    )
    return jax.shard_map(
        per_device, mesh=mesh, in_specs=in_specs, out_specs=out_specs, check_vma=False
    )
```

```python
import math

import jax
import jax.numpy as jnp
from jax import lax
from jax.experimental import pallas as pl
from jax.experimental.pallas import tpu as pltpu
from jax.sharding import PartitionSpec as P

D = 640
HQ = 4
HD = 256
FF = 2048
SEG = 256
STEP = 10


EPS_NORM = 1e-06
BETA_ONE = 0.9
BETA_TWO = 0.999
ADAM_EPS = 1e-08
RATE_MATRIX = 0.1
RATE_GAIN = 0.5
DECAY_RATE = 0.1
ROPE_BASE = 1000000.0
NEGATIVE = -1e30
SCALE_SCORE = 0.0625


def rms_norm(values, gain_row):
    factor = lax.rsqrt(jnp.mean(values * values, axis=-1, keepdims=True) + EPS_NORM)
    return values * factor * gain_row


def angles(position, width):
    half_width = width // 2
    frequency = jnp.exp(
        jnp.arange(half_width, dtype=jnp.float32) * (-2.0 * math.log(ROPE_BASE) / width)
    )
    angle_table = position.astype(jnp.float32)[:, None] * frequency[None, :]
    return (jnp.cos(angle_table), jnp.sin(angle_table))


def rotate(values, cosine, sine):
    half_width = values.shape[-1] // 2
    leading = values[..., :half_width]
    trailing = values[..., half_width:]
    return jnp.concatenate(
        [leading * cosine - trailing * sine, trailing * cosine + leading * sine], axis=-1
    )


def layout(lengths, total):
    seq_ends = jnp.cumsum(lengths)
    seq_starts = seq_ends - lengths
    stream_index = jnp.arange(total, dtype=jnp.int32)
    segment = jnp.sum((stream_index[:, None] >= seq_ends[None, :]).astype(jnp.int32), axis=1)
    seq_begin = jnp.max(
        jnp.where(stream_index[:, None] >= seq_starts[None, :], seq_starts[None, :], 0), axis=1
    )
    return (segment, stream_index - seq_begin)


def head_in(values, gain_row, cosine, sine):
    return rotate(rms_norm(values, gain_row), cosine, sine)


def geglu(gate_up):
    return jax.nn.gelu(gate_up[:, :FF], approximate=True) * gate_up[:, FF:]


def split_gains(gain_all):
    return (
        gain_all[0:D],
        gain_all[D : 2 * D],
        gain_all[2 * D : 3 * D],
        gain_all[3 * D : 4 * D],
        gain_all[4 * D : 4 * D + HD],
        gain_all[4 * D + HD : 4 * D + 2 * HD],
    )


def adam_step(master, moment_one, moment_two, gradient, rate, decay):
    moment_new = BETA_ONE * moment_one + (1.0 - BETA_ONE) * gradient
    square_new = BETA_TWO * moment_two + (1.0 - BETA_TWO) * gradient * gradient
    moment_hat = moment_new / (1.0 - BETA_ONE**STEP)
    square_hat = square_new / (1.0 - BETA_TWO**STEP)
    master_new = master * (1.0 - rate * decay) - rate * moment_hat / (
        jnp.sqrt(square_hat) + ADAM_EPS
    )
    return (moment_new, square_new, master_new)


LOG2E = 1.4426950408889634
KEYS = 512
MEMBERS = 16
PACK = 32
HEAD = 24
REACH = 3
BLOCKS = 4 * REACH
NT = (((1,), (1,)), ((), ()))
TN = (((0,), (0,)), ((), ()))
F32 = jnp.float32
BF16 = jnp.bfloat16


def shift_z(values, k):
    return lax.ppermute(values, "group", [(i, (i + 4 * k) % MEMBERS) for i in range(MEMBERS)])


def line_up(values, lowest):
    return lax.ppermute(values, "group", [(i, i + 4) for i in range(4 * lowest, MEMBERS - 4)])


def line_down(values, lowest):
    return lax.ppermute(values, "group", [(i, i - 4) for i in range(4 * lowest, MEMBERS)])


def swap_x(values):
    return lax.ppermute(values, "group", [(i, i ^ 2) for i in range(MEMBERS)])


def swap_core(values):
    return lax.ppermute(values, "group", [(i, i ^ 1) for i in range(MEMBERS)])


def spread(lines):
    near = lines + [swap_x(line) for line in lines]
    return near + [swap_core(block) for block in near]


def gather_all(own):
    return spread([own] + [shift_z(own, k) for k in (1, 2, 3)])


def gather_keys(own, later):
    first = line_up(own, 0)
    second, over, over_first, later = lax.optimization_barrier(
        (line_up(first, 1), swap_x(own), swap_x(first), later)
    )
    near = [own, first, second, over, over_first, swap_x(second)]
    return near + [swap_core(block) for block in near], later


def scatter_keys(far, near_far, near):
    running = None
    for k in range(REACH - 1, -1, -1):
        came = swap_core(far[k]).astype(F32)
        over = swap_x((near_far[k].astype(F32) + came[1]).astype(BF16))
        total = near[k].astype(F32) + came[0] + over.astype(F32)
        if running is not None:
            total = total + running.astype(F32)
        if k:
            running = line_down(total.astype(BF16), k)
    return total


def scatter_x(near, came):
    return swap_x((near[4:].astype(F32) + came[4:].astype(F32)).astype(BF16))


def scatter_z(near, came, over):
    total = [near[k].astype(F32) + came[k].astype(F32) + over[k].astype(F32) for k in range(4)]
    for k in (1, 2, 3):
        total[0] = total[0] + shift_z(total[k].astype(BF16), k).astype(F32)
    return total[0].astype(BF16)


def over_replicas(shard):
    if lax.axis_size("replica") == 2:
        other = lax.ppermute(shard, "replica", [(0, 1), (1, 0)])
        return shard.astype(F32) + other.astype(F32)
    return lax.psum(shard, "replica").astype(F32)


def owner_up(info, place):
    cr, xr, k = place // 8, place // 4 % 2, place % 4
    return ((info[1] + k) & 3) * 4 + (info[2] ^ xr) * 2 + (info[3] ^ cr)


def order_kernel(info, *refs):
    blocks = refs[:MEMBERS]
    full_ref, rows = refs[MEMBERS], refs[-1]
    count = rows.shape[0] // MEMBERS
    for place in range(MEMBERS):
        cr, xr, k = place // 8, place // 4 % 2, place % 4
        owner = ((info[1] - k) & 3) * 4 + (info[2] ^ xr) * 2 + (info[3] ^ cr)
        values = blocks[place][...].astype(F32)
        rows[pl.ds(pl.multiple_of(owner * count, 8), count)] = values[:count]
        if len(refs) > MEMBERS + 2:
            refs[MEMBERS + 1][pl.ds(owner, 1)] = values[count : count + 1]
    full_ref[...] = rows[...].astype(BF16)


def order_rows(info, blocks, name):
    rows, columns = blocks[0].shape
    count = rows // 8 * 8
    vmem = pl.BlockSpec(memory_space=pltpu.VMEM)
    shapes = [jax.ShapeDtypeStruct((MEMBERS * count, columns), BF16)]
    if rows > count:
        shapes.append(jax.ShapeDtypeStruct((MEMBERS, columns), F32))
    return pl.pallas_call(
        order_kernel,
        out_shape=shapes,
        in_specs=[pl.BlockSpec(memory_space=pltpu.SMEM)] + [vmem] * MEMBERS,
        out_specs=[vmem] * len(shapes),
        scratch_shapes=[pltpu.VMEM((MEMBERS * count, columns), F32)],
        compiler_params=pltpu.CompilerParams(vmem_limit_bytes=32 * 1024 * 1024),
        cost_estimate=pl.CostEstimate(flops=0, bytes_accessed=4_000_000, transcendentals=0),
        name=name,
    )(info, *blocks)


def gradient_kernel(tile, pairs, extra, info, *refs):
    operands = refs[: 2 * pairs + extra]
    near, far = refs[2 * pairs + extra : 2 * pairs + extra + 2]
    sums = refs[2 * pairs + extra + 2 :]
    columns = near.shape[2]
    for begin in range(0, columns, tile):
        at = slice(begin, begin + tile)
        for pair in range(pairs):
            left, right = operands[2 * pair], operands[2 * pair + 1]
            sums[pair][...] = lax.dot_general(
                left[...], right[:, at], TN, preferred_element_type=F32
            )
        for place in range(MEMBERS):
            owner = owner_up(info, place)
            parts = []
            for pair in range(pairs):
                count = sums[pair].shape[0] // MEMBERS
                parts.append(sums[pair][pl.ds(pl.multiple_of(owner * count, 8), count)])
            if extra:
                row = operands[2 * pairs][pl.ds(owner, 1), at]
                parts.append(jnp.broadcast_to(row, (8, tile)))
            block = jnp.concatenate(parts, axis=0) if len(parts) > 1 else parts[0]
            target = far if place >= 8 else near
            target[place % 8, :, at] = block.astype(BF16)


def weight_gradient(info, pairs, gains, tile, name):
    columns = pairs[0][1].shape[1]
    tokens_here = pairs[0][0].shape[0]
    counts = [left.shape[1] // MEMBERS for left, _ in pairs]
    rows = sum(counts) + (8 if gains is not None else 0)
    operands = [operand for pair in pairs for operand in pair]
    if gains is not None:
        operands.append(gains)
    shape = jax.ShapeDtypeStruct((MEMBERS // 2, rows, columns), BF16)
    vmem = pl.BlockSpec(memory_space=pltpu.VMEM)
    return pl.pallas_call(
        lambda *refs: gradient_kernel(tile, len(pairs), int(gains is not None), *refs),
        out_shape=(shape, shape),
        in_specs=[pl.BlockSpec(memory_space=pltpu.SMEM)] + [vmem] * len(operands),
        out_specs=(vmem, vmem),
        scratch_shapes=[pltpu.VMEM((MEMBERS * count, tile), F32) for count in counts],
        compiler_params=pltpu.CompilerParams(vmem_limit_bytes=48 * 1024 * 1024),
        cost_estimate=pl.CostEstimate(
            flops=2 * tokens_here * columns * MEMBERS * sum(counts),
            bytes_accessed=4 * MEMBERS * rows * columns,
            transcendentals=0,
        ),
        name=name,
    )(info, *operands)


def pack_shards(out_shard, down_shard, gu_shard):
    mixed = jnp.concatenate([out_shard, down_shard], axis=0)
    rows, columns = mixed.shape
    tiles = mixed.reshape(rows // PACK, PACK, columns // 128, 128).transpose(1, 0, 2, 3)
    flat = tiles.reshape(PACK, -1)
    flat = jnp.pad(flat, ((0, 0), (0, gu_shard.shape[1] - flat.shape[1])))
    return jnp.concatenate([flat, gu_shard], axis=0)


def unpack_down(packed, rows):
    tiles = packed[:HEAD].reshape(HEAD // 8, 8, -1, 128).transpose(0, 2, 1, 3)
    count = rows // 8 * (D // 128)
    tiles = tiles.reshape(-1, 8, 128)[:count].reshape(rows // 8, D // 128, 8, 128)
    return tiles.transpose(0, 2, 1, 3).reshape(rows, D)


def unpack_kernel(packed, out_ref, down_ref, gu_ref):
    out_rows, down_rows = out_ref.shape[0] // 2, down_ref.shape[0] // 2
    for member in range(2):
        for i in range((out_rows + down_rows) // PACK):
            for j in range(D // 128):
                tile = 128 * (i * (D // 128) + j)
                values = packed[member, 0:PACK, tile : tile + 128]
                if i < out_rows // PACK:
                    row = member * out_rows + i * PACK
                    out_ref[row : row + PACK, 128 * j : 128 * j + 128] = values
                else:
                    row = member * down_rows + i * PACK - out_rows
                    down_ref[row : row + PACK, 128 * j : 128 * j + 128] = values
    for begin in range(0, 2 * FF, 1024):
        at = slice(begin, begin + 1024)
        both = [packed[member, PACK:, at].astype(F32) for member in range(2)]
        gu_ref[:, at] = jnp.concatenate(both, axis=0).astype(BF16)


def unpack_weights(packed):
    rows = packed.shape[1]
    out_rows, down_rows, gu_rows = HQ * HD // MEMBERS, FF // MEMBERS, rows - PACK
    return pl.pallas_call(
        unpack_kernel,
        grid=(MEMBERS // 2,),
        out_shape=(
            jax.ShapeDtypeStruct((HQ * HD, D), BF16),
            jax.ShapeDtypeStruct((FF, D), BF16),
            jax.ShapeDtypeStruct((MEMBERS * gu_rows, 2 * FF), BF16),
        ),
        in_specs=[pl.BlockSpec((2, rows, 2 * FF), lambda i: (i, 0, 0))],
        out_specs=(
            pl.BlockSpec((2 * out_rows, D), lambda i: (i, 0)),
            pl.BlockSpec((2 * down_rows, D), lambda i: (i, 0)),
            pl.BlockSpec((2 * gu_rows, 2 * FF), lambda i: (i, 0)),
        ),
        compiler_params=pltpu.CompilerParams(vmem_limit_bytes=32 * 1024 * 1024),
        cost_estimate=pl.CostEstimate(flops=0, bytes_accessed=19_000_000, transcendentals=0),
        name="unpack_weights",
    )(packed)


def feed_back_kernel(down, hidden, gate_up, ff, w_down, w_gu, db_ref, packed, dgu, sums):
    tile = 512
    root = math.sqrt(2.0 / math.pi)
    for begin in range(0, FF, tile):
        at = slice(begin, begin + tile)
        at_up = slice(FF + begin, FF + begin + tile)
        dh = lax.dot_general(down[...], w_down[at, :], NT, preferred_element_type=F32)
        gate, up = gate_up[:, at], gate_up[:, at_up]
        square = gate * gate
        wave = jnp.tanh(root * gate * (1.0 + 0.044715 * square))
        half = 0.5 * (1.0 + wave)
        slope = half + 0.5 * gate * (1.0 - wave * wave) * (root * (1.0 + 3.0 * 0.044715 * square))
        dgate = (dh * up * slope).astype(BF16)
        dup = (dh * gate * half).astype(BF16)
        dgu[:, at] = dgate
        dgu[:, at_up] = dup
        term = lax.dot_general(dgate, w_gu[:, at], NT, preferred_element_type=F32)
        term += lax.dot_general(dup, w_gu[:, at_up], NT, preferred_element_type=F32)
        if begin:
            db_ref[...] += term
        else:
            db_ref[...] = term
        sums[at, :] = lax.dot_general(hidden[:, at], down[...], TN, preferred_element_type=F32)
    gu_rows = packed.shape[1] - HEAD
    down_rows = FF // MEMBERS
    slabs = 2 * FF // 128
    for begin in range(0, 2 * FF, tile):
        block = lax.dot_general(
            ff[...], dgu[:, begin : begin + tile], TN, preferred_element_type=F32
        )
        for member in range(MEMBERS):
            lanes = []
            for slab in range(begin // 128, (begin + tile) // 128):
                parts = []
                for r in range(HEAD // 8):
                    i, j = divmod(r * slabs + slab, D // 128)
                    if 8 * i < down_rows:
                        row = member * down_rows + 8 * i
                        parts.append(sums[row : row + 8, 128 * j : 128 * j + 128])
                    else:
                        parts.append(jnp.zeros((8, 128), F32))
                lanes.append(jnp.concatenate(parts, axis=0))
            top = jnp.concatenate(lanes, axis=1)
            rows = block[member * gu_rows : (member + 1) * gu_rows]
            packed[member, :, begin : begin + tile] = jnp.concatenate([top, rows], axis=0).astype(
                BF16
            )


def feed_back(down, hidden, gate_up, ff, w_down, w_gu):
    vmem = pl.BlockSpec(memory_space=pltpu.VMEM)
    tokens_here = ff.shape[0]
    return pl.pallas_call(
        feed_back_kernel,
        out_shape=(
            jax.ShapeDtypeStruct((tokens_here, D), F32),
            jax.ShapeDtypeStruct((MEMBERS, HEAD + D // MEMBERS, 2 * FF), BF16),
        ),
        in_specs=[vmem] * 6,
        out_specs=(vmem, vmem),
        scratch_shapes=[pltpu.VMEM((tokens_here, 2 * FF), BF16), pltpu.VMEM((FF, D), F32)],
        compiler_params=pltpu.CompilerParams(vmem_limit_bytes=56 * 1024 * 1024),
        cost_estimate=pl.CostEstimate(
            flops=16 * tokens_here * D * FF, bytes_accessed=32_000_000, transcendentals=1_000_000
        ),
        name="feed_back",
    )(down, hidden, gate_up, ff, w_down, w_gu)


def key_range(info, stream):
    first = info[0]
    bound = info[4 + stream]
    low = jnp.where(first >= bound, bound, 0)
    high = jnp.where(first + SEG - 1 >= bound, bound, 0)
    return first, bound, low, high


def load_blocks(info, blocks, kv, sem):
    z, x, c = info[1], info[2], info[3]
    copies = []
    for place in range(len(blocks)):
        cr, xr, k = place // (2 * REACH), place // REACH % 2, place % REACH
        owner = ((z - k) & 3) * 4 + (x ^ xr) * 2 + (c ^ cr)
        copies.append(pltpu.make_async_copy(blocks[place], kv.at[owner], sem.at[place]))
    for copy in copies:
        copy.start()
    return copies


def forward_kernel(info, q_ref, *refs):
    blocks = refs[:BLOCKS]
    o_ref, lse_ref, kv, acc, total, sem = refs[BLOCKS:]
    copies = load_blocks(info, blocks, kv, sem)
    for copy in copies:
        copy.wait()

    def one_stream(stream, carry):
        mine = pl.ds(pl.multiple_of(stream * SEG, SEG), SEG)
        first, bound, low, high = key_range(info, stream)
        begin = low // KEYS
        diagonal = first // KEYS
        clear = jnp.clip((high + KEYS - 1) // KEYS, begin, diagonal)
        acc[...] = jnp.zeros_like(acc)
        total[...] = jnp.zeros_like(total)

        def visit(j, masked):
            keys = kv[pl.ds(2 * j, 2), stream, :, 0:HD].reshape(KEYS, HD)
            values = kv[pl.ds(2 * j, 2), stream, :, HD : 2 * HD].reshape(KEYS, HD)
            if masked:
                row = first + lax.broadcasted_iota(jnp.int32, (SEG, KEYS), 0)
                col = j * KEYS + lax.broadcasted_iota(jnp.int32, (SEG, KEYS), 1)
                mask = (col <= row) & (col >= jnp.where(row >= bound, bound, 0))
            for head in range(HQ):
                rows = slice(head * SEG, (head + 1) * SEG)
                query = q_ref[mine, head * HD : (head + 1) * HD]
                score = lax.dot_general(query, keys, NT, preferred_element_type=F32)
                prob = jnp.exp2(score * (SCALE_SCORE * LOG2E))
                if masked:
                    prob = jnp.where(mask, prob, 0.0)
                total[rows] += (
                    prob[:, 0:128] + prob[:, 128:256] + prob[:, 256:384] + prob[:, 384:512]
                )
                acc[rows] += jnp.dot(prob.astype(BF16), values, preferred_element_type=F32)

        def masked_step(i, carry):
            visit(jnp.where(i < clear, i, diagonal), True)
            return carry

        def clear_step(j, carry):
            visit(j, False)
            return carry

        lax.fori_loop(begin, clear + 1, masked_step, 0)
        lax.fori_loop(clear, diagonal, clear_step, 0)
        for head in range(HQ):
            rows = slice(head * SEG, (head + 1) * SEG)
            part = total[rows]
            out = acc[rows] / jnp.sum(part, axis=1, keepdims=True)
            o_ref[mine, head * HD : (head + 1) * HD] = out.astype(BF16)
            lse_ref[stream, :, rows] = jnp.log2(jnp.sum(part.T, axis=0, keepdims=True))
        return carry

    lax.fori_loop(0, 2, one_stream, 0)


def attention_forward(info, query, blocks):
    vmem = pl.BlockSpec(memory_space=pltpu.VMEM)
    return pl.pallas_call(
        forward_kernel,
        out_shape=(
            jax.ShapeDtypeStruct((2 * SEG, HQ * HD), BF16),
            jax.ShapeDtypeStruct((2, 1, HQ * SEG), F32),
        ),
        in_specs=[pl.BlockSpec(memory_space=pltpu.SMEM), vmem]
        + [pl.BlockSpec(memory_space=pl.ANY)] * BLOCKS,
        out_specs=(vmem, vmem),
        scratch_shapes=[
            pltpu.VMEM((MEMBERS, 2, SEG, 2 * HD), BF16),
            pltpu.VMEM((HQ * SEG, HD), F32),
            pltpu.VMEM((HQ * SEG, 128), F32),
            pltpu.SemaphoreType.DMA((BLOCKS,)),
        ],
        compiler_params=pltpu.CompilerParams(vmem_limit_bytes=40 * 1024 * 1024),
        cost_estimate=pl.CostEstimate(
            flops=7_000_000_000, bytes_accessed=9_000_000, transcendentals=7_000_000
        ),
        name="attention_forward",
    )(info, query, *blocks)


def backward_kernel(info, q_ref, o_ref, do_ref, lse_ref, *refs):
    blocks = refs[:BLOCKS]
    dq_ref = refs[BLOCKS]
    far = refs[BLOCKS + 1 : BLOCKS + 1 + REACH]
    near_far = refs[BLOCKS + 1 + REACH : BLOCKS + 1 + 2 * REACH]
    near = refs[BLOCKS + 1 + 2 * REACH : BLOCKS + 1 + 3 * REACH]
    kv, dkv, qs, qt, dos, dot_, dqt, delta, sem, out_sem = refs[BLOCKS + 1 + 3 * REACH :]
    copies = load_blocks(info, blocks, kv, sem)
    z, x, c = info[1], info[2], info[3]

    def clean(place, carry):
        dkv[place] = jnp.zeros((2, SEG, 2 * HD), BF16)
        return carry

    lax.fori_loop(0, BLOCKS, clean, 0)
    for copy in copies:
        copy.wait()

    def one_stream(stream, carry):
        first, bound, low, _ = key_range(info, stream)
        mine = pl.ds(pl.multiple_of(stream * SEG, SEG), SEG)
        for head in range(HQ):
            rows = slice(head * SEG, (head + 1) * SEG)
            lanes = slice(head * HD, (head + 1) * HD)
            query = q_ref[mine, lanes]
            grad = do_ref[mine, lanes]
            qs[rows] = query
            dos[rows] = grad
            qt[:, rows] = query.T
            dot_[:, rows] = grad.T
            both = grad.astype(F32) * o_ref[mine, lanes].astype(F32)
            delta[:, rows] = jnp.sum((both[:, 0:128] + both[:, 128:256]).T, axis=0, keepdims=True)
        dqt[...] = jnp.zeros_like(dqt)
        shape = (SEG, HQ * SEG)

        def visit(j, carry):
            keys = kv[j, stream, :, 0:HD]
            values = kv[j, stream, :, HD : 2 * HD]
            score = jnp.dot(keys, qt[...], preferred_element_type=F32)
            prob = jnp.exp2(score * (SCALE_SCORE * LOG2E) - lse_ref[stream])
            row = first + (lax.broadcasted_iota(jnp.int32, (1, HQ * SEG), 1) & (SEG - 1))
            start = jnp.where(row >= bound, bound, 0)
            col = j * SEG + lax.broadcasted_iota(jnp.int32, shape, 0)
            prob = jnp.where((col <= row) & (col >= start), prob, 0.0)
            dprob = jnp.dot(values, dot_[...], preferred_element_type=F32)
            dscore = (prob * (dprob - delta[...])).astype(BF16)
            dv = jnp.dot(prob.astype(BF16), dos[...], preferred_element_type=F32)
            dk = jnp.dot(dscore, qs[...], preferred_element_type=F32)
            dqt[...] += jnp.dot(keys.T, dscore, preferred_element_type=F32)
            place = ((j & 1) ^ c) * (2 * REACH) + (z - (j >> 2)) * 2 + (((j >> 1) & 1) ^ x)
            dkv[place, stream, :, 0:HD] = (dk * SCALE_SCORE).astype(BF16)
            dkv[place, stream, :, HD : 2 * HD] = dv.astype(BF16)
            return carry

        lax.fori_loop(low // SEG, first // SEG + 1, visit, 0)
        for head in range(HQ):
            rows = slice(head * SEG, (head + 1) * SEG)
            dq_ref[mine, head * HD : (head + 1) * HD] = dqt[:, rows].T * SCALE_SCORE
        return carry

    lax.fori_loop(0, 2, one_stream, 0)
    outs = []
    for k in range(REACH):
        outs.append((dkv.at[pl.ds(2 * REACH + 2 * k, 2)], far[k]))
        outs.append((dkv.at[2 * k + 1], near_far[k]))
        outs.append((dkv.at[2 * k], near[k]))
    copies = [
        pltpu.make_async_copy(source, target, out_sem.at[n])
        for n, (source, target) in enumerate(outs)
    ]
    for copy in copies:
        copy.start()
    for copy in copies:
        copy.wait()


def attention_backward(info, query, out, grad_out, lse, blocks):
    one = jax.ShapeDtypeStruct((2, SEG, 2 * HD), BF16)
    two = jax.ShapeDtypeStruct((2, 2, SEG, 2 * HD), BF16)
    vmem = pl.BlockSpec(memory_space=pltpu.VMEM)
    anywhere = pl.BlockSpec(memory_space=pl.ANY)
    result = pl.pallas_call(
        backward_kernel,
        out_shape=[jax.ShapeDtypeStruct((2 * SEG, HQ * HD), F32)]
        + [two] * REACH
        + [one] * (2 * REACH),
        in_specs=[pl.BlockSpec(memory_space=pltpu.SMEM)] + [vmem] * 4 + [anywhere] * BLOCKS,
        out_specs=[vmem] + [anywhere] * (3 * REACH),
        scratch_shapes=[
            pltpu.VMEM((MEMBERS, 2, SEG, 2 * HD), BF16),
            pltpu.VMEM((BLOCKS, 2, SEG, 2 * HD), BF16),
            pltpu.VMEM((HQ * SEG, HD), BF16),
            pltpu.VMEM((HD, HQ * SEG), BF16),
            pltpu.VMEM((HQ * SEG, HD), BF16),
            pltpu.VMEM((HD, HQ * SEG), BF16),
            pltpu.VMEM((HD, HQ * SEG), F32),
            pltpu.VMEM((1, HQ * SEG), F32),
            pltpu.SemaphoreType.DMA((BLOCKS,)),
            pltpu.SemaphoreType.DMA((3 * REACH,)),
        ],
        compiler_params=pltpu.CompilerParams(vmem_limit_bytes=52 * 1024 * 1024),
        cost_estimate=pl.CostEstimate(
            flops=17_000_000_000, bytes_accessed=20_000_000, transcendentals=7_000_000
        ),
        name="attention_backward",
    )(info, query, out, grad_out, lse, *blocks)
    return result[0], result[1 : 1 + REACH], result[1 + REACH : 1 + 2 * REACH], result[1 + 2 * REACH :]


def per_device(
    tokens,
    cotangent,
    lengths,
    w_qkv,
    w_out,
    w_gu,
    w_down,
    norm_gains,
    first_qkv,
    first_out,
    first_gu,
    first_down,
    first_gains,
    second_qkv,
    second_out,
    second_gu,
    second_down,
    second_gains,
):
    streams = tokens.shape[0]
    row_count = streams * SEG
    member_index = lax.axis_index("group")
    tok_rows = tokens.reshape(row_count, D).astype(F32)
    grad_out = cotangent.reshape(row_count, D).astype(F32)
    start_row = member_index * SEG
    boundary = lengths[:, 0]
    info = jnp.concatenate(
        [
            jnp.stack([start_row, member_index // 4, member_index // 2 % 2, member_index % 2]),
            boundary,
        ]
    ).astype(jnp.int32)
    q_width = HQ * HD
    low_qkv = w_qkv.astype(BF16)
    gain_count = norm_gains.shape[0]
    gain_row = jnp.pad(norm_gains.astype(BF16), (0, 2 * HD - gain_count))
    full_kv, gain_rows = order_rows(
        info,
        gather_all(jnp.concatenate([low_qkv[:, q_width:], gain_row[None]], axis=0)),
        "order_kv",
    )
    full_gains = gain_rows[:, :gain_count].reshape(-1)
    gain_in, gain_pa, gain_pf, gain_po, gain_query, gain_key = split_gains(full_gains)
    out_rows = w_out.shape[0]
    down_rows = w_down.shape[0]
    full_out, full_down, full_gu = unpack_weights(
        lax.all_gather(
            pack_shards(w_out.astype(BF16), w_down.astype(BF16), w_gu.astype(BF16)),
            "group",
            axis=0,
            tiled=False,
        )
    )
    index_mine = start_row + jnp.arange(SEG, dtype=jnp.int32)
    position_mine = index_mine[None, :] - jnp.where(
        index_mine[None, :] >= boundary[:, None], boundary[:, None], 0
    )
    cosine, sine = angles(position_mine.reshape(row_count), HD)
    normed_in, pull_in = jax.vjp(rms_norm, tok_rows, gain_in)
    input_low = normed_in.astype(BF16)
    kv_rows = jnp.dot(input_low, full_kv, preferred_element_type=F32)
    key_rot, pull_key = jax.vjp(
        lambda rows, gain: head_in(rows, gain, cosine, sine), kv_rows[:, :HD], gain_key
    )
    kv_low = jnp.concatenate([key_rot.astype(BF16), kv_rows[:, HD:].astype(BF16)], axis=1)
    blocks, low_q = gather_keys(kv_low.reshape(streams, SEG, 2 * HD), low_qkv[:, :q_width])
    (full_q,) = order_rows(info, gather_all(low_q), "order_q")
    query_rows = jnp.dot(input_low, full_q, preferred_element_type=F32)
    query_rot, pull_query = [], []
    for head in range(HQ):
        rotated, pull = jax.vjp(
            lambda rows, gain: head_in(rows, gain, cosine, sine),
            query_rows[:, head * HD : (head + 1) * HD],
            gain_query,
        )
        query_rot.append(rotated.astype(BF16))
        pull_query.append(pull)
    query_low = jnp.concatenate(query_rot, axis=1)
    attn_low, lse = attention_forward(info, query_low, blocks)
    attn_proj = jnp.dot(attn_low, full_out, preferred_element_type=F32)
    post_attn, pull_attn = jax.vjp(rms_norm, attn_proj, gain_pa)
    middle = tok_rows + post_attn
    normed_ff, pull_ff = jax.vjp(rms_norm, middle, gain_pf)
    ff_low = normed_ff.astype(BF16)
    gate_up = jnp.dot(ff_low, full_gu, preferred_element_type=F32)
    hidden = geglu(gate_up)
    hidden_low = hidden.astype(BF16)
    down_proj = jnp.dot(hidden_low, full_down, preferred_element_type=F32)
    post_ff, pull_post = jax.vjp(rms_norm, down_proj, gain_po)
    layer_out = (middle + post_ff).astype(BF16).reshape(streams, SEG, D)
    grad_down, grad_gain_po = pull_post(grad_out)
    down_low = grad_down.astype(BF16)
    grad_normed_ff, packed = feed_back(down_low, hidden_low, gate_up, ff_low, full_down, full_gu)
    mine = lax.psum_scatter(packed, "group", scatter_dimension=0, tiled=False)
    grad_middle_ff, grad_gain_pf = pull_ff(grad_normed_ff)
    grad_middle = grad_out + grad_middle_ff
    grad_attn_proj, grad_gain_pa = pull_attn(grad_middle)
    proj_low = grad_attn_proj.astype(BF16)
    grad_attn_low = jnp.dot(proj_low, full_out.T, preferred_element_type=F32).astype(BF16)
    near_out, far_out = weight_gradient(info, [(attn_low, proj_low)], None, 640, "gradient_out")
    grad_attn_low, near_out = lax.optimization_barrier((grad_attn_low, near_out))
    came_out = swap_core(far_out)
    over_out = scatter_x(near_out, came_out)
    grad_query, far, near_far, near = attention_backward(
        info, query_low, attn_low, grad_attn_low, lse, blocks
    )
    grad_kv = scatter_keys(far, near_far, near).reshape(row_count, 2 * HD)
    grad_query_rows, grad_gain_q = [], 0.0
    for head in range(HQ):
        rows, gain = pull_query[head](grad_query[:, head * HD : (head + 1) * HD])
        grad_query_rows.append(rows.astype(BF16))
        grad_gain_q = grad_gain_q + gain
    query_grad_low = jnp.concatenate(grad_query_rows, axis=1)
    near_q, far_q = weight_gradient(
        info, [(input_low, query_grad_low)], None, 512, "gradient_q"
    )
    came_q = swap_core(far_q)
    over_q = scatter_x(near_q, came_q)
    grad_kv, over_q, over_out, mine = lax.optimization_barrier((grad_kv, over_q, over_out, mine))
    sum_out = over_replicas(scatter_z(near_out, came_out, over_out))
    sum_q = over_replicas(scatter_z(near_q, came_q, over_q))
    grad_key_rows, grad_gain_k = pull_key(grad_kv[:, :HD])
    kv_grad_low = jnp.concatenate(
        [grad_key_rows.astype(BF16), grad_kv[:, HD:].astype(BF16)], axis=1
    )
    grad_normed_in = jnp.dot(query_grad_low, full_q.T, preferred_element_type=F32) + jnp.dot(
        kv_grad_low, full_kv.T, preferred_element_type=F32
    )
    grad_tokens_in, grad_gain_in = pull_in(grad_normed_in)
    token_grad = (grad_middle + grad_tokens_in).reshape(streams, SEG, D)
    wgrad_gains = jnp.concatenate(
        [grad_gain_in, grad_gain_pa, grad_gain_pf, grad_gain_po, grad_gain_q, grad_gain_k]
    )
    gains_out = jnp.pad(
        wgrad_gains.reshape(MEMBERS, gain_count), ((0, 0), (0, 2 * HD - gain_count))
    )
    near_kv, far_kv = weight_gradient(
        info, [(input_low, kv_grad_low)], gains_out, 2 * HD, "gradient_kv"
    )
    came_kv = swap_core(far_kv)
    sum_kv = over_replicas(scatter_z(near_kv, came_kv, scatter_x(near_kv, came_kv)))
    shard_qkv = jnp.concatenate([sum_q, sum_kv[:-8]], axis=1)
    shard_gains = sum_kv[-1, :gain_count]
    sum_packed = over_replicas(mine)
    sum_gu = sum_packed[HEAD:]
    sum_down = unpack_down(sum_packed, down_rows)
    upd_qkv = adam_step(w_qkv, first_qkv, second_qkv, shard_qkv, RATE_MATRIX, DECAY_RATE)
    upd_out = adam_step(w_out, first_out, second_out, sum_out, RATE_MATRIX, DECAY_RATE)
    upd_gu = adam_step(w_gu, first_gu, second_gu, sum_gu, RATE_MATRIX, DECAY_RATE)
    upd_down = adam_step(w_down, first_down, second_down, sum_down, RATE_MATRIX, DECAY_RATE)
    upd_gains = adam_step(norm_gains, first_gains, second_gains, shard_gains, RATE_GAIN, 0.0)
    return (layer_out, token_grad, *upd_qkv, *upd_out, *upd_gu, *upd_down, *upd_gains)


def solution(mesh):
    in_specs = (
        P("replica", "group", None),
        P("replica", "group", None),
        P("replica", None),
        P("group", None),
        P("group", None),
        P("group", None),
        P("group", None),
        P("group"),
        P("group", None),
        P("group", None),
        P("group", None),
        P("group", None),
        P("group"),
        P("group", None),
        P("group", None),
        P("group", None),
        P("group", None),
        P("group"),
    )
    out_specs = (
        P("replica", "group", None),
        P("replica", "group", None),
        P("group", None),
        P("group", None),
        P("group", None),
        P("group", None),
        P("group", None),
        P("group", None),
        P("group", None),
        P("group", None),
        P("group", None),
        P("group", None),
        P("group", None),
        P("group", None),
        P("group"),
        P("group"),
        P("group"),
    )
    return jax.shard_map(
        per_device, mesh=mesh, in_specs=in_specs, out_specs=out_specs, check_vma=False
    )
```

```python
import math

import jax
import jax.numpy as jnp
from jax import lax
from jax.experimental import pallas as pl
from jax.experimental.pallas import tpu as pltpu
from jax.sharding import PartitionSpec as P

D = 640
HQ = 4
HD = 256
FF = 2048
SEG = 256
STEP = 10


EPS_NORM = 1e-06
BETA_ONE = 0.9
BETA_TWO = 0.999
ADAM_EPS = 1e-08
RATE_MATRIX = 0.1
RATE_GAIN = 0.5
DECAY_RATE = 0.1
ROPE_BASE = 1000000.0
NEGATIVE = -1e30
SCALE_SCORE = 0.0625


def rms_norm(values, gain_row):
    factor = lax.rsqrt(jnp.mean(values * values, axis=-1, keepdims=True) + EPS_NORM)
    return values * factor * gain_row


def angles(position, width):
    half_width = width // 2
    frequency = jnp.exp(
        jnp.arange(half_width, dtype=jnp.float32) * (-2.0 * math.log(ROPE_BASE) / width)
    )
    angle_table = position.astype(jnp.float32)[:, None] * frequency[None, :]
    return (jnp.cos(angle_table), jnp.sin(angle_table))


def rotate(values, cosine, sine):
    half_width = values.shape[-1] // 2
    leading = values[..., :half_width]
    trailing = values[..., half_width:]
    return jnp.concatenate(
        [leading * cosine - trailing * sine, trailing * cosine + leading * sine], axis=-1
    )


def layout(lengths, total):
    seq_ends = jnp.cumsum(lengths)
    seq_starts = seq_ends - lengths
    stream_index = jnp.arange(total, dtype=jnp.int32)
    segment = jnp.sum((stream_index[:, None] >= seq_ends[None, :]).astype(jnp.int32), axis=1)
    seq_begin = jnp.max(
        jnp.where(stream_index[:, None] >= seq_starts[None, :], seq_starts[None, :], 0), axis=1
    )
    return (segment, stream_index - seq_begin)


def head_in(values, gain_row, cosine, sine):
    return rotate(rms_norm(values, gain_row), cosine, sine)


def geglu(gate_up):
    return jax.nn.gelu(gate_up[:, :FF], approximate=True) * gate_up[:, FF:]


def split_gains(gain_all):
    return (
        gain_all[0:D],
        gain_all[D : 2 * D],
        gain_all[2 * D : 3 * D],
        gain_all[3 * D : 4 * D],
        gain_all[4 * D : 4 * D + HD],
        gain_all[4 * D + HD : 4 * D + 2 * HD],
    )


def adam_step(master, moment_one, moment_two, gradient, rate, decay):
    moment_new = BETA_ONE * moment_one + (1.0 - BETA_ONE) * gradient
    square_new = BETA_TWO * moment_two + (1.0 - BETA_TWO) * gradient * gradient
    moment_hat = moment_new / (1.0 - BETA_ONE**STEP)
    square_hat = square_new / (1.0 - BETA_TWO**STEP)
    master_new = master * (1.0 - rate * decay) - rate * moment_hat / (
        jnp.sqrt(square_hat) + ADAM_EPS
    )
    return (moment_new, square_new, master_new)


LOG2E = 1.4426950408889634
KEYS = 512
MEMBERS = 16
PACK = 32
HEAD = 24
REACH = 3
BLOCKS = 4 * REACH
NT = (((1,), (1,)), ((), ()))
TN = (((0,), (0,)), ((), ()))
F32 = jnp.float32
BF16 = jnp.bfloat16


def shift_z(values, k):
    return lax.ppermute(values, "group", [(i, (i + 4 * k) % MEMBERS) for i in range(MEMBERS)])


def line_up(values, lowest):
    return lax.ppermute(values, "group", [(i, i + 4) for i in range(4 * lowest, MEMBERS - 4)])


def line_down(values, lowest):
    return lax.ppermute(values, "group", [(i, i - 4) for i in range(4 * lowest, MEMBERS)])


def swap_x(values):
    return lax.ppermute(values, "group", [(i, i ^ 2) for i in range(MEMBERS)])


def swap_core(values):
    return lax.ppermute(values, "group", [(i, i ^ 1) for i in range(MEMBERS)])


def spread(lines):
    near = lines + [swap_x(line) for line in lines]
    return near + [swap_core(block) for block in near]


def gather_all(own):
    return spread([own] + [shift_z(own, k) for k in (1, 2, 3)])


def gather_keys(own, later):
    first = line_up(own, 0)
    second, over, over_first, later = lax.optimization_barrier(
        (line_up(first, 1), swap_x(own), swap_x(first), later)
    )
    near = [own, first, second, over, over_first, swap_x(second)]
    return near + [swap_core(block) for block in near], later


def scatter_keys(far, near_far, near):
    running = None
    for k in range(REACH - 1, -1, -1):
        came = swap_core(far[k]).astype(F32)
        over = swap_x((near_far[k].astype(F32) + came[1]).astype(BF16))
        total = near[k].astype(F32) + came[0] + over.astype(F32)
        if running is not None:
            total = total + running.astype(F32)
        if k:
            running = line_down(total.astype(BF16), k)
    return total


def scatter_x(near, came):
    return swap_x((near[4:].astype(F32) + came[4:].astype(F32)).astype(BF16))


def scatter_z(near, came, over):
    total = [near[k].astype(F32) + came[k].astype(F32) + over[k].astype(F32) for k in range(4)]
    for k in (1, 2, 3):
        total[0] = total[0] + shift_z(total[k].astype(BF16), k).astype(F32)
    return total[0].astype(BF16)


def over_replicas(shard):
    if lax.axis_size("replica") == 2:
        other = lax.ppermute(shard, "replica", [(0, 1), (1, 0)])
        return shard.astype(F32) + other.astype(F32)
    return lax.psum(shard, "replica").astype(F32)


def owner_up(info, place):
    cr, xr, k = place // 8, place // 4 % 2, place % 4
    return ((info[1] + k) & 3) * 4 + (info[2] ^ xr) * 2 + (info[3] ^ cr)


def order_kernel(info, *refs):
    blocks = refs[:MEMBERS]
    full_ref, rows = refs[MEMBERS], refs[-1]
    count = rows.shape[0] // MEMBERS
    for place in range(MEMBERS):
        cr, xr, k = place // 8, place // 4 % 2, place % 4
        owner = ((info[1] - k) & 3) * 4 + (info[2] ^ xr) * 2 + (info[3] ^ cr)
        values = blocks[place][...].astype(F32)
        rows[pl.ds(pl.multiple_of(owner * count, 8), count)] = values[:count]
        if len(refs) > MEMBERS + 2:
            refs[MEMBERS + 1][pl.ds(owner, 1)] = values[count : count + 1]
    full_ref[...] = rows[...].astype(BF16)


def order_rows(info, blocks, name):
    rows, columns = blocks[0].shape
    count = rows // 8 * 8
    vmem = pl.BlockSpec(memory_space=pltpu.VMEM)
    shapes = [jax.ShapeDtypeStruct((MEMBERS * count, columns), BF16)]
    if rows > count:
        shapes.append(jax.ShapeDtypeStruct((MEMBERS, columns), F32))
    return pl.pallas_call(
        order_kernel,
        out_shape=shapes,
        in_specs=[pl.BlockSpec(memory_space=pltpu.SMEM)] + [vmem] * MEMBERS,
        out_specs=[vmem] * len(shapes),
        scratch_shapes=[pltpu.VMEM((MEMBERS * count, columns), F32)],
        compiler_params=pltpu.CompilerParams(vmem_limit_bytes=32 * 1024 * 1024),
        cost_estimate=pl.CostEstimate(flops=0, bytes_accessed=4_000_000, transcendentals=0),
        name=name,
    )(info, *blocks)


def gradient_kernel(tile, pairs, extra, info, *refs):
    operands = refs[: 2 * pairs + extra]
    near, far = refs[2 * pairs + extra : 2 * pairs + extra + 2]
    sums = refs[2 * pairs + extra + 2 :]
    columns = near.shape[2]
    for begin in range(0, columns, tile):
        at = slice(begin, begin + tile)
        for pair in range(pairs):
            left, right = operands[2 * pair], operands[2 * pair + 1]
            sums[pair][...] = lax.dot_general(
                left[...], right[:, at], TN, preferred_element_type=F32
            )
        for place in range(MEMBERS):
            owner = owner_up(info, place)
            parts = []
            for pair in range(pairs):
                count = sums[pair].shape[0] // MEMBERS
                parts.append(sums[pair][pl.ds(pl.multiple_of(owner * count, 8), count)])
            if extra:
                row = operands[2 * pairs][pl.ds(owner, 1), at]
                parts.append(jnp.broadcast_to(row, (8, tile)))
            block = jnp.concatenate(parts, axis=0) if len(parts) > 1 else parts[0]
            target = far if place >= 8 else near
            target[place % 8, :, at] = block.astype(BF16)


def weight_gradient(info, pairs, gains, tile, name):
    columns = pairs[0][1].shape[1]
    tokens_here = pairs[0][0].shape[0]
    counts = [left.shape[1] // MEMBERS for left, _ in pairs]
    rows = sum(counts) + (8 if gains is not None else 0)
    operands = [operand for pair in pairs for operand in pair]
    if gains is not None:
        operands.append(gains)
    shape = jax.ShapeDtypeStruct((MEMBERS // 2, rows, columns), BF16)
    vmem = pl.BlockSpec(memory_space=pltpu.VMEM)
    return pl.pallas_call(
        lambda *refs: gradient_kernel(tile, len(pairs), int(gains is not None), *refs),
        out_shape=(shape, shape),
        in_specs=[pl.BlockSpec(memory_space=pltpu.SMEM)] + [vmem] * len(operands),
        out_specs=(vmem, vmem),
        scratch_shapes=[pltpu.VMEM((MEMBERS * count, tile), F32) for count in counts],
        compiler_params=pltpu.CompilerParams(vmem_limit_bytes=48 * 1024 * 1024),
        cost_estimate=pl.CostEstimate(
            flops=2 * tokens_here * columns * MEMBERS * sum(counts),
            bytes_accessed=4 * MEMBERS * rows * columns,
            transcendentals=0,
        ),
        name=name,
    )(info, *operands)


def pack_shards(out_shard, down_shard, gu_shard):
    mixed = jnp.concatenate([out_shard, down_shard], axis=0)
    rows, columns = mixed.shape
    tiles = mixed.reshape(rows // PACK, PACK, columns // 128, 128).transpose(1, 0, 2, 3)
    flat = tiles.reshape(PACK, -1)
    flat = jnp.pad(flat, ((0, 0), (0, gu_shard.shape[1] - flat.shape[1])))
    return jnp.concatenate([flat, gu_shard], axis=0)


def unpack_down(packed, rows):
    tiles = packed[:HEAD].reshape(HEAD // 8, 8, -1, 128).transpose(0, 2, 1, 3)
    count = rows // 8 * (D // 128)
    tiles = tiles.reshape(-1, 8, 128)[:count].reshape(rows // 8, D // 128, 8, 128)
    return tiles.transpose(0, 2, 1, 3).reshape(rows, D)


def unpack_kernel(packed, out_ref, down_ref, gu_ref):
    out_rows, down_rows = out_ref.shape[0] // 2, down_ref.shape[0] // 2
    for member in range(2):
        for i in range((out_rows + down_rows) // PACK):
            for j in range(D // 128):
                tile = 128 * (i * (D // 128) + j)
                values = packed[member, 0:PACK, tile : tile + 128]
                if i < out_rows // PACK:
                    row = member * out_rows + i * PACK
                    out_ref[row : row + PACK, 128 * j : 128 * j + 128] = values
                else:
                    row = member * down_rows + i * PACK - out_rows
                    down_ref[row : row + PACK, 128 * j : 128 * j + 128] = values
    for begin in range(0, 2 * FF, 1024):
        at = slice(begin, begin + 1024)
        both = [packed[member, PACK:, at].astype(F32) for member in range(2)]
        gu_ref[:, at] = jnp.concatenate(both, axis=0).astype(BF16)


def unpack_weights(packed):
    rows = packed.shape[1]
    out_rows, down_rows, gu_rows = HQ * HD // MEMBERS, FF // MEMBERS, rows - PACK
    return pl.pallas_call(
        unpack_kernel,
        grid=(MEMBERS // 2,),
        out_shape=(
            jax.ShapeDtypeStruct((HQ * HD, D), BF16),
            jax.ShapeDtypeStruct((FF, D), BF16),
            jax.ShapeDtypeStruct((MEMBERS * gu_rows, 2 * FF), BF16),
        ),
        in_specs=[pl.BlockSpec((2, rows, 2 * FF), lambda i: (i, 0, 0))],
        out_specs=(
            pl.BlockSpec((2 * out_rows, D), lambda i: (i, 0)),
            pl.BlockSpec((2 * down_rows, D), lambda i: (i, 0)),
            pl.BlockSpec((2 * gu_rows, 2 * FF), lambda i: (i, 0)),
        ),
        compiler_params=pltpu.CompilerParams(vmem_limit_bytes=32 * 1024 * 1024),
        cost_estimate=pl.CostEstimate(flops=0, bytes_accessed=19_000_000, transcendentals=0),
        name="unpack_weights",
    )(packed)


def feed_back_kernel(down, hidden, gate_up, ff, w_down, w_gu, db_ref, packed, dgu, sums):
    tile = 512
    root = math.sqrt(2.0 / math.pi)
    for begin in range(0, FF, tile):
        at = slice(begin, begin + tile)
        at_up = slice(FF + begin, FF + begin + tile)
        dh = lax.dot_general(down[...], w_down[at, :], NT, preferred_element_type=F32)
        gate, up = gate_up[:, at], gate_up[:, at_up]
        square = gate * gate
        wave = jnp.tanh(root * gate * (1.0 + 0.044715 * square))
        half = 0.5 * (1.0 + wave)
        slope = half + 0.5 * gate * (1.0 - wave * wave) * (root * (1.0 + 3.0 * 0.044715 * square))
        dgate = (dh * up * slope).astype(BF16)
        dup = (dh * gate * half).astype(BF16)
        dgu[:, at] = dgate
        dgu[:, at_up] = dup
        term = lax.dot_general(dgate, w_gu[:, at], NT, preferred_element_type=F32)
        term += lax.dot_general(dup, w_gu[:, at_up], NT, preferred_element_type=F32)
        if begin:
            db_ref[...] += term
        else:
            db_ref[...] = term
        sums[at, :] = lax.dot_general(hidden[:, at], down[...], TN, preferred_element_type=F32)
    gu_rows = packed.shape[1] - HEAD
    down_rows = FF // MEMBERS
    slabs = 2 * FF // 128
    for begin in range(0, 2 * FF, tile):
        block = lax.dot_general(
            ff[...], dgu[:, begin : begin + tile], TN, preferred_element_type=F32
        )
        for member in range(MEMBERS):
            lanes = []
            for slab in range(begin // 128, (begin + tile) // 128):
                parts = []
                for r in range(HEAD // 8):
                    i, j = divmod(r * slabs + slab, D // 128)
                    if 8 * i < down_rows:
                        row = member * down_rows + 8 * i
                        parts.append(sums[row : row + 8, 128 * j : 128 * j + 128])
                    else:
                        parts.append(jnp.zeros((8, 128), F32))
                lanes.append(jnp.concatenate(parts, axis=0))
            top = jnp.concatenate(lanes, axis=1)
            rows = block[member * gu_rows : (member + 1) * gu_rows]
            packed[member, :, begin : begin + tile] = jnp.concatenate([top, rows], axis=0).astype(
                BF16
            )


def feed_back(down, hidden, gate_up, ff, w_down, w_gu):
    vmem = pl.BlockSpec(memory_space=pltpu.VMEM)
    tokens_here = ff.shape[0]
    return pl.pallas_call(
        feed_back_kernel,
        out_shape=(
            jax.ShapeDtypeStruct((tokens_here, D), F32),
            jax.ShapeDtypeStruct((MEMBERS, HEAD + D // MEMBERS, 2 * FF), BF16),
        ),
        in_specs=[vmem] * 6,
        out_specs=(vmem, vmem),
        scratch_shapes=[pltpu.VMEM((tokens_here, 2 * FF), BF16), pltpu.VMEM((FF, D), F32)],
        compiler_params=pltpu.CompilerParams(vmem_limit_bytes=56 * 1024 * 1024),
        cost_estimate=pl.CostEstimate(
            flops=16 * tokens_here * D * FF, bytes_accessed=32_000_000, transcendentals=1_000_000
        ),
        name="feed_back",
    )(down, hidden, gate_up, ff, w_down, w_gu)


def key_range(info, stream):
    first = info[0]
    bound = info[4 + stream]
    low = jnp.where(first >= bound, bound, 0)
    high = jnp.where(first + SEG - 1 >= bound, bound, 0)
    return first, bound, low, high


def load_blocks(info, blocks, kv, sem):
    z, x, c = info[1], info[2], info[3]
    copies = []
    for place in range(len(blocks)):
        cr, xr, k = place // (2 * REACH), place // REACH % 2, place % REACH
        owner = ((z - k) & 3) * 4 + (x ^ xr) * 2 + (c ^ cr)
        copies.append(pltpu.make_async_copy(blocks[place], kv.at[owner], sem.at[place]))
    for copy in copies:
        copy.start()
    return copies


def forward_kernel(info, q_ref, *refs):
    blocks = refs[:BLOCKS]
    o_ref, lse_ref, kv, acc, total, sem = refs[BLOCKS:]
    copies = load_blocks(info, blocks, kv, sem)
    for copy in copies:
        copy.wait()

    def one_stream(stream, carry):
        mine = pl.ds(pl.multiple_of(stream * SEG, SEG), SEG)
        first, bound, low, high = key_range(info, stream)
        begin = low // KEYS
        diagonal = first // KEYS
        clear = jnp.clip((high + KEYS - 1) // KEYS, begin, diagonal)
        acc[...] = jnp.zeros_like(acc)
        total[...] = jnp.zeros_like(total)

        def visit(j, masked):
            keys = kv[pl.ds(2 * j, 2), stream, :, 0:HD].reshape(KEYS, HD)
            values = kv[pl.ds(2 * j, 2), stream, :, HD : 2 * HD].reshape(KEYS, HD)
            if masked:
                row = first + lax.broadcasted_iota(jnp.int32, (SEG, KEYS), 0)
                col = j * KEYS + lax.broadcasted_iota(jnp.int32, (SEG, KEYS), 1)
                mask = (col <= row) & (col >= jnp.where(row >= bound, bound, 0))
            for head in range(HQ):
                rows = slice(head * SEG, (head + 1) * SEG)
                query = q_ref[mine, head * HD : (head + 1) * HD]
                score = lax.dot_general(query, keys, NT, preferred_element_type=F32)
                prob = jnp.exp2(score * (SCALE_SCORE * LOG2E))
                if masked:
                    prob = jnp.where(mask, prob, 0.0)
                total[rows] += (
                    prob[:, 0:128] + prob[:, 128:256] + prob[:, 256:384] + prob[:, 384:512]
                )
                acc[rows] += jnp.dot(prob.astype(BF16), values, preferred_element_type=F32)

        def masked_step(i, carry):
            visit(jnp.where(i < clear, i, diagonal), True)
            return carry

        def clear_step(j, carry):
            visit(j, False)
            return carry

        lax.fori_loop(begin, clear + 1, masked_step, 0)
        lax.fori_loop(clear, diagonal, clear_step, 0)
        for head in range(HQ):
            rows = slice(head * SEG, (head + 1) * SEG)
            part = total[rows]
            out = acc[rows] / jnp.sum(part, axis=1, keepdims=True)
            o_ref[mine, head * HD : (head + 1) * HD] = out.astype(BF16)
            lse_ref[stream, :, rows] = jnp.log2(jnp.sum(part.T, axis=0, keepdims=True))
        return carry

    lax.fori_loop(0, 2, one_stream, 0)


def attention_forward(info, query, blocks):
    vmem = pl.BlockSpec(memory_space=pltpu.VMEM)
    return pl.pallas_call(
        forward_kernel,
        out_shape=(
            jax.ShapeDtypeStruct((2 * SEG, HQ * HD), BF16),
            jax.ShapeDtypeStruct((2, 1, HQ * SEG), F32),
        ),
        in_specs=[pl.BlockSpec(memory_space=pltpu.SMEM), vmem]
        + [pl.BlockSpec(memory_space=pl.ANY)] * BLOCKS,
        out_specs=(vmem, vmem),
        scratch_shapes=[
            pltpu.VMEM((MEMBERS, 2, SEG, 2 * HD), BF16),
            pltpu.VMEM((HQ * SEG, HD), F32),
            pltpu.VMEM((HQ * SEG, 128), F32),
            pltpu.SemaphoreType.DMA((BLOCKS,)),
        ],
        compiler_params=pltpu.CompilerParams(vmem_limit_bytes=40 * 1024 * 1024),
        cost_estimate=pl.CostEstimate(
            flops=7_000_000_000, bytes_accessed=9_000_000, transcendentals=7_000_000
        ),
        name="attention_forward",
    )(info, query, *blocks)


def backward_kernel(info, q_ref, o_ref, do_ref, lse_ref, *refs):
    blocks = refs[:BLOCKS]
    dq_ref = refs[BLOCKS]
    far = refs[BLOCKS + 1 : BLOCKS + 1 + REACH]
    near_far = refs[BLOCKS + 1 + REACH : BLOCKS + 1 + 2 * REACH]
    near = refs[BLOCKS + 1 + 2 * REACH : BLOCKS + 1 + 3 * REACH]
    kv, dkv, qs, qt, dos, dot_, dqt, delta, sem, out_sem = refs[BLOCKS + 1 + 3 * REACH :]
    copies = load_blocks(info, blocks, kv, sem)
    z, x, c = info[1], info[2], info[3]

    def clean(place, carry):
        dkv[place] = jnp.zeros((2, SEG, 2 * HD), BF16)
        return carry

    lax.fori_loop(0, BLOCKS, clean, 0)
    for copy in copies:
        copy.wait()

    def one_stream(stream, carry):
        first, bound, low, high = key_range(info, stream)
        mine = pl.ds(pl.multiple_of(stream * SEG, SEG), SEG)
        for head in range(HQ):
            rows = slice(head * SEG, (head + 1) * SEG)
            lanes = slice(head * HD, (head + 1) * HD)
            query = q_ref[mine, lanes]
            grad = do_ref[mine, lanes]
            qs[rows] = query
            dos[rows] = grad
            qt[:, rows] = query.T
            dot_[:, rows] = grad.T
            both = grad.astype(F32) * o_ref[mine, lanes].astype(F32)
            delta[:, rows] = jnp.sum((both[:, 0:128] + both[:, 128:256]).T, axis=0, keepdims=True)
        dqt[...] = jnp.zeros_like(dqt)

        def visit(j, masked):
            keys = kv[j, stream, :, 0:HD]
            values = kv[j, stream, :, HD : 2 * HD]
            width = HQ * SEG // 2
            if masked:
                row = first + (lax.broadcasted_iota(jnp.int32, (1, width), 1) & (SEG - 1))
                start = jnp.where(row >= bound, bound, 0)
                col = j * SEG + lax.broadcasted_iota(jnp.int32, (SEG, width), 0)
                mask = (col <= row) & (col >= start)
            keys_turned = keys.T
            dks, dvs = [], []
            for part in range(2):
                at = slice(part * width, (part + 1) * width)
                score = jnp.dot(keys, qt[:, at], preferred_element_type=F32)
                dprob = jnp.dot(values, dot_[:, at], preferred_element_type=F32)
                prob = jnp.exp2(score * (SCALE_SCORE * LOG2E) - lse_ref[stream, :, at])
                if masked:
                    prob = jnp.where(mask, prob, 0.0)
                dscore = (prob * (dprob - delta[:, at])).astype(BF16)
                dvs.append(jnp.dot(prob.astype(BF16), dos[at], preferred_element_type=F32))
                dks.append(jnp.dot(dscore, qs[at], preferred_element_type=F32))
                dqt[:, at] += jnp.dot(keys_turned, dscore, preferred_element_type=F32)
            place = ((j & 1) ^ c) * (2 * REACH) + (z - (j >> 2)) * 2 + (((j >> 1) & 1) ^ x)
            dkv[place, stream, :, 0:HD] = ((dks[0] + dks[1]) * SCALE_SCORE).astype(BF16)
            dkv[place, stream, :, HD : 2 * HD] = (dvs[0] + dvs[1]).astype(BF16)

        begin = low // SEG
        diagonal = first // SEG
        clear = jnp.clip((high + SEG - 1) // SEG, begin, diagonal)

        def masked_step(i, carry):
            visit(jnp.where(i < clear, i, diagonal), True)
            return carry

        def clear_step(j, carry):
            visit(j, False)
            return carry

        lax.fori_loop(begin, clear + 1, masked_step, 0)
        lax.fori_loop(clear, diagonal, clear_step, 0)
        for head in range(HQ):
            rows = slice(head * SEG, (head + 1) * SEG)
            dq_ref[mine, head * HD : (head + 1) * HD] = dqt[:, rows].T * SCALE_SCORE
        return carry

    lax.fori_loop(0, 2, one_stream, 0)
    outs = []
    for k in range(REACH):
        outs.append((dkv.at[pl.ds(2 * REACH + 2 * k, 2)], far[k]))
        outs.append((dkv.at[2 * k + 1], near_far[k]))
        outs.append((dkv.at[2 * k], near[k]))
    copies = [
        pltpu.make_async_copy(source, target, out_sem.at[n])
        for n, (source, target) in enumerate(outs)
    ]
    for copy in copies:
        copy.start()
    for copy in copies:
        copy.wait()


def attention_backward(info, query, out, grad_out, lse, blocks):
    one = jax.ShapeDtypeStruct((2, SEG, 2 * HD), BF16)
    two = jax.ShapeDtypeStruct((2, 2, SEG, 2 * HD), BF16)
    vmem = pl.BlockSpec(memory_space=pltpu.VMEM)
    anywhere = pl.BlockSpec(memory_space=pl.ANY)
    result = pl.pallas_call(
        backward_kernel,
        out_shape=[jax.ShapeDtypeStruct((2 * SEG, HQ * HD), F32)]
        + [two] * REACH
        + [one] * (2 * REACH),
        in_specs=[pl.BlockSpec(memory_space=pltpu.SMEM)] + [vmem] * 4 + [anywhere] * BLOCKS,
        out_specs=[vmem] + [anywhere] * (3 * REACH),
        scratch_shapes=[
            pltpu.VMEM((MEMBERS, 2, SEG, 2 * HD), BF16),
            pltpu.VMEM((BLOCKS, 2, SEG, 2 * HD), BF16),
            pltpu.VMEM((HQ * SEG, HD), BF16),
            pltpu.VMEM((HD, HQ * SEG), BF16),
            pltpu.VMEM((HQ * SEG, HD), BF16),
            pltpu.VMEM((HD, HQ * SEG), BF16),
            pltpu.VMEM((HD, HQ * SEG), F32),
            pltpu.VMEM((1, HQ * SEG), F32),
            pltpu.SemaphoreType.DMA((BLOCKS,)),
            pltpu.SemaphoreType.DMA((3 * REACH,)),
        ],
        compiler_params=pltpu.CompilerParams(vmem_limit_bytes=52 * 1024 * 1024),
        cost_estimate=pl.CostEstimate(
            flops=500_000_000, bytes_accessed=1_000_000, transcendentals=0
        ),
        name="attention_backward",
    )(info, query, out, grad_out, lse, *blocks)
    return result[0], result[1 : 1 + REACH], result[1 + REACH : 1 + 2 * REACH], result[1 + 2 * REACH :]


def per_device(
    tokens,
    cotangent,
    lengths,
    w_qkv,
    w_out,
    w_gu,
    w_down,
    norm_gains,
    first_qkv,
    first_out,
    first_gu,
    first_down,
    first_gains,
    second_qkv,
    second_out,
    second_gu,
    second_down,
    second_gains,
):
    streams = tokens.shape[0]
    row_count = streams * SEG
    member_index = lax.axis_index("group")
    tok_rows = tokens.reshape(row_count, D).astype(F32)
    grad_out = cotangent.reshape(row_count, D).astype(F32)
    start_row = member_index * SEG
    boundary = lengths[:, 0]
    info = jnp.concatenate(
        [
            jnp.stack([start_row, member_index // 4, member_index // 2 % 2, member_index % 2]),
            boundary,
        ]
    ).astype(jnp.int32)
    q_width = HQ * HD
    low_qkv = w_qkv.astype(BF16)
    gain_count = norm_gains.shape[0]
    gain_row = jnp.pad(norm_gains.astype(BF16), (0, 2 * HD - gain_count))
    full_kv, gain_rows = order_rows(
        info,
        gather_all(jnp.concatenate([low_qkv[:, q_width:], gain_row[None]], axis=0)),
        "order_kv",
    )
    full_gains = gain_rows[:, :gain_count].reshape(-1)
    gain_in, gain_pa, gain_pf, gain_po, gain_query, gain_key = split_gains(full_gains)
    out_rows = w_out.shape[0]
    down_rows = w_down.shape[0]
    full_out, full_down, full_gu = unpack_weights(
        lax.all_gather(
            pack_shards(w_out.astype(BF16), w_down.astype(BF16), w_gu.astype(BF16)),
            "group",
            axis=0,
            tiled=False,
        )
    )
    index_mine = start_row + jnp.arange(SEG, dtype=jnp.int32)
    position_mine = index_mine[None, :] - jnp.where(
        index_mine[None, :] >= boundary[:, None], boundary[:, None], 0
    )
    cosine, sine = angles(position_mine.reshape(row_count), HD)
    normed_in, pull_in = jax.vjp(rms_norm, tok_rows, gain_in)
    input_low = normed_in.astype(BF16)
    kv_rows = jnp.dot(input_low, full_kv, preferred_element_type=F32)
    key_rot, pull_key = jax.vjp(
        lambda rows, gain: head_in(rows, gain, cosine, sine), kv_rows[:, :HD], gain_key
    )
    kv_low = jnp.concatenate([key_rot.astype(BF16), kv_rows[:, HD:].astype(BF16)], axis=1)
    blocks, low_q = gather_keys(kv_low.reshape(streams, SEG, 2 * HD), low_qkv[:, :q_width])
    (full_q,) = order_rows(info, gather_all(low_q), "order_q")
    query_rows = jnp.dot(input_low, full_q, preferred_element_type=F32)
    query_rot, pull_query = [], []
    for head in range(HQ):
        rotated, pull = jax.vjp(
            lambda rows, gain: head_in(rows, gain, cosine, sine),
            query_rows[:, head * HD : (head + 1) * HD],
            gain_query,
        )
        query_rot.append(rotated.astype(BF16))
        pull_query.append(pull)
    query_low = jnp.concatenate(query_rot, axis=1)
    attn_low, lse = attention_forward(info, query_low, blocks)
    attn_proj = jnp.dot(attn_low, full_out, preferred_element_type=F32)
    post_attn, pull_attn = jax.vjp(rms_norm, attn_proj, gain_pa)
    middle = tok_rows + post_attn
    normed_ff, pull_ff = jax.vjp(rms_norm, middle, gain_pf)
    ff_low = normed_ff.astype(BF16)
    gate_up = jnp.dot(ff_low, full_gu, preferred_element_type=F32)
    hidden = geglu(gate_up)
    hidden_low = hidden.astype(BF16)
    down_proj = jnp.dot(hidden_low, full_down, preferred_element_type=F32)
    post_ff, pull_post = jax.vjp(rms_norm, down_proj, gain_po)
    layer_out = (middle + post_ff).astype(BF16).reshape(streams, SEG, D)
    grad_down, grad_gain_po = pull_post(grad_out)
    down_low = grad_down.astype(BF16)
    grad_normed_ff, packed = feed_back(down_low, hidden_low, gate_up, ff_low, full_down, full_gu)
    mine = lax.psum_scatter(packed, "group", scatter_dimension=0, tiled=False)
    grad_middle_ff, grad_gain_pf = pull_ff(grad_normed_ff)
    grad_middle = grad_out + grad_middle_ff
    grad_attn_proj, grad_gain_pa = pull_attn(grad_middle)
    proj_low = grad_attn_proj.astype(BF16)
    grad_attn_low = jnp.dot(proj_low, full_out.T, preferred_element_type=F32).astype(BF16)
    near_out, far_out = weight_gradient(info, [(attn_low, proj_low)], None, 640, "gradient_out")
    grad_attn_low, near_out = lax.optimization_barrier((grad_attn_low, near_out))
    came_out = swap_core(far_out)
    over_out = scatter_x(near_out, came_out)
    grad_query, far, near_far, near = attention_backward(
        info, query_low, attn_low, grad_attn_low, lse, blocks
    )
    grad_kv = scatter_keys(far, near_far, near).reshape(row_count, 2 * HD)
    grad_query_rows, grad_gain_q = [], 0.0
    for head in range(HQ):
        rows, gain = pull_query[head](grad_query[:, head * HD : (head + 1) * HD])
        grad_query_rows.append(rows.astype(BF16))
        grad_gain_q = grad_gain_q + gain
    query_grad_low = jnp.concatenate(grad_query_rows, axis=1)
    near_q, far_q = weight_gradient(
        info, [(input_low, query_grad_low)], None, 512, "gradient_q"
    )
    came_q = swap_core(far_q)
    over_q = scatter_x(near_q, came_q)
    shard_q = scatter_z(near_q, came_q, over_q)
    shard_out = scatter_z(near_out, came_out, over_out)
    grad_kv, shard_q, shard_out, mine = lax.optimization_barrier(
        (grad_kv, shard_q, shard_out, mine)
    )
    grad_key_rows, grad_gain_k = pull_key(grad_kv[:, :HD])
    kv_grad_low = jnp.concatenate(
        [grad_key_rows.astype(BF16), grad_kv[:, HD:].astype(BF16)], axis=1
    )
    grad_normed_in = jnp.dot(query_grad_low, full_q.T, preferred_element_type=F32) + jnp.dot(
        kv_grad_low, full_kv.T, preferred_element_type=F32
    )
    grad_tokens_in, grad_gain_in = pull_in(grad_normed_in)
    token_grad = (grad_middle + grad_tokens_in).reshape(streams, SEG, D)
    wgrad_gains = jnp.concatenate(
        [grad_gain_in, grad_gain_pa, grad_gain_pf, grad_gain_po, grad_gain_q, grad_gain_k]
    )
    gains_out = jnp.pad(
        wgrad_gains.reshape(MEMBERS, gain_count), ((0, 0), (0, 2 * HD - gain_count))
    )
    near_kv, far_kv = weight_gradient(
        info, [(input_low, kv_grad_low)], gains_out, 2 * HD, "gradient_kv"
    )
    came_kv = swap_core(far_kv)
    over_kv, mine, shard_q, shard_out = lax.optimization_barrier(
        (scatter_x(near_kv, came_kv), mine, shard_q, shard_out)
    )
    sum_kv = over_replicas(scatter_z(near_kv, came_kv, over_kv))
    sum_q = over_replicas(shard_q)
    sum_out = over_replicas(shard_out)
    shard_qkv = jnp.concatenate([sum_q, sum_kv[:-8]], axis=1)
    shard_gains = sum_kv[-1, :gain_count]
    sum_packed = over_replicas(mine)
    sum_gu = sum_packed[HEAD:]
    sum_down = unpack_down(sum_packed, down_rows)
    upd_qkv = adam_step(w_qkv, first_qkv, second_qkv, shard_qkv, RATE_MATRIX, DECAY_RATE)
    upd_out = adam_step(w_out, first_out, second_out, sum_out, RATE_MATRIX, DECAY_RATE)
    upd_gu = adam_step(w_gu, first_gu, second_gu, sum_gu, RATE_MATRIX, DECAY_RATE)
    upd_down = adam_step(w_down, first_down, second_down, sum_down, RATE_MATRIX, DECAY_RATE)
    upd_gains = adam_step(norm_gains, first_gains, second_gains, shard_gains, RATE_GAIN, 0.0)
    return (layer_out, token_grad, *upd_qkv, *upd_out, *upd_gu, *upd_down, *upd_gains)


def solution(mesh):
    in_specs = (
        P("replica", "group", None),
        P("replica", "group", None),
        P("replica", None),
        P("group", None),
        P("group", None),
        P("group", None),
        P("group", None),
        P("group"),
        P("group", None),
        P("group", None),
        P("group", None),
        P("group", None),
        P("group"),
        P("group", None),
        P("group", None),
        P("group", None),
        P("group", None),
        P("group"),
    )
    out_specs = (
        P("replica", "group", None),
        P("replica", "group", None),
        P("group", None),
        P("group", None),
        P("group", None),
        P("group", None),
        P("group", None),
        P("group", None),
        P("group", None),
        P("group", None),
        P("group", None),
        P("group", None),
        P("group", None),
        P("group", None),
        P("group"),
        P("group"),
        P("group"),
    )
    return jax.shard_map(
        per_device, mesh=mesh, in_specs=in_specs, out_specs=out_specs, check_vma=False
    )
```

```python
import math

import jax
import jax.numpy as jnp
from jax import lax
from jax.experimental import pallas as pl
from jax.experimental.pallas import tpu as pltpu
from jax.sharding import PartitionSpec as P

D = 640
HQ = 4
HD = 256
FF = 2048
SEG = 256
STEP = 10


EPS_NORM = 1e-06
BETA_ONE = 0.9
BETA_TWO = 0.999
ADAM_EPS = 1e-08
RATE_MATRIX = 0.1
RATE_GAIN = 0.5
DECAY_RATE = 0.1
ROPE_BASE = 1000000.0
NEGATIVE = -1e30
SCALE_SCORE = 0.0625


def rms_norm(values, gain_row):
    factor = lax.rsqrt(jnp.mean(values * values, axis=-1, keepdims=True) + EPS_NORM)
    return values * factor * gain_row


def angles(position, width):
    half_width = width // 2
    frequency = jnp.exp(
        jnp.arange(half_width, dtype=jnp.float32) * (-2.0 * math.log(ROPE_BASE) / width)
    )
    angle_table = position.astype(jnp.float32)[:, None] * frequency[None, :]
    return (jnp.cos(angle_table), jnp.sin(angle_table))


def rotate(values, cosine, sine):
    half_width = values.shape[-1] // 2
    leading = values[..., :half_width]
    trailing = values[..., half_width:]
    return jnp.concatenate(
        [leading * cosine - trailing * sine, trailing * cosine + leading * sine], axis=-1
    )


def layout(lengths, total):
    seq_ends = jnp.cumsum(lengths)
    seq_starts = seq_ends - lengths
    stream_index = jnp.arange(total, dtype=jnp.int32)
    segment = jnp.sum((stream_index[:, None] >= seq_ends[None, :]).astype(jnp.int32), axis=1)
    seq_begin = jnp.max(
        jnp.where(stream_index[:, None] >= seq_starts[None, :], seq_starts[None, :], 0), axis=1
    )
    return (segment, stream_index - seq_begin)


def head_in(values, gain_row, cosine, sine):
    return rotate(rms_norm(values, gain_row), cosine, sine)


def geglu(gate_up):
    return jax.nn.gelu(gate_up[:, :FF], approximate=True) * gate_up[:, FF:]


def split_gains(gain_all):
    return (
        gain_all[0:D],
        gain_all[D : 2 * D],
        gain_all[2 * D : 3 * D],
        gain_all[3 * D : 4 * D],
        gain_all[4 * D : 4 * D + HD],
        gain_all[4 * D + HD : 4 * D + 2 * HD],
    )


def adam_step(master, moment_one, moment_two, gradient, rate, decay):
    moment_new = BETA_ONE * moment_one + (1.0 - BETA_ONE) * gradient
    square_new = BETA_TWO * moment_two + (1.0 - BETA_TWO) * gradient * gradient
    moment_hat = moment_new / (1.0 - BETA_ONE**STEP)
    square_hat = square_new / (1.0 - BETA_TWO**STEP)
    master_new = master * (1.0 - rate * decay) - rate * moment_hat / (
        jnp.sqrt(square_hat) + ADAM_EPS
    )
    return (moment_new, square_new, master_new)


LOG2E = 1.4426950408889634
KEYS = 512
MEMBERS = 16
PACK = 32
HEAD = 24
REACH = 3
BLOCKS = 4 * REACH
NT = (((1,), (1,)), ((), ()))
TN = (((0,), (0,)), ((), ()))
F32 = jnp.float32
BF16 = jnp.bfloat16


def shift_z(values, k):
    return lax.ppermute(values, "group", [(i, (i + 4 * k) % MEMBERS) for i in range(MEMBERS)])


def line_up(values, lowest):
    return lax.ppermute(values, "group", [(i, i + 4) for i in range(4 * lowest, MEMBERS - 4)])


def line_down(values, lowest):
    return lax.ppermute(values, "group", [(i, i - 4) for i in range(4 * lowest, MEMBERS)])


def swap_x(values):
    return lax.ppermute(values, "group", [(i, i ^ 2) for i in range(MEMBERS)])


def swap_core(values):
    return lax.ppermute(values, "group", [(i, i ^ 1) for i in range(MEMBERS)])


def spread(lines):
    near = lines + [swap_x(line) for line in lines]
    return near + [swap_core(block) for block in near]


def gather_all(own):
    return spread([own] + [shift_z(own, k) for k in (1, 2, 3)])


def gather_keys(own, later):
    first = line_up(own, 0)
    second, over, over_first, later = lax.optimization_barrier(
        (line_up(first, 1), swap_x(own), swap_x(first), later)
    )
    near = [own, first, second, over, over_first, swap_x(second)]
    return near + [swap_core(block) for block in near], later


def scatter_keys(far, near_far, near):
    running = None
    for k in range(REACH - 1, -1, -1):
        came = swap_core(far[k]).astype(F32)
        over = swap_x((near_far[k].astype(F32) + came[1]).astype(BF16))
        total = near[k].astype(F32) + came[0] + over.astype(F32)
        if running is not None:
            total = total + running.astype(F32)
        if k:
            running = line_down(total.astype(BF16), k)
    return total


def scatter_x(near, came):
    return swap_x((near[4:].astype(F32) + came[4:].astype(F32)).astype(BF16))


def scatter_z(near, came, over):
    total = [near[k].astype(F32) + came[k].astype(F32) + over[k].astype(F32) for k in range(4)]
    for k in (1, 2, 3):
        total[0] = total[0] + shift_z(total[k].astype(BF16), k).astype(F32)
    return total[0].astype(BF16)


def over_replicas(shard):
    if lax.axis_size("replica") == 2:
        other = lax.ppermute(shard, "replica", [(0, 1), (1, 0)])
        return shard.astype(F32) + other.astype(F32)
    return lax.psum(shard, "replica").astype(F32)


def owner_up(info, place):
    cr, xr, k = place // 8, place // 4 % 2, place % 4
    return ((info[1] + k) & 3) * 4 + (info[2] ^ xr) * 2 + (info[3] ^ cr)


def order_kernel(info, *refs):
    blocks = refs[:MEMBERS]
    full_ref, rows = refs[MEMBERS], refs[-1]
    count = rows.shape[0] // MEMBERS
    for place in range(MEMBERS):
        cr, xr, k = place // 8, place // 4 % 2, place % 4
        owner = ((info[1] - k) & 3) * 4 + (info[2] ^ xr) * 2 + (info[3] ^ cr)
        values = blocks[place][...].astype(F32)
        rows[pl.ds(pl.multiple_of(owner * count, 8), count)] = values[:count]
        if len(refs) > MEMBERS + 2:
            refs[MEMBERS + 1][pl.ds(owner, 1)] = values[count : count + 1]
    full_ref[...] = rows[...].astype(BF16)


def order_rows(info, blocks, name):
    rows, columns = blocks[0].shape
    count = rows // 8 * 8
    vmem = pl.BlockSpec(memory_space=pltpu.VMEM)
    shapes = [jax.ShapeDtypeStruct((MEMBERS * count, columns), BF16)]
    if rows > count:
        shapes.append(jax.ShapeDtypeStruct((MEMBERS, columns), F32))
    return pl.pallas_call(
        order_kernel,
        out_shape=shapes,
        in_specs=[pl.BlockSpec(memory_space=pltpu.SMEM)] + [vmem] * MEMBERS,
        out_specs=[vmem] * len(shapes),
        scratch_shapes=[pltpu.VMEM((MEMBERS * count, columns), F32)],
        compiler_params=pltpu.CompilerParams(vmem_limit_bytes=32 * 1024 * 1024),
        cost_estimate=pl.CostEstimate(flops=0, bytes_accessed=4_000_000, transcendentals=0),
        name=name,
    )(info, *blocks)


def gradient_kernel(tile, pairs, extra, info, *refs):
    operands = refs[: 2 * pairs + extra]
    near, far = refs[2 * pairs + extra : 2 * pairs + extra + 2]
    sums = refs[2 * pairs + extra + 2 :]
    columns = near.shape[2]
    for begin in range(0, columns, tile):
        at = slice(begin, begin + tile)
        for pair in range(pairs):
            left, right = operands[2 * pair], operands[2 * pair + 1]
            sums[pair][...] = lax.dot_general(
                left[...], right[:, at], TN, preferred_element_type=F32
            )
        for place in range(MEMBERS):
            owner = owner_up(info, place)
            parts = []
            for pair in range(pairs):
                count = sums[pair].shape[0] // MEMBERS
                parts.append(sums[pair][pl.ds(pl.multiple_of(owner * count, 8), count)])
            if extra:
                row = operands[2 * pairs][pl.ds(owner, 1), at]
                parts.append(jnp.broadcast_to(row, (8, tile)))
            block = jnp.concatenate(parts, axis=0) if len(parts) > 1 else parts[0]
            target = far if place >= 8 else near
            target[place % 8, :, at] = block.astype(BF16)


def weight_gradient(info, pairs, gains, tile, name):
    columns = pairs[0][1].shape[1]
    tokens_here = pairs[0][0].shape[0]
    counts = [left.shape[1] // MEMBERS for left, _ in pairs]
    rows = sum(counts) + (8 if gains is not None else 0)
    operands = [operand for pair in pairs for operand in pair]
    if gains is not None:
        operands.append(gains)
    shape = jax.ShapeDtypeStruct((MEMBERS // 2, rows, columns), BF16)
    vmem = pl.BlockSpec(memory_space=pltpu.VMEM)
    return pl.pallas_call(
        lambda *refs: gradient_kernel(tile, len(pairs), int(gains is not None), *refs),
        out_shape=(shape, shape),
        in_specs=[pl.BlockSpec(memory_space=pltpu.SMEM)] + [vmem] * len(operands),
        out_specs=(vmem, vmem),
        scratch_shapes=[pltpu.VMEM((MEMBERS * count, tile), F32) for count in counts],
        compiler_params=pltpu.CompilerParams(vmem_limit_bytes=48 * 1024 * 1024),
        cost_estimate=pl.CostEstimate(
            flops=2 * tokens_here * columns * MEMBERS * sum(counts),
            bytes_accessed=4 * MEMBERS * rows * columns,
            transcendentals=0,
        ),
        name=name,
    )(info, *operands)


def pack_shards(out_shard, down_shard, gu_shard):
    mixed = jnp.concatenate([out_shard, down_shard], axis=0)
    rows, columns = mixed.shape
    tiles = mixed.reshape(rows // PACK, PACK, columns // 128, 128).transpose(1, 0, 2, 3)
    flat = tiles.reshape(PACK, -1)
    flat = jnp.pad(flat, ((0, 0), (0, gu_shard.shape[1] - flat.shape[1])))
    return jnp.concatenate([flat, gu_shard], axis=0)


def unpack_down(packed, rows):
    tiles = packed[:HEAD].reshape(HEAD // 8, 8, -1, 128).transpose(0, 2, 1, 3)
    count = rows // 8 * (D // 128)
    tiles = tiles.reshape(-1, 8, 128)[:count].reshape(rows // 8, D // 128, 8, 128)
    return tiles.transpose(0, 2, 1, 3).reshape(rows, D)


def unpack_kernel(packed, out_ref, down_ref, gu_ref):
    out_rows, down_rows = out_ref.shape[0] // 2, down_ref.shape[0] // 2
    for member in range(2):
        for i in range((out_rows + down_rows) // PACK):
            for j in range(D // 128):
                tile = 128 * (i * (D // 128) + j)
                values = packed[member, 0:PACK, tile : tile + 128]
                if i < out_rows // PACK:
                    row = member * out_rows + i * PACK
                    out_ref[row : row + PACK, 128 * j : 128 * j + 128] = values
                else:
                    row = member * down_rows + i * PACK - out_rows
                    down_ref[row : row + PACK, 128 * j : 128 * j + 128] = values
    for begin in range(0, 2 * FF, 1024):
        at = slice(begin, begin + 1024)
        both = [packed[member, PACK:, at].astype(F32) for member in range(2)]
        gu_ref[:, at] = jnp.concatenate(both, axis=0).astype(BF16)


def unpack_weights(packed):
    rows = packed.shape[1]
    out_rows, down_rows, gu_rows = HQ * HD // MEMBERS, FF // MEMBERS, rows - PACK
    return pl.pallas_call(
        unpack_kernel,
        grid=(MEMBERS // 2,),
        out_shape=(
            jax.ShapeDtypeStruct((HQ * HD, D), BF16),
            jax.ShapeDtypeStruct((FF, D), BF16),
            jax.ShapeDtypeStruct((MEMBERS * gu_rows, 2 * FF), BF16),
        ),
        in_specs=[pl.BlockSpec((2, rows, 2 * FF), lambda i: (i, 0, 0))],
        out_specs=(
            pl.BlockSpec((2 * out_rows, D), lambda i: (i, 0)),
            pl.BlockSpec((2 * down_rows, D), lambda i: (i, 0)),
            pl.BlockSpec((2 * gu_rows, 2 * FF), lambda i: (i, 0)),
        ),
        compiler_params=pltpu.CompilerParams(vmem_limit_bytes=32 * 1024 * 1024),
        cost_estimate=pl.CostEstimate(flops=0, bytes_accessed=19_000_000, transcendentals=0),
        name="unpack_weights",
    )(packed)


def feed_back_kernel(down, hidden, gate_up, ff, w_down, w_gu, db_ref, packed, dgu, sums):
    tile = 512
    root = math.sqrt(2.0 / math.pi)
    for begin in range(0, FF, tile):
        at = slice(begin, begin + tile)
        at_up = slice(FF + begin, FF + begin + tile)
        dh = lax.dot_general(down[...], w_down[at, :], NT, preferred_element_type=F32)
        gate, up = gate_up[:, at], gate_up[:, at_up]
        square = gate * gate
        wave = jnp.tanh(root * gate * (1.0 + 0.044715 * square))
        half = 0.5 * (1.0 + wave)
        slope = half + 0.5 * gate * (1.0 - wave * wave) * (root * (1.0 + 3.0 * 0.044715 * square))
        dgate = (dh * up * slope).astype(BF16)
        dup = (dh * gate * half).astype(BF16)
        dgu[:, at] = dgate
        dgu[:, at_up] = dup
        term = lax.dot_general(dgate, w_gu[:, at], NT, preferred_element_type=F32)
        term += lax.dot_general(dup, w_gu[:, at_up], NT, preferred_element_type=F32)
        if begin:
            db_ref[...] += term
        else:
            db_ref[...] = term
        sums[at, :] = lax.dot_general(hidden[:, at], down[...], TN, preferred_element_type=F32)
    gu_rows = packed.shape[1] - HEAD
    down_rows = FF // MEMBERS
    slabs = 2 * FF // 128
    for begin in range(0, 2 * FF, tile):
        block = lax.dot_general(
            ff[...], dgu[:, begin : begin + tile], TN, preferred_element_type=F32
        )
        for member in range(MEMBERS):
            lanes = []
            for slab in range(begin // 128, (begin + tile) // 128):
                parts = []
                for r in range(HEAD // 8):
                    i, j = divmod(r * slabs + slab, D // 128)
                    if 8 * i < down_rows:
                        row = member * down_rows + 8 * i
                        parts.append(sums[row : row + 8, 128 * j : 128 * j + 128])
                    else:
                        parts.append(jnp.zeros((8, 128), F32))
                lanes.append(jnp.concatenate(parts, axis=0))
            top = jnp.concatenate(lanes, axis=1)
            rows = block[member * gu_rows : (member + 1) * gu_rows]
            packed[member, :, begin : begin + tile] = jnp.concatenate([top, rows], axis=0).astype(
                BF16
            )


def feed_back(down, hidden, gate_up, ff, w_down, w_gu):
    vmem = pl.BlockSpec(memory_space=pltpu.VMEM)
    tokens_here = ff.shape[0]
    return pl.pallas_call(
        feed_back_kernel,
        out_shape=(
            jax.ShapeDtypeStruct((tokens_here, D), F32),
            jax.ShapeDtypeStruct((MEMBERS, HEAD + D // MEMBERS, 2 * FF), BF16),
        ),
        in_specs=[vmem] * 6,
        out_specs=(vmem, vmem),
        scratch_shapes=[pltpu.VMEM((tokens_here, 2 * FF), BF16), pltpu.VMEM((FF, D), F32)],
        compiler_params=pltpu.CompilerParams(vmem_limit_bytes=56 * 1024 * 1024),
        cost_estimate=pl.CostEstimate(
            flops=16 * tokens_here * D * FF, bytes_accessed=32_000_000, transcendentals=1_000_000
        ),
        name="feed_back",
    )(down, hidden, gate_up, ff, w_down, w_gu)


def key_range(info, stream):
    first = info[0]
    bound = info[4 + stream]
    low = jnp.where(first >= bound, bound, 0)
    high = jnp.where(first + SEG - 1 >= bound, bound, 0)
    return first, bound, low, high


def load_blocks(info, blocks, kv, sem):
    z, x, c = info[1], info[2], info[3]
    copies = []
    for place in range(len(blocks)):
        cr, xr, k = place // (2 * REACH), place // REACH % 2, place % REACH
        owner = ((z - k) & 3) * 4 + (x ^ xr) * 2 + (c ^ cr)
        copies.append(pltpu.make_async_copy(blocks[place], kv.at[owner], sem.at[place]))
    for copy in copies:
        copy.start()
    return copies


def forward_kernel(info, q_ref, *refs):
    blocks = refs[:BLOCKS]
    o_ref, lse_ref, kv, acc, total, sem = refs[BLOCKS:]
    copies = load_blocks(info, blocks, kv, sem)
    for copy in copies:
        copy.wait()

    def one_stream(stream, carry):
        mine = pl.ds(pl.multiple_of(stream * SEG, SEG), SEG)
        first, bound, low, high = key_range(info, stream)
        begin = low // KEYS
        diagonal = first // KEYS
        clear = jnp.clip((high + KEYS - 1) // KEYS, begin, diagonal)
        acc[...] = jnp.zeros_like(acc)
        total[...] = jnp.zeros_like(total)

        def visit(j, masked):
            keys = kv[pl.ds(2 * j, 2), stream, :, 0:HD].reshape(KEYS, HD)
            values = kv[pl.ds(2 * j, 2), stream, :, HD : 2 * HD].reshape(KEYS, HD)
            if masked:
                row = first + lax.broadcasted_iota(jnp.int32, (SEG, KEYS), 0)
                col = j * KEYS + lax.broadcasted_iota(jnp.int32, (SEG, KEYS), 1)
                mask = (col <= row) & (col >= jnp.where(row >= bound, bound, 0))
            for head in range(HQ):
                rows = slice(head * SEG, (head + 1) * SEG)
                query = q_ref[mine, head * HD : (head + 1) * HD]
                score = lax.dot_general(query, keys, NT, preferred_element_type=F32)
                prob = jnp.exp2(score * (SCALE_SCORE * LOG2E))
                if masked:
                    prob = jnp.where(mask, prob, 0.0)
                total[rows] += (
                    prob[:, 0:128] + prob[:, 128:256] + prob[:, 256:384] + prob[:, 384:512]
                )
                acc[rows] += jnp.dot(prob.astype(BF16), values, preferred_element_type=F32)

        def masked_step(i, carry):
            visit(jnp.where(i < clear, i, diagonal), True)
            return carry

        def clear_step(j, carry):
            visit(j, False)
            return carry

        lax.fori_loop(begin, clear + 1, masked_step, 0)
        lax.fori_loop(clear, diagonal, clear_step, 0)
        for head in range(HQ):
            rows = slice(head * SEG, (head + 1) * SEG)
            part = total[rows]
            out = acc[rows] / jnp.sum(part, axis=1, keepdims=True)
            o_ref[mine, head * HD : (head + 1) * HD] = out.astype(BF16)
            lse_ref[stream, :, rows] = jnp.log2(jnp.sum(part.T, axis=0, keepdims=True))
        return carry

    lax.fori_loop(0, 2, one_stream, 0)


def attention_forward(info, query, blocks):
    vmem = pl.BlockSpec(memory_space=pltpu.VMEM)
    return pl.pallas_call(
        forward_kernel,
        out_shape=(
            jax.ShapeDtypeStruct((2 * SEG, HQ * HD), BF16),
            jax.ShapeDtypeStruct((2, 1, HQ * SEG), F32),
        ),
        in_specs=[pl.BlockSpec(memory_space=pltpu.SMEM), vmem]
        + [pl.BlockSpec(memory_space=pl.ANY)] * BLOCKS,
        out_specs=(vmem, vmem),
        scratch_shapes=[
            pltpu.VMEM((MEMBERS, 2, SEG, 2 * HD), BF16),
            pltpu.VMEM((HQ * SEG, HD), F32),
            pltpu.VMEM((HQ * SEG, 128), F32),
            pltpu.SemaphoreType.DMA((BLOCKS,)),
        ],
        compiler_params=pltpu.CompilerParams(vmem_limit_bytes=40 * 1024 * 1024),
        cost_estimate=pl.CostEstimate(
            flops=7_000_000_000, bytes_accessed=9_000_000, transcendentals=7_000_000
        ),
        name="attention_forward",
    )(info, query, *blocks)


def backward_kernel(info, q_ref, o_ref, do_ref, lse_ref, *refs):
    blocks = refs[:BLOCKS]
    dq_ref = refs[BLOCKS]
    far = refs[BLOCKS + 1 : BLOCKS + 1 + REACH]
    near_far = refs[BLOCKS + 1 + REACH : BLOCKS + 1 + 2 * REACH]
    near = refs[BLOCKS + 1 + 2 * REACH : BLOCKS + 1 + 3 * REACH]
    kv, dkv, qs, qt, dos, dot_, dqt, delta, sem, out_sem = refs[BLOCKS + 1 + 3 * REACH :]
    copies = load_blocks(info, blocks, kv, sem)
    z, x, c = info[1], info[2], info[3]

    def clean(place, carry):
        dkv[place] = jnp.zeros((2, SEG, 2 * HD), BF16)
        return carry

    lax.fori_loop(0, BLOCKS, clean, 0)
    for copy in copies:
        copy.wait()

    def one_stream(stream, carry):
        first, bound, low, high = key_range(info, stream)
        mine = pl.ds(pl.multiple_of(stream * SEG, SEG), SEG)
        for head in range(HQ):
            rows = slice(head * SEG, (head + 1) * SEG)
            lanes = slice(head * HD, (head + 1) * HD)
            query = q_ref[mine, lanes]
            grad = do_ref[mine, lanes]
            qs[rows] = query
            dos[rows] = grad
            qt[:, rows] = query.T
            dot_[:, rows] = grad.T
            both = grad.astype(F32) * o_ref[mine, lanes].astype(F32)
            delta[:, rows] = jnp.sum((both[:, 0:128] + both[:, 128:256]).T, axis=0, keepdims=True)
        dqt[...] = jnp.zeros_like(dqt)

        def visit(j, count, masked):
            rows_here = count * SEG
            keys = kv[pl.ds(j, count), stream, :, 0:HD].reshape(rows_here, HD)
            values = kv[pl.ds(j, count), stream, :, HD : 2 * HD].reshape(rows_here, HD)
            score = jnp.dot(keys, qt[...], preferred_element_type=F32)
            prob = jnp.exp2(score * (SCALE_SCORE * LOG2E) - lse_ref[stream])
            if masked:
                row = first + (lax.broadcasted_iota(jnp.int32, (1, HQ * SEG), 1) & (SEG - 1))
                start = jnp.where(row >= bound, bound, 0)
                col = j * SEG + lax.broadcasted_iota(jnp.int32, (rows_here, HQ * SEG), 0)
                prob = jnp.where((col <= row) & (col >= start), prob, 0.0)
            dprob = jnp.dot(values, dot_[...], preferred_element_type=F32)
            dscore = (prob * (dprob - delta[...])).astype(BF16)
            dv = jnp.dot(prob.astype(BF16), dos[...], preferred_element_type=F32).astype(BF16)
            dk = jnp.dot(dscore, qs[...], preferred_element_type=F32)
            dk = (dk * SCALE_SCORE).astype(BF16)
            dqt[...] += jnp.dot(keys.T, dscore, preferred_element_type=F32)
            for n in range(count):
                at = j + n
                place = ((at & 1) ^ c) * (2 * REACH) + (z - (at >> 2)) * 2 + (((at >> 1) & 1) ^ x)
                dkv[place, stream, :, 0:HD] = dk[n * SEG : (n + 1) * SEG]
                dkv[place, stream, :, HD : 2 * HD] = dv[n * SEG : (n + 1) * SEG]

        begin = low // SEG
        diagonal = first // SEG
        clear = jnp.clip((high + SEG - 1) // SEG, begin, diagonal)
        pairs = (diagonal - clear) // 2

        def masked_step(i, carry):
            visit(jnp.where(i < clear, i, i + 2 * pairs), 1, True)
            return carry

        def clear_step(i, carry):
            visit(clear + 2 * i, 2, False)
            return carry

        lax.fori_loop(begin, diagonal + 1 - 2 * pairs, masked_step, 0)
        lax.fori_loop(0, pairs, clear_step, 0)
        for head in range(HQ):
            rows = slice(head * SEG, (head + 1) * SEG)
            dq_ref[mine, head * HD : (head + 1) * HD] = dqt[:, rows].T * SCALE_SCORE
        return carry

    lax.fori_loop(0, 2, one_stream, 0)
    outs = []
    for k in range(REACH):
        outs.append((dkv.at[pl.ds(2 * REACH + 2 * k, 2)], far[k]))
        outs.append((dkv.at[2 * k + 1], near_far[k]))
        outs.append((dkv.at[2 * k], near[k]))
    copies = [
        pltpu.make_async_copy(source, target, out_sem.at[n])
        for n, (source, target) in enumerate(outs)
    ]
    for copy in copies:
        copy.start()
    for copy in copies:
        copy.wait()


def attention_backward(info, query, out, grad_out, lse, blocks):
    one = jax.ShapeDtypeStruct((2, SEG, 2 * HD), BF16)
    two = jax.ShapeDtypeStruct((2, 2, SEG, 2 * HD), BF16)
    vmem = pl.BlockSpec(memory_space=pltpu.VMEM)
    anywhere = pl.BlockSpec(memory_space=pl.ANY)
    result = pl.pallas_call(
        backward_kernel,
        out_shape=[jax.ShapeDtypeStruct((2 * SEG, HQ * HD), F32)]
        + [two] * REACH
        + [one] * (2 * REACH),
        in_specs=[pl.BlockSpec(memory_space=pltpu.SMEM)] + [vmem] * 4 + [anywhere] * BLOCKS,
        out_specs=[vmem] + [anywhere] * (3 * REACH),
        scratch_shapes=[
            pltpu.VMEM((MEMBERS, 2, SEG, 2 * HD), BF16),
            pltpu.VMEM((BLOCKS, 2, SEG, 2 * HD), BF16),
            pltpu.VMEM((HQ * SEG, HD), BF16),
            pltpu.VMEM((HD, HQ * SEG), BF16),
            pltpu.VMEM((HQ * SEG, HD), BF16),
            pltpu.VMEM((HD, HQ * SEG), BF16),
            pltpu.VMEM((HD, HQ * SEG), F32),
            pltpu.VMEM((1, HQ * SEG), F32),
            pltpu.SemaphoreType.DMA((BLOCKS,)),
            pltpu.SemaphoreType.DMA((3 * REACH,)),
        ],
        compiler_params=pltpu.CompilerParams(vmem_limit_bytes=52 * 1024 * 1024),
        cost_estimate=pl.CostEstimate(
            flops=500_000_000, bytes_accessed=1_000_000, transcendentals=0
        ),
        name="attention_backward",
    )(info, query, out, grad_out, lse, *blocks)
    return result[0], result[1 : 1 + REACH], result[1 + REACH : 1 + 2 * REACH], result[1 + 2 * REACH :]


def per_device(
    tokens,
    cotangent,
    lengths,
    w_qkv,
    w_out,
    w_gu,
    w_down,
    norm_gains,
    first_qkv,
    first_out,
    first_gu,
    first_down,
    first_gains,
    second_qkv,
    second_out,
    second_gu,
    second_down,
    second_gains,
):
    streams = tokens.shape[0]
    row_count = streams * SEG
    member_index = lax.axis_index("group")
    tok_rows = tokens.reshape(row_count, D).astype(F32)
    grad_out = cotangent.reshape(row_count, D).astype(F32)
    start_row = member_index * SEG
    boundary = lengths[:, 0]
    info = jnp.concatenate(
        [
            jnp.stack([start_row, member_index // 4, member_index // 2 % 2, member_index % 2]),
            boundary,
        ]
    ).astype(jnp.int32)
    q_width = HQ * HD
    low_qkv = w_qkv.astype(BF16)
    gain_count = norm_gains.shape[0]
    gain_row = jnp.pad(norm_gains.astype(BF16), (0, 2 * HD - gain_count))
    full_kv, gain_rows = order_rows(
        info,
        gather_all(jnp.concatenate([low_qkv[:, q_width:], gain_row[None]], axis=0)),
        "order_kv",
    )
    full_gains = gain_rows[:, :gain_count].reshape(-1)
    gain_in, gain_pa, gain_pf, gain_po, gain_query, gain_key = split_gains(full_gains)
    out_rows = w_out.shape[0]
    down_rows = w_down.shape[0]
    full_out, full_down, full_gu = unpack_weights(
        lax.all_gather(
            pack_shards(w_out.astype(BF16), w_down.astype(BF16), w_gu.astype(BF16)),
            "group",
            axis=0,
            tiled=False,
        )
    )
    index_mine = start_row + jnp.arange(SEG, dtype=jnp.int32)
    position_mine = index_mine[None, :] - jnp.where(
        index_mine[None, :] >= boundary[:, None], boundary[:, None], 0
    )
    cosine, sine = angles(position_mine.reshape(row_count), HD)
    normed_in, pull_in = jax.vjp(rms_norm, tok_rows, gain_in)
    input_low = normed_in.astype(BF16)
    kv_rows = jnp.dot(input_low, full_kv, preferred_element_type=F32)
    key_rot, pull_key = jax.vjp(
        lambda rows, gain: head_in(rows, gain, cosine, sine), kv_rows[:, :HD], gain_key
    )
    kv_low = jnp.concatenate([key_rot.astype(BF16), kv_rows[:, HD:].astype(BF16)], axis=1)
    blocks, low_q = gather_keys(kv_low.reshape(streams, SEG, 2 * HD), low_qkv[:, :q_width])
    (full_q,) = order_rows(info, gather_all(low_q), "order_q")
    query_rows = jnp.dot(input_low, full_q, preferred_element_type=F32)
    query_rot, pull_query = [], []
    for head in range(HQ):
        rotated, pull = jax.vjp(
            lambda rows, gain: head_in(rows, gain, cosine, sine),
            query_rows[:, head * HD : (head + 1) * HD],
            gain_query,
        )
        query_rot.append(rotated.astype(BF16))
        pull_query.append(pull)
    query_low = jnp.concatenate(query_rot, axis=1)
    attn_low, lse = attention_forward(info, query_low, blocks)
    attn_proj = jnp.dot(attn_low, full_out, preferred_element_type=F32)
    post_attn, pull_attn = jax.vjp(rms_norm, attn_proj, gain_pa)
    middle = tok_rows + post_attn
    normed_ff, pull_ff = jax.vjp(rms_norm, middle, gain_pf)
    ff_low = normed_ff.astype(BF16)
    gate_up = jnp.dot(ff_low, full_gu, preferred_element_type=F32)
    hidden = geglu(gate_up)
    hidden_low = hidden.astype(BF16)
    down_proj = jnp.dot(hidden_low, full_down, preferred_element_type=F32)
    post_ff, pull_post = jax.vjp(rms_norm, down_proj, gain_po)
    layer_out = (middle + post_ff).astype(BF16).reshape(streams, SEG, D)
    grad_down, grad_gain_po = pull_post(grad_out)
    down_low = grad_down.astype(BF16)
    grad_normed_ff, packed = feed_back(down_low, hidden_low, gate_up, ff_low, full_down, full_gu)
    mine = lax.psum_scatter(packed, "group", scatter_dimension=0, tiled=False)
    grad_middle_ff, grad_gain_pf = pull_ff(grad_normed_ff)
    grad_middle = grad_out + grad_middle_ff
    grad_attn_proj, grad_gain_pa = pull_attn(grad_middle)
    proj_low = grad_attn_proj.astype(BF16)
    grad_attn_low = jnp.dot(proj_low, full_out.T, preferred_element_type=F32).astype(BF16)
    near_out, far_out = weight_gradient(info, [(attn_low, proj_low)], None, 640, "gradient_out")
    grad_attn_low, near_out = lax.optimization_barrier((grad_attn_low, near_out))
    came_out = swap_core(far_out)
    over_out = scatter_x(near_out, came_out)
    grad_query, far, near_far, near = attention_backward(
        info, query_low, attn_low, grad_attn_low, lse, blocks
    )
    grad_kv = scatter_keys(far, near_far, near).reshape(row_count, 2 * HD)
    grad_query_rows, grad_gain_q = [], 0.0
    for head in range(HQ):
        rows, gain = pull_query[head](grad_query[:, head * HD : (head + 1) * HD])
        grad_query_rows.append(rows.astype(BF16))
        grad_gain_q = grad_gain_q + gain
    query_grad_low = jnp.concatenate(grad_query_rows, axis=1)
    near_q, far_q = weight_gradient(
        info, [(input_low, query_grad_low)], None, 512, "gradient_q"
    )
    came_q = swap_core(far_q)
    over_q = scatter_x(near_q, came_q)
    grad_kv, over_q, over_out, mine = lax.optimization_barrier((grad_kv, over_q, over_out, mine))
    grad_key_rows, grad_gain_k = pull_key(grad_kv[:, :HD])
    kv_grad_low = jnp.concatenate(
        [grad_key_rows.astype(BF16), grad_kv[:, HD:].astype(BF16)], axis=1
    )
    kv_grad_low, shard_q, shard_out = lax.optimization_barrier(
        (
            kv_grad_low,
            scatter_z(near_q, came_q, over_q),
            scatter_z(near_out, came_out, over_out),
        )
    )
    grad_normed_in = jnp.dot(query_grad_low, full_q.T, preferred_element_type=F32) + jnp.dot(
        kv_grad_low, full_kv.T, preferred_element_type=F32
    )
    grad_tokens_in, grad_gain_in = pull_in(grad_normed_in)
    token_grad = (grad_middle + grad_tokens_in).reshape(streams, SEG, D)
    wgrad_gains = jnp.concatenate(
        [grad_gain_in, grad_gain_pa, grad_gain_pf, grad_gain_po, grad_gain_q, grad_gain_k]
    )
    gains_out = jnp.pad(
        wgrad_gains.reshape(MEMBERS, gain_count), ((0, 0), (0, 2 * HD - gain_count))
    )
    near_kv, far_kv = weight_gradient(
        info, [(input_low, kv_grad_low)], gains_out, 2 * HD, "gradient_kv"
    )
    came_kv = swap_core(far_kv)
    over_kv, sum_packed = lax.optimization_barrier(
        (scatter_x(near_kv, came_kv), over_replicas(mine))
    )
    sum_kv = over_replicas(scatter_z(near_kv, came_kv, over_kv))
    sum_q = over_replicas(shard_q)
    sum_out = over_replicas(shard_out)
    shard_qkv = jnp.concatenate([sum_q, sum_kv[:-8]], axis=1)
    shard_gains = sum_kv[-1, :gain_count]
    sum_gu = sum_packed[HEAD:]
    sum_down = unpack_down(sum_packed, down_rows)
    upd_qkv = adam_step(w_qkv, first_qkv, second_qkv, shard_qkv, RATE_MATRIX, DECAY_RATE)
    upd_out = adam_step(w_out, first_out, second_out, sum_out, RATE_MATRIX, DECAY_RATE)
    upd_gu = adam_step(w_gu, first_gu, second_gu, sum_gu, RATE_MATRIX, DECAY_RATE)
    upd_down = adam_step(w_down, first_down, second_down, sum_down, RATE_MATRIX, DECAY_RATE)
    upd_gains = adam_step(norm_gains, first_gains, second_gains, shard_gains, RATE_GAIN, 0.0)
    return (layer_out, token_grad, *upd_qkv, *upd_out, *upd_gu, *upd_down, *upd_gains)


def solution(mesh):
    in_specs = (
        P("replica", "group", None),
        P("replica", "group", None),
        P("replica", None),
        P("group", None),
        P("group", None),
        P("group", None),
        P("group", None),
        P("group"),
        P("group", None),
        P("group", None),
        P("group", None),
        P("group", None),
        P("group"),
        P("group", None),
        P("group", None),
        P("group", None),
        P("group", None),
        P("group"),
    )
    out_specs = (
        P("replica", "group", None),
        P("replica", "group", None),
        P("group", None),
        P("group", None),
        P("group", None),
        P("group", None),
        P("group", None),
        P("group", None),
        P("group", None),
        P("group", None),
        P("group", None),
        P("group", None),
        P("group", None),
        P("group", None),
        P("group"),
        P("group"),
        P("group"),
    )
    return jax.shard_map(
        per_device, mesh=mesh, in_specs=in_specs, out_specs=out_specs, check_vma=False
    )
```
